32 devices in a mesh: head: 2 (over y), blk: 16 (over z, x, core).
Axes of the slice: x: 2, y: 2, z: 4, core: 2. Of those that a mesh axis runs over, the one named last changes fastest.
Arguments:
- tokens: bfloat16 [8192, 768], P(('blk', 'head')), may hold values from -6 to 6
- w_qkv: bfloat16 [768, 2304], P(('blk', 'head')), may hold values from -0.21875 to 0.21875
- w_out: bfloat16 [768, 768], P(('blk', 'head')), may hold values from -1.5 to 1.5
- w_ff1: bfloat16 [768, 3072], P(('blk', 'head')), may hold values from -0.21875 to 0.21875
- w_ff2: bfloat16 [3072, 768], P(('blk', 'head')), may hold values from -0.109375 to 0.109375
- norm_gains: bfloat16 [2, 768], P(None, ('blk', 'head')), may hold values from 0.5 to 1.5
- norm_biases: bfloat16 [2, 768], P(None, ('blk', 'head')), may hold values from -4 to 4
- proj_biases: bfloat16 [4, 768], P(None, ('blk', 'head')), may hold values from -2 to 2
- ff_bias: bfloat16 [3072], P(('blk', 'head')), may hold values from -6 to 6
- doc_starts: int32 [33], replicated, may hold values from 1 to 8192, as said below
- d_out: bfloat16 [8192, 768], P(('blk', 'head')), may hold values from -6 to 6
Outputs:
- out: bfloat16 [8192, 768], P(('blk', 'head'))
- d_tokens: bfloat16 [8192, 768], P(('blk', 'head'))
- g_qkv: float32 [768, 2304], P(('blk', 'head'))
- g_out: float32 [768, 768], P(('blk', 'head'))
- g_ff1: float32 [768, 3072], P(('blk', 'head'))
- g_ff2: float32 [3072, 768], P(('blk', 'head'))
- g_gains: float32 [2, 768], P(None, ('blk', 'head'))
- g_norm_biases: float32 [2, 768], P(None, ('blk', 'head'))
- g_proj_biases: float32 [4, 768], P(None, ('blk', 'head'))
- g_ff_bias: float32 [3072], P(('blk', 'head'))
The draws below stay inside these ranges and needn't reach their ends.
Inputs may be any that keep to these rules, and one draw needn't show every extreme that they name: doc_starts[0] is 1 or more and the entries never fall. Each entry below 8192 starts a document that runs to the next larger entry; the last one runs past 8192 on to position doc_starts[0] - 1 of the start. Every document holds 1 to 2048 tokens, and the one that runs past the end holds exactly 2048; entries equal to 8192 start no document.
All inputs are finite; a program needn't handle non-finite values.
Results may differ from the reference program's by a relative error of at most 0.025.
Values may be sent and summed in bfloat16 or wider, within the bound.
A program may use at most 128 MiB of HBM per device.

```python
import jax
import jax.numpy as jnp
from jax import lax

D = 768
H = 12
HD = 64
FF = 3072
BLOCK = 512
DOC_MOST = 2048
TOKENS = 8192
DOCS = 33


def draw_doc_starts(key, part):
    shortest = DOC_MOST // 8
    offset = jax.random.randint(jax.random.fold_in(key, 13), (), BLOCK, DOC_MOST - BLOCK + 1, dtype=jnp.int32)
    limit = TOKENS - DOC_MOST + offset
    lengths = jax.random.randint(jax.random.fold_in(key, 11), (DOCS - 1,), shortest, DOC_MOST + 1, dtype=jnp.int32)
    ends = jnp.cumsum(lengths).astype(jnp.int32)
    middle = offset + jnp.concatenate([jnp.zeros((1,), jnp.int32), ends[:-1]])
    middle = jnp.where(middle < limit, middle, TOKENS).astype(jnp.int32)
    joined = jnp.concatenate([middle, jnp.reshape(limit, (1,)).astype(jnp.int32)])
    return jnp.sort(joined).astype(jnp.int32)


def strengthened(values, stream_key, source, target, blocks, factor):
    def block_of(dim):
        return (jnp.arange(values.shape[dim]) // (values.shape[dim] // blocks)).reshape((-1,) + (1,) * (values.ndim - 1 - dim))

    near = jax.random.permutation(stream_key, blocks)[block_of(target)]
    other_side = (block_of(target) + blocks // 2) % blocks
    return jnp.where((block_of(source) == near) | (block_of(source) == other_side), factor * values, values)


def block_scale(stream_key, dims, pieces, smallest, high):
    gain, own = 1.0, jax.random.fold_in(stream_key, 6)
    for axis_at, blocks in pieces:
        heights = jnp.exp(jax.random.uniform(jax.random.fold_in(own, axis_at), (blocks,), jnp.float32, smallest / len(pieces), high / len(pieces)))
        gain = gain * jnp.repeat(heights, dims[axis_at] // blocks).reshape([-1 if axis == axis_at else 1 for axis in range(len(dims))])
    return gain


def normal_values(key, extent, width, bound, split=(), held_as=jnp.bfloat16):
    array = width * jax.random.normal(key, extent, jnp.float32)
    if split:
        array = array * block_scale(key, extent, split, -0.22, 0.18)
    return jnp.clip(array, -bound, bound).astype(held_as)


def bell_draw_with(own_key, shape, scale, bound, split, heavy, kind=jnp.bfloat16):
    drawn = scale * jax.random.normal(own_key, shape, jnp.float32)
    if split:
        drawn = drawn * block_scale(own_key, shape, split, -0.22, 0.18)
    return jnp.clip(strengthened(drawn, jax.random.fold_in(own_key, 3), *heavy), -bound, bound).astype(kind)


def setup_inputs(seed: int = 0) -> dict:
    key_list = jax.random.split(jax.random.key(seed), 12)
    tokens = normal_values(key_list[0], (TOKENS, D), 1.0, 6.0, ((0, 32),))
    w_qkv = normal_values(key_list[1], (D, 3 * D), D ** -0.5, 0.21875, ((0, 32),))
    w_out = normal_values(key_list[2], (D, D), (HD // 4) ** -0.5, 1.5, ((0, 32),))
    w_ff1 = normal_values(key_list[3], (D, FF), D ** -0.5, 0.21875, ((0, 32),))
    w_ff2 = normal_values(key_list[4], (FF, D), FF ** -0.5, 0.109375, ((0, 32),))
    norm_gains = jnp.clip(1.0 + 0.1 * jax.random.normal(key_list[5], (2, D), jnp.float32), 0.5, 1.5).astype(jnp.bfloat16)
    norm_biases = normal_values(key_list[6], (2, D), 0.3, 4.0, ((1, 32),))
    proj_biases = normal_values(key_list[7], (4, D), 0.15, 2.0, ((1, 32),))
    ff_bias = normal_values(key_list[8], (FF,), 0.5, 6.0, ((0, 32),))
    doc_starts = draw_doc_starts(jax.random.fold_in(key_list[11], 71), 0)
    d_out = bell_draw_with(key_list[10], (TOKENS, D), 1.0, 6.0, ((0, 32),), (0, 1, 32, 2.75))
    return {"tokens": tokens, "w_qkv": w_qkv, "w_out": w_out, "w_ff1": w_ff1, "w_ff2": w_ff2, "norm_gains": norm_gains, "norm_biases": norm_biases, "proj_biases": proj_biases, "ff_bias": ff_bias, "doc_starts": doc_starts, "d_out": d_out}


@jax.custom_vjp
def low(v):
    return lax.optimization_barrier(v.astype(jnp.bfloat16)).astype(jnp.float32)

@jax.custom_vjp
def low_back(v):
    return v

def low_keep(v):
    return (low(v), None)

def low_pass(kept, grad):
    return (grad,)

def back_keep(v):
    return (v, None)

def back_low(kept, grad):
    return (low(grad),)
low.defvjp(low_keep, low_pass)
low_back.defvjp(back_keep, back_low)
EPSILON = 1e-06
NEGATIVE = -1e+30
HIGHEST = lax.Precision.HIGHEST

def product(left, right):
    return jnp.dot(left, right, precision=HIGHEST, preferred_element_type=jnp.float32)

def norm_rows(values, gain_row, shift_row):
    center = values - lax.optimization_barrier(jnp.mean(values, axis=-1, keepdims=True))
    spread = lax.optimization_barrier(jnp.mean(center * center, axis=-1, keepdims=True))
    return center * lax.rsqrt(spread + EPSILON) * gain_row + shift_row

def gelu_exact(values):
    return 0.5 * values * (1.0 + jax.scipy.special.erf(values * 0.7071067811865476))

def doc_index(doc_starts, first_pos, how_many, total_rows):
    places = first_pos + jnp.arange(how_many, dtype=jnp.int32)
    counted = lax.optimization_barrier(jnp.sum((doc_starts[None, :] <= places[:, None]).astype(jnp.int32), axis=1))
    live = jnp.sum((doc_starts < total_rows).astype(jnp.int32))
    return jnp.mod(counted, live).astype(jnp.int32)

def wrap_pad(values, pad_rows):
    return jnp.concatenate([values[TOKENS - pad_rows:], values, values[:pad_rows]], axis=0)

def attention(queries, key_vals, value_vals, doc_ids):
    row_span = min(512, BLOCK)
    reach_pad = DOC_MOST
    key_pad = wrap_pad(key_vals, reach_pad)
    value_pad = wrap_pad(value_vals, reach_pad)
    ids_pad = wrap_pad(doc_ids, reach_pad)
    score_scale = HD ** (-0.5)

    def one_block(start_row):
        query_rows = lax.dynamic_slice_in_dim(queries, start_row, row_span, 0)
        query_ids = lax.dynamic_slice_in_dim(doc_ids, start_row, row_span, 0)
        key_rows = lax.dynamic_slice_in_dim(key_pad, start_row, row_span + 2 * reach_pad, 0)
        value_rows = lax.dynamic_slice_in_dim(value_pad, start_row, row_span + 2 * reach_pad, 0)
        key_ids = lax.dynamic_slice_in_dim(ids_pad, start_row, row_span + 2 * reach_pad, 0)
        scores = jnp.einsum('qhd,khd->hqk', query_rows, key_rows, precision=HIGHEST) * score_scale
        scores = low_back(scores)
        allowed = query_ids[:, None] == key_ids[None, :]
        scores = jnp.where(allowed[None, :, :], scores, NEGATIVE)
        probabilities = low(jax.nn.softmax(scores, axis=-1))
        return jnp.einsum('hqk,khd->qhd', probabilities, value_rows, precision=HIGHEST)
    start_rows = jnp.arange(TOKENS // row_span, dtype=jnp.int32) * row_span
    blocks = lax.map(jax.checkpoint(one_block), start_rows)
    return blocks.reshape(TOKENS, H, HD)

def layer_forward(tokens, w_qkv, w_out, w_ff1, w_ff2, norm_gains, norm_biases, proj_biases, ff_bias, doc_ids):
    joined = product(tokens, w_qkv)
    queries = low(low_back(joined[:, :D] + proj_biases[0]))
    key_vals = low(low_back(joined[:, D:2 * D]))
    value_vals = low(low_back(joined[:, 2 * D:] + proj_biases[1]))
    context = attention(queries.reshape(TOKENS, H, HD), key_vals.reshape(TOKENS, H, HD), value_vals.reshape(TOKENS, H, HD), doc_ids).reshape(TOKENS, D)
    context = low(low_back(context))
    attn_out = low_back(product(context, w_out) + proj_biases[2])
    hidden = norm_rows(tokens + attn_out, norm_gains[0], norm_biases[0])
    pre_act = low_back(product(low(hidden), w_ff1) + ff_bias)
    act_low = low(gelu_exact(pre_act))
    ff_out = low_back(product(act_low, w_ff2) + proj_biases[3])
    return norm_rows(hidden + ff_out, norm_gains[1], norm_biases[1])

def reference(tokens, w_qkv, w_out, w_ff1, w_ff2, norm_gains, norm_biases, proj_biases, ff_bias, doc_starts, d_out):
    doc_ids = doc_index(doc_starts, 0, TOKENS, TOKENS)
    floats = [item.astype(jnp.float32) for item in (tokens, w_qkv, w_out, w_ff1, w_ff2, norm_gains, norm_biases, proj_biases, ff_bias)]
    result, pullback = jax.vjp(lambda *params: layer_forward(*params, doc_ids), *floats)
    gradients = pullback(d_out.astype(jnp.float32))
    return (result.astype(jnp.bfloat16), gradients[0].astype(jnp.bfloat16), gradients[1], gradients[2], gradients[3], gradients[4], gradients[5], gradients[6], gradients[7], gradients[8])
```

```python
import functools

import jax
import jax.numpy as jnp
from jax import lax
from jax.experimental import pallas as pl
from jax.experimental.pallas import tpu as pltpu
from jax.sharding import PartitionSpec as P

H = 12
HD = 64
DOC_MOST = 2048
EPSILON = 1e-06
NEGATIVE = -1e30
MESH = pl.DeviceIdType.MESH
F32 = jnp.float32
BF16 = jnp.bfloat16
VMEM_BYTES = 60 * 1024 * 1024
CHIPS = 4
GROUP = 4
QW = 256
KW = 384
HW = (H // CHIPS) * HD


def div(a, b):
    return lax.div(a, jnp.int32(b))


def rem(a, b):
    return lax.rem(a, jnp.int32(b))


def nn(a, b):
    return lax.dot_general(a, b, (((1,), (0,)), ((), ())), preferred_element_type=F32)


def nt(a, b):
    return lax.dot_general(a, b, (((1,), (1,)), ((), ())), preferred_element_type=F32)


def tn(a, b):
    return lax.dot_general(a, b, (((0,), (0,)), ((), ())), preferred_element_type=F32)


def rows_at(start, count, unit=16):
    return pl.ds(pl.multiple_of(start, unit), count)


class Place:
    def __init__(self, repeat, groups):
        self.repeat = repeat
        blk, head = lax.axis_index("blk"), lax.axis_index("head")
        self.index = blk * 2 + head
        self.unit = div(self.index, repeat)
        self.core, self.x, self.y = rem(blk, 2), rem(div(blk, 2), 2), head
        self.group, self.groups = div(blk, GROUP), groups

    def bit(self, k):
        return rem(div(self.unit, 1 << k), 2)

    def partner(self, k):
        other = self.index + (1 - 2 * self.bit(k)) * (self.repeat << k)
        return {"blk": div(other, 2), "head": rem(other, 2)}

    def member(self, x, core, y):
        return {"blk": self.group * GROUP + 2 * x + core, "head": y}

    def beside(self, step):
        group = rem(self.group + self.groups + step, self.groups)
        return {"blk": group * GROUP + 2 * self.x + self.core, "head": self.y}

    def greet(self, cube=True, group=True, beside=True):
        barrier = pltpu.get_barrier_semaphore()
        partners = []
        if cube:
            partners += [self.partner(k) for k in range(5)]
        if group:
            partners += [
                self.member(
                    rem(self.x + dx, 2), rem(self.core + dc, 2), rem(self.y + dy, 2)
                )
                for dx in range(2)
                for dc in range(2)
                for dy in range(2)
                if dx + dc + dy
            ]
        if beside:
            partners += [self.beside(1), self.beside(-1)]
        for partner in partners:
            pl.semaphore_signal(barrier, inc=1, device_id=partner, device_id_type=MESH)
        pl.semaphore_wait(barrier, len(partners))


def remote(src, dst, send, recv, device):
    return pltpu.make_async_remote_copy(
        src_ref=src, dst_ref=dst, send_sem=send, recv_sem=recv, device_id=device, device_id_type=MESH
    )


class Pieces:
    def __init__(self, place, ref, rows, first, width, order, by_columns):
        self.place, self.ref, self.rows, self.first, self.width = place, ref, rows, first, width
        self.order, self.by_columns = order, by_columns
        self.shape = (rows, width // 2) if by_columns else (rows // 2, width)
        self.deltas = [(1 - 2 * place.bit(k)) * (1 << k) for k in order]

    def unit_of(self, mask, base=0):
        unit = self.place.unit
        for at in range(5):
            if isinstance(mask, int):
                if mask >> at & 1:
                    unit = unit + self.deltas[at]
            else:
                unit = unit + rem(div(mask, 1 << at), 2) * self.deltas[at]
        return unit

    def region(self, unit):
        slab, half = div(unit, 2), rem(unit, 2)
        if self.by_columns:
            return (
                rows_at(slab * self.rows, self.rows),
                rows_at(self.first + half * self.shape[1], self.shape[1], 128),
            )
        return (rows_at(unit * self.shape[0], self.shape[0]), pl.ds(self.first, self.width))

    def piece(self, mask):
        return self.ref.at[self.region(self.unit_of(mask))]


class Gather(Pieces):
    def begin(self, send, recv):
        self.send, self.recv = send, recv
        self.feed(0, 0)

    def copy(self, phase, mask, arriving=False):
        at = (1 << phase) - 1 + mask
        ref = self.piece(mask + (1 << phase) if arriving else mask)
        return remote(ref, ref, self.send.at[at], self.recv.at[at], self.place.partner(self.order[phase]))

    def feed(self, mask, phase):
        for later in range(phase, 5):
            self.copy(later, mask).start()

    def step(self, phase):
        def one(mask, carry):
            self.copy(phase, mask, True).wait_recv()
            self.feed(mask + (1 << phase), phase + 1)
            return carry

        lax.fori_loop(0, 1 << phase, one, 0)

    def finish(self):
        for phase in range(5):

            def one(mask, carry, phase=phase):
                self.copy(phase, mask).wait_send()
                return carry

            lax.fori_loop(0, 1 << phase, one, 0)


class Scatter(Pieces):
    def begin(self, landing, send, recv):
        self.landing, self.send, self.recv = landing, send, recv

        def one(j, carry):
            self.copy(0, j).start()
            return carry

        lax.fori_loop(0, 16, one, 0)

    def copy(self, phase, j):
        at = 32 - (1 << (5 - phase)) + j
        mask = (2 * j + 1) * (1 << phase)
        return remote(
            self.piece(mask),
            self.landing.at[at],
            self.send.at[at],
            self.recv.at[at],
            self.place.partner(self.order[phase]),
        )

    def absorb(self, phase, j):
        self.copy(phase, j).wait_recv()
        at = 32 - (1 << (5 - phase)) + j
        rows, columns = self.region(self.unit_of(j * (2 << phase)))
        total = self.ref[rows, columns].astype(F32) + self.landing[at].astype(F32)
        self.ref[rows, columns] = total.astype(BF16)
        return total

    def step(self, phase):
        half = 1 << (3 - phase)

        def odd(jj, carry):
            self.absorb(phase, 2 * jj + 1)
            self.copy(phase + 1, jj).start()
            return carry

        def even(jj, carry):
            self.absorb(phase, 2 * jj)
            return carry

        lax.fori_loop(0, half, odd, 0)
        lax.fori_loop(0, half, even, 0)

    def last(self):
        return self.absorb(4, 0)

    def finish(self):
        for phase in range(5):

            def one(j, carry, phase=phase):
                self.copy(phase, j).wait_send()
                return carry

            lax.fori_loop(0, 1 << (4 - phase), one, 0)


def to_heads(place, packed, landed, send, recv):
    tok = packed.shape[1]
    mine = rows_at(2 * tok * place.core + tok * place.y, tok)
    slot = 2 * place.core + place.y
    alone = place.core == place.x
    for dx in range(2):
        for dy in range(2):
            tx, ty = rem(place.x + dx, 2), rem(place.y + dy, 2)
            copy = remote(
                packed.at[2 * tx + ty],
                landed.at[mine],
                send.at[2 * dx + dy],
                recv.at[slot],
                place.member(tx, place.x, ty),
            )
            if dx + dy:
                copy.start()
            else:
                pl.when(jnp.logical_not(alone))(copy.start)

                @pl.when(alone)
                def _(tx=tx, ty=ty):
                    landed[mine] = packed[2 * tx + ty]


def to_heads_wait(place, packed, landed, send, recv):
    tok = packed.shape[1]
    alone = place.core == place.x
    for cs in range(2):
        for ys in range(2):
            part = landed.at[pl.ds(2 * tok * cs + tok * ys, tok)]
            copy = remote(part, part, send.at[0], recv.at[2 * cs + ys], place.member(place.x, 1 - place.core, place.y))
            own = alone & (place.core == cs) & (place.y == ys)
            pl.when(jnp.logical_not(own))(copy.wait_recv)


def to_heads_drain(place, packed, landed, send, recv):
    for at in range(4):
        copy = remote(packed.at[0], packed.at[0], send.at[at], recv.at[0], place.member(place.x, 1 - place.core, place.y))
        if at:
            copy.wait_send()
        else:
            pl.when(place.core != place.x)(copy.wait_send)


def to_tokens(place, rows, landed, send, recv):
    tok = landed.shape[1]
    chip = 2 * place.x + place.y
    for cs in range(2):
        for ys in range(2):
            part = pl.ds(2 * tok * cs + tok * ys, tok)
            own = (place.core == place.x) & (place.core == cs) & (place.y == ys)
            copy = remote(
                rows.at[part], landed.at[chip], send.at[2 * cs + ys], recv.at[chip], place.member(place.core, cs, ys)
            )
            pl.when(jnp.logical_not(own))(copy.start)

            @pl.when(own)
            def _(part=part):
                landed[chip] = rows[part]


def to_tokens_wait(place, rows, landed, send, recv):
    for xs in range(2):
        for ys in range(2):
            at = 2 * xs + ys
            own = (place.core == place.x) & (place.x == xs) & (place.y == ys)
            copy = remote(
                landed.at[at], landed.at[at], send.at[at], recv.at[at], place.member(place.x, 1 - place.core, place.y)
            )
            pl.when(jnp.logical_not(own))(copy.wait_recv)


def to_tokens_drain(place, rows, landed, send, recv):
    for cs in range(2):
        for ys in range(2):
            own = (place.core == place.x) & (place.core == cs) & (place.y == ys)
            at = 2 * cs + ys
            copy = remote(
                landed.at[at], landed.at[at], send.at[at], recv.at[at], place.member(place.x, 1 - place.core, place.y)
            )
            pl.when(jnp.logical_not(own))(copy.wait_send)


def spread_rows(small, per, width, keep):
    lane = lax.broadcasted_iota(jnp.int32, (128, width), 1).astype(F32)
    turn = jnp.floor((lane + 0.5) * (1.0 / per))
    place = lane - per * turn
    pick = (place == lax.broadcasted_iota(jnp.int32, (128, width), 0).astype(F32)).astype(BF16)
    wide = nn(small, pick)
    row = lax.broadcasted_iota(jnp.int32, wide.shape, 0)
    column = lax.broadcasted_iota(jnp.int32, wide.shape, 1)
    low = lax.shift_right_logical(row, 4 if keep is None else 0) * per
    wide = jnp.where((column >= low) & (column < low + per), wide, 0.0)
    if keep is None:
        return jnp.sum(wide.reshape(-1, 16, width), axis=0)
    return jnp.sum(wide, axis=0, keepdims=True)


AG_PLAN = dict(qkv=(4, 3, 2, 0, 1), out=(4, 3, 0, 2, 1), ff1=(4, 3, 0, 2, 1), ff2=(4, 3, 2, 0, 1))
RS_PLAN = dict(qkv=(1, 0, 2, 3, 4), out=(1, 2, 0, 3, 4), ff1=(1, 2, 0, 3, 4), ff2=(1, 0, 2, 3, 4))


def matrices(dim, ff):
    return (("qkv", 0, 3 * dim), ("out", 3 * dim, dim), ("ff1", 4 * dim, ff))


def enter_kernel(
    repeat, groups,
    shard3, shard_ff2, small, tokens,
    all3_out, ff2_out, params_out, ffb_out, q_out, kv_out,
    stage, all3, all_ff2, smalls, params, pack_q, pack_kv, q_rows, window,
    y_sems, small_send, small_recv, gather_send, gather_recv, q_send, q_recv,
    kv_send, kv_recv, near_send, near_recv, side_send, side_recv, local,
):
    place = Place(repeat, groups)
    dim, joined = all3.shape
    ff = all_ff2.shape[0]
    tok = tokens.shape[0]
    unit_rows = dim // 32
    slab = 2 * unit_rows
    own_ff2 = pltpu.make_async_copy(
        shard_ff2, all_ff2.at[rows_at(place.unit * (ff // 32), ff // 32)], local.at[0]
    )
    own_ff2.start()
    smalls[rows_at(place.unit * 16, 16)] = small[...]
    place.greet()
    cuts = matrices(dim, ff)
    y_copies = []
    def half_columns(at, half):
        name, first, width = cuts[at]
        return (slice(None), rows_at(first + half * (width // 2), width // 2, 128))

    for at in range(3):
        mine, other = half_columns(at, place.bit(0)), half_columns(at, 1 - place.bit(0))
        out = remote(shard3.at[other], stage.at[other], y_sems.at[at], y_sems.at[4 + at], place.partner(0))
        back = remote(shard3.at[mine], stage.at[mine], y_sems.at[at], y_sems.at[4 + at], place.partner(0))
        out.start()
        y_copies.append((out, back))

    def small_copy(phase):
        rows = rows_at(div(place.unit, 1 << phase) * (16 << phase), 16 << phase)
        other = div(place.unit, 1 << phase) + (1 - 2 * place.bit(phase))
        there = rows_at(other * (16 << phase), 16 << phase)
        return [
            remote(smalls.at[part], smalls.at[part], small_send.at[phase], small_recv.at[phase], place.partner(phase))
            for part in (rows, there)
        ]

    small_copy(0)[0].start()
    gathers = {
        name: Gather(place, all3, slab, first, width, AG_PLAN[name], True) for name, first, width in cuts
    }
    gathers["ff2"] = Gather(place, all_ff2, ff // 16, 0, dim, AG_PLAN["ff2"], False)
    here = rows_at(div(place.unit, 2) * slab, slab)

    def merge(at):
        y_copies[at][1].wait_recv()
        name, first, width = cuts[at]
        low = place.bit(0) == 0
        for column in range(0, width // 2, 384):
            part = rows_at(first + place.bit(0) * (width // 2) + column, 384, 128)
            mine, other = shard3[:unit_rows, part].astype(F32), stage[:unit_rows, part].astype(F32)
            whole = jnp.concatenate([jnp.where(low, mine, other), jnp.where(low, other, mine)], axis=0)
            all3[here, part] = whole.astype(BF16)
        gathers[name].begin(gather_send.at[at], gather_recv.at[at])

    merge(0)
    own_ff2.wait()
    gathers["ff2"].begin(gather_send.at[3], gather_recv.at[3])
    merge(2)
    merge(1)
    for phase in range(5):
        small_copy(phase)[1].wait_recv()
        if phase < 4:
            small_copy(phase + 1)[0].start()
        gathers["qkv"].step(phase)
        if phase < 2:
            for name in ("ff2", "ff1", "out"):
                gathers[name].step(phase)
    params[...] = spread_rows(smalls[...], unit_rows, dim, None)
    rows16 = lax.broadcasted_iota(jnp.int32, (32, 512), 0) * 16 + 8
    chosen = (rows16 == lax.broadcasted_iota(jnp.int32, (32, 512), 1)).astype(BF16)
    ffb_out[...] = jnp.broadcast_to(
        spread_rows(nn(chosen, smalls[...]).astype(BF16), ff // 32, ff, 0), ffb_out.shape
    )
    params_out[...] = params[...]
    rows = tokens[...]
    values = []
    for part, bias in ((0, 4), (1, None), (2, 5)):
        made = nn(rows, all3[:, part * dim:(part + 1) * dim])
        if bias is not None:
            made = made + params[bias:bias + 1, :]
        values.append(made)
    for chip in range(CHIPS):
        cut = slice(HW * chip, HW * (chip + 1))
        pack_kv[chip] = jnp.concatenate([values[1][:, cut], values[2][:, cut]], axis=1).astype(BF16)
    mine = rows_at(4 * tok * place.x + 2 * tok * place.core + tok * place.y, tok)

    def kv_copy(dx, dy):
        tx, ty = rem(place.x + dx, 2), rem(place.y + dy, 2)
        at = 2 * dx + dy
        src = pack_kv.at[2 * tx + ty]
        out = remote(src, window.at[1].at[mine], kv_send.at[at], kv_recv.at[at], place.member(tx, place.core, ty))
        there = rows_at(4 * tok * tx + 2 * tok * place.core + tok * ty, tok)
        back = remote(src, window.at[1].at[there], kv_send.at[at], kv_recv.at[at], place.member(tx, place.core, ty))
        return out, back

    for dx, dy in ((1, 1), (1, 0), (0, 1)):
        kv_copy(dx, dy)[0].start()
    window[1, mine] = pack_kv[2 * place.x + place.y]
    for chip in range(CHIPS):
        cut = slice(HW * chip, HW * (chip + 1))
        pack_q[chip] = jnp.concatenate([values[0][:, cut], jnp.zeros((tok, QW - HW), F32)], axis=1).astype(BF16)
    to_heads(place, pack_q, q_rows, q_send, q_recv)

    sibling = place.member(place.x, 1 - place.core, place.y)

    def stretch(slot, half, core):
        return window.at[slot].at[rows_at(4 * tok * half + 2 * tok * core, 2 * tok)]

    def near(slot, half, arriving=False):
        ref = stretch(slot, half, 1 - place.core if arriving else place.core)
        at = 2 * slot + half
        return remote(ref, ref, near_send.at[at], near_recv.at[at], sibling)

    def side(step, half):
        at = (1 - step) + half
        return remote(
            stretch(1, half, place.core), stretch(1 - step, half, place.core), side_send.at[at], side_recv.at[at],
            place.beside(step),
        )

    for dx, dy in ((1, 1), (1, 0), (0, 1)):
        kv_copy(dx, dy)[1].wait_recv()
    for half in range(2):
        for step in (1, -1):
            side(step, half).start()
    for half in range(2):
        near(1, half).start()
    for phase in range(2, 5):
        for name in ("ff2", "ff1", "out"):
            gathers[name].step(phase)
    for gather in gathers.values():
        gather.finish()
    copies = [
        pltpu.make_async_copy(all3, all3_out, local.at[0]),
        pltpu.make_async_copy(all_ff2, ff2_out, local.at[1]),
    ]
    for copy in copies:
        copy.start()
    for half in range(2):
        for step in (1, -1):
            side(step, half).wait_recv()
            near(1 - step, half).start()
    for slot in range(3):
        for half in range(2):
            near(slot, half, True).wait_recv()
    to_heads_wait(place, pack_q, q_rows, q_send, q_recv)
    last = [
        pltpu.make_async_copy(q_rows, q_out, local.at[2]),
        pltpu.make_async_copy(window, kv_out, local.at[3]),
    ]
    for copy in last:
        copy.start()
    for out, back in y_copies:
        out.wait_send()
    for phase in range(5):
        small_copy(phase)[0].wait_send()
    for dx, dy in ((1, 1), (1, 0), (0, 1)):
        kv_copy(dx, dy)[0].wait_send()
    for half in range(2):
        for step in (1, -1):
            side(step, half).wait_send()
        for slot in range(3):
            near(slot, half).wait_send()
    to_heads_drain(place, pack_q, q_rows, q_send, q_recv)
    for copy in copies + last:
        copy.wait()


VM = pl.BlockSpec(memory_space=pltpu.VMEM)
HBM = pl.BlockSpec(memory_space=pl.ANY)
DMA = pltpu.SemaphoreType.DMA


def enter(repeat, groups, shard3, shard_ff2, small, tokens):
    tok, dim = tokens.shape
    joined = shard3.shape[1]
    ff = shard_ff2.shape[0] * 32
    shape = jax.ShapeDtypeStruct
    return pl.pallas_call(
        functools.partial(enter_kernel, repeat, groups),
        out_shape=(
            shape((dim, joined), BF16), shape((ff, dim), BF16), shape((16, dim), F32), shape((8, ff), F32),
            shape((4 * tok, QW), BF16), shape((3, 8 * tok, KW), BF16),
        ),
        in_specs=[VM] * 4,
        out_specs=(HBM, HBM, VM, VM, HBM, HBM),
        scratch_shapes=[
            pltpu.VMEM(shard3.shape, BF16), pltpu.VMEM((dim, joined), BF16), pltpu.VMEM((ff, dim), BF16),
            pltpu.VMEM((512, 128), BF16), pltpu.VMEM((16, dim), F32),
            pltpu.VMEM((CHIPS, tok, QW), BF16), pltpu.VMEM((CHIPS, tok, KW), BF16),
            pltpu.VMEM((4 * tok, QW), BF16), pltpu.VMEM((3, 8 * tok, KW), BF16),
            DMA((8,)), DMA((5,)), DMA((5,)), DMA((4, 31)), DMA((4, 31)), DMA((4,)), DMA((4,)),
            DMA((4,)), DMA((4,)), DMA((6,)), DMA((6,)), DMA((4,)), DMA((4,)), DMA((4,)),
        ],
        compiler_params=pltpu.CompilerParams(
            collective_id=1, has_side_effects=True, vmem_limit_bytes=VMEM_BYTES
        ),
    )(shard3, shard_ff2, small, tokens)


def pack_small(norm_gains, norm_biases, proj_biases, ff_bias):
    rows = jnp.concatenate([norm_gains, norm_biases, proj_biases], axis=0)
    rows = jnp.pad(rows, ((0, 0), (0, 128 - rows.shape[1])))
    hidden = jnp.pad(ff_bias, (0, 128 - ff_bias.shape[0]))[None]
    return jnp.concatenate([rows, hidden, jnp.zeros((7, 128), rows.dtype)], axis=0)


QT = 512
KT = 512


def lane_mask(shape, low, high, axis):
    lane = lax.broadcasted_iota(jnp.int32, shape, axis)
    return (lane >= low) & (lane < high)


HEAD_QUERY = ((0, 0), (0, 64), (128, 0))
HEAD_VALUE = ((128, 64), (256, 0), (256, 64))
HEAD_CONTEXT = ((0, 64), (128, 0), (128, 64))


def head_rows(ref, rows, spot):
    tile, place = spot
    part = ref[rows, tile:tile + 128]
    return jnp.where(lane_mask(part.shape, place, place + HD, 1), part, jnp.zeros_like(part))


def forward_kernel(bounds, queries, window, query_ids, key_ids, context_out, sums_out):
    count = queries.shape[0]
    scale = HD ** (-0.5)

    def tile(at, carry):
        rows = rows_at(at * QT, QT)
        ids = query_ids[0:1, rows_at(at * QT, QT, 128)]
        parts = []
        scaled = [head_rows(queries, rows, HEAD_QUERY[head]) * jnp.asarray(scale, BF16) for head in range(3)]

        def visit(j, state):
            keys = rows_at(j * KT, KT)
            allowed = jnp.concatenate([key_ids[keys, :]] * (QT // 128), axis=1) == ids
            tops, terms, fresh = [], [], []
            scores = [
                jnp.where(allowed, nt(window[keys, tile_at:tile_at + 128], scaled[head]), NEGATIVE)
                for head, (tile_at, place) in enumerate(HEAD_QUERY)
            ]
            for head in range(3):
                tops.append(jnp.maximum(state[3 * head], jnp.max(scores[head], axis=0, keepdims=True)))
            for head in range(3):
                terms.append(jnp.exp(scores[head] - tops[head]))
            for head in range(3):
                highest, total, weighted = state[3 * head:3 * head + 3]
                tile_at = HEAD_VALUE[head][0]
                factor = jnp.exp(highest - tops[head])
                total = total * factor + jnp.sum(terms[head], axis=0, keepdims=True)
                weighted = weighted * factor + tn(window[keys, tile_at:tile_at + 128], terms[head].astype(BF16))
                fresh += [tops[head], total, weighted]
            return tuple(fresh)

        start = []
        for head in range(3):
            start += [jnp.full((1, QT), NEGATIVE, F32), jnp.zeros((1, QT), F32), jnp.zeros((128, QT), F32)]
        state = lax.fori_loop(bounds[0, at], bounds[1, at], visit, tuple(start))
        made = []
        for head in range(3):
            highest, total, weighted = state[3 * head:3 * head + 3]
            whole = weighted / total
            place = HEAD_CONTEXT[head][1]
            made.append(jnp.where(lane_mask(whole.shape, place, place + HD, 0), whole, 0.0))
            sums_out[head:head + 1, rows_at(at * QT, QT, 128)] = highest + jnp.log(total)
        context_out[rows, 0:128] = made[0].T
        context_out[rows, 128:256] = (made[1] + made[2]).T
        return carry

    lax.fori_loop(0, count // QT, tile, 0)


SM = pl.BlockSpec(memory_space=pltpu.SMEM)


def forward(bounds, queries, window, query_ids, key_ids):
    count = queries.shape[0]
    shape = jax.ShapeDtypeStruct
    return pl.pallas_call(
        forward_kernel,
        out_shape=(shape((count, QW), F32), shape((8, count), F32)),
        in_specs=[SM] + [VM] * 4,
        out_specs=(VM, VM),
        compiler_params=pltpu.CompilerParams(vmem_limit_bytes=VMEM_BYTES),
    )(bounds, queries, window, query_ids, key_ids)


def backward_kernel(bounds, queries, window, query_ids, key_ids, context, grads, sums, query_out, window_out, acc):
    count = queries.shape[0]
    scale = HD ** (-0.5)
    acc[...] = jnp.zeros_like(acc)

    def tile(at, carry):
        rows = rows_at(at * QT, QT)
        ids = query_ids[0:1, rows_at(at * QT, QT, 128)]
        scaled, grad, delta, sum_rows = [], [], [], []
        for head in range(3):
            scaled.append(head_rows(queries, rows, HEAD_QUERY[head]) * jnp.asarray(scale, BF16))
            mine = head_rows(grads, rows, HEAD_CONTEXT[head])
            tile_at = HEAD_CONTEXT[head][0]
            product = mine.astype(F32) * context[rows, tile_at:tile_at + 128]
            grad.append(mine)
            delta.append(
                lax.dot_general(
                    jnp.ones((8, 128), F32), product, (((1,), (1,)), ((), ())),
                    precision=lax.Precision.HIGHEST, preferred_element_type=F32,
                )[0:1]
            )
            sum_rows.append(sums[head:head + 1, rows_at(at * QT, QT, 128)])

        def visit(j, state):
            keys = rows_at(j * KT, KT)
            allowed = jnp.concatenate([key_ids[keys, :]] * (QT // 128), axis=1) == ids
            fresh, key_grads, value_grads = [], [], []
            for head in range(3):
                key = window[keys, HEAD_QUERY[head][0]:HEAD_QUERY[head][0] + 128]
                value = window[keys, HEAD_VALUE[head][0]:HEAD_VALUE[head][0] + 128]
                probs = jnp.where(allowed, jnp.exp(nt(key, scaled[head]) - sum_rows[head]), 0.0)
                spread = nt(value, grad[head])
                steps = (probs * (spread - delta[head])).astype(BF16)
                value_grads.append(nn(probs.astype(BF16), grad[head]))
                key_grads.append(nn(steps, scaled[head]))
                fresh.append(state[head] + tn(key, steps))
            acc[keys, 0:128] += key_grads[0] + key_grads[1]
            acc[keys, 128:256] += key_grads[2] + value_grads[0]
            acc[keys, 256:384] += value_grads[1] + value_grads[2]
            return tuple(fresh)

        state = lax.fori_loop(
            bounds[0, at], bounds[1, at], visit, tuple(jnp.zeros((128, QT), F32) for _ in range(3))
        )
        made = []
        for head in range(3):
            place = HEAD_QUERY[head][1]
            made.append(jnp.where(lane_mask(state[head].shape, place, place + HD, 0), state[head] * scale, 0.0))
        query_out[rows, 0:128] = (made[0] + made[1]).T.astype(BF16)
        query_out[rows, 128:256] = made[2].T.astype(BF16)
        return carry

    lax.fori_loop(0, count // QT, tile, 0)

    def store(at, carry):
        rows = rows_at(at * KT, KT)
        window_out[rows, :] = acc[rows, :].astype(BF16)
        return carry

    lax.fori_loop(0, acc.shape[0] // KT, store, 0)


def backward(bounds, queries, window, query_ids, key_ids, context, grads, sums):
    shape = jax.ShapeDtypeStruct
    return pl.pallas_call(
        backward_kernel,
        out_shape=(shape(queries.shape, BF16), shape(window.shape, BF16)),
        in_specs=[SM] + [VM] * 7,
        out_specs=(VM, VM),
        scratch_shapes=[pltpu.VMEM(window.shape, F32)],
        compiler_params=pltpu.CompilerParams(vmem_limit_bytes=VMEM_BYTES),
    )(bounds, queries, window, query_ids, key_ids, context, grads, sums)


def doc_tables(doc_starts, core, group, half_rows, total_rows):
    window = 6 * half_rows
    live = jnp.sum((doc_starts < total_rows).astype(jnp.int32))

    def ids(places):
        return lax.rem(jnp.sum((doc_starts[None, :] <= places[:, None]).astype(jnp.int32), axis=1), live)

    start = group * 2 * half_rows
    key_ids = ids(jnp.mod(start - 2 * half_rows + jnp.arange(window, dtype=jnp.int32), total_rows))
    query_ids = lax.dynamic_slice_in_dim(key_ids, 2 * half_rows + core * half_rows, half_rows)
    tiles = query_ids.reshape(-1, QT)
    keys = key_ids.reshape(1, -1, KT)

    def any_tile(edge):
        return jnp.any(keys == edge[:, None, None], axis=2)

    order = jnp.arange(window // KT, dtype=jnp.int32)[None]
    low = jnp.min(jnp.where(any_tile(tiles[:, 0]), order, window), axis=1)
    high = jnp.max(jnp.where(any_tile(tiles[:, -1]), order + 1, 0), axis=1)
    return (
        jnp.stack([low, high]),
        jnp.broadcast_to(query_ids[None], (8, half_rows)),
        jnp.broadcast_to(key_ids[:, None], (window, 128)),
    )


def norm_forward(values):
    center = values - jnp.mean(values, axis=-1, keepdims=True)
    scale = lax.rsqrt(jnp.mean(center * center, axis=-1, keepdims=True) + EPSILON)
    return center * scale, scale


def norm_backward(grad, unit_rows, scale, gain):
    inner = grad * gain
    gain_row = jnp.sum(grad * unit_rows, axis=0, keepdims=True)
    shift_row = jnp.sum(grad, axis=0, keepdims=True)
    back = scale * (
        inner
        - jnp.mean(inner, axis=-1, keepdims=True)
        - unit_rows * jnp.mean(inner * unit_rows, axis=-1, keepdims=True)
    )
    return back, gain_row, shift_row


def column_sum(values):
    return jnp.sum(values.astype(F32), axis=0, keepdims=True)


def middle_kernel(
    repeat, groups,
    context, tokens, d_out, params, ffb, all3, all_ff2,
    out, d_mid_out, grads_out, grad_o3, grad_ff2, sum_rows,
    w_out, w_ff1, w_ff2, ctx_rows, parts, pack, grad_rows, act, slope, d_pre,
    send, recv, back_send, back_recv, local,
):
    place = Place(repeat, groups)
    tok, dim = tokens.shape
    ff = w_ff1.shape[1]
    loads = [
        pltpu.make_async_copy(all3.at[:, pl.ds(3 * dim, dim)], w_out, local.at[0]),
        pltpu.make_async_copy(all3.at[:, pl.ds(4 * dim, ff)], w_ff1, local.at[1]),
        pltpu.make_async_copy(all_ff2, w_ff2, local.at[2]),
    ]
    for load in loads:
        load.start()
    ctx_rows[...] = context[...].astype(BF16)
    place.greet(cube=False, beside=False)
    to_tokens(place, ctx_rows, parts, send, recv)
    to_tokens_wait(place, ctx_rows, parts, send, recv)
    joined = jnp.concatenate([parts[chip][:, QW - HW:].astype(F32) for chip in range(CHIPS)], axis=1).astype(BF16)
    loads[0].wait()
    gains, shifts = [params[at:at + 1, :] for at in (0, 1)], [params[at:at + 1, :] for at in (2, 3)]
    mid = tokens[...].astype(F32) + (nn(joined, w_out[...]) + params[6:7, :])
    unit_first, scale_first = norm_forward(mid)
    hidden = unit_first * gains[0] + shifts[0]
    low = hidden.astype(BF16)
    loads[1].wait()
    loads[2].wait()
    ff_out = jnp.zeros((tok, dim), F32)
    for first in range(0, ff, dim):
        cut = slice(first, first + dim)
        pre = nn(low, w_ff1[:, cut]) + ffb[0:1, cut]
        bell = 0.5 * (1.0 + lax.erf(pre * 0.7071067811865476))
        made = (pre * bell).astype(BF16)
        act[:, cut] = made
        slope[:, cut] = bell + pre * jnp.exp(-0.5 * pre * pre) * 0.3989422804014327
        ff_out = ff_out + nn(made, w_ff2[cut, :])
    unit_second, scale_second = norm_forward(hidden + (ff_out + params[7:8, :]))
    out[...] = (unit_second * gains[1] + shifts[1]).astype(BF16)
    d_sum, gain_second, shift_second = norm_backward(d_out[...].astype(F32), unit_second, scale_second, gains[1])
    d_ff = d_sum.astype(BF16)
    d_hidden = d_sum
    for first in range(0, ff, dim):
        cut = slice(first, first + dim)
        made = (nt(d_ff, w_ff2[cut, :]) * slope[:, cut]).astype(BF16)
        d_pre[:, cut] = made
        d_hidden = d_hidden + nt(made, w_ff1[:, cut])
    d_mid, gain_first, shift_first = norm_backward(d_hidden, unit_first, scale_first, gains[0])
    d_mid_out[...] = d_mid
    d_attn = d_mid.astype(BF16)
    d_context = nt(d_attn, w_out[...])
    for chip in range(CHIPS):
        pack[chip] = jnp.concatenate(
            [jnp.zeros((tok, QW - HW), F32), d_context[:, HW * chip:HW * (chip + 1)]], axis=1
        ).astype(BF16)
    to_heads(place, pack, grad_rows, back_send, back_recv)
    for first in range(0, ff, dim):
        cut = slice(first, first + dim)
        grad_ff2[cut, :] = tn(act[:, cut], d_ff).astype(BF16)
        grad_o3[:, dim + first:2 * dim + first] = tn(low, d_pre[:, cut]).astype(BF16)
        sum_rows[8 + first // dim:9 + first // dim, :] = column_sum(d_pre[:, cut])
    grad_o3[:, 0:dim] = tn(joined, d_attn).astype(BF16)
    for at, row in enumerate(
        (
            gain_first, gain_second, shift_first, shift_second,
            jnp.zeros((1, dim), F32), jnp.zeros((1, dim), F32), column_sum(d_attn), column_sum(d_ff),
        )
    ):
        sum_rows[at:at + 1, :] = row
    sum_rows[8 + ff // dim:, :] = jnp.zeros((8 - ff // dim, dim), F32)
    to_heads_wait(place, pack, grad_rows, back_send, back_recv)
    grads_out[...] = grad_rows[...]
    to_tokens_drain(place, ctx_rows, parts, send, recv)
    to_heads_drain(place, pack, grad_rows, back_send, back_recv)


def middle(repeat, groups, context, tokens, d_out, params, ffb, all3, all_ff2):
    tok, dim = tokens.shape
    ff = all_ff2.shape[0]
    shape = jax.ShapeDtypeStruct
    vm = pltpu.VMEM
    return pl.pallas_call(
        functools.partial(middle_kernel, repeat, groups),
        out_shape=(
            shape((tok, dim), BF16), shape((tok, dim), F32), shape((4 * tok, QW), BF16),
            shape((dim, dim + ff), BF16), shape((ff, dim), BF16), shape((16, dim), F32),
        ),
        in_specs=[VM] * 5 + [HBM] * 2,
        out_specs=(VM,) * 6,
        scratch_shapes=[
            vm((dim, dim), BF16), vm((dim, ff), BF16), vm((ff, dim), BF16), vm((4 * tok, QW), BF16),
            vm((CHIPS, tok, QW), BF16), vm((CHIPS, tok, QW), BF16), vm((4 * tok, QW), BF16),
            vm((tok, ff), BF16), vm((tok, ff), F32), vm((tok, ff), BF16),
            DMA((4,)), DMA((4,)), DMA((4,)), DMA((4,)), DMA((4,)),
        ],
        compiler_params=pltpu.CompilerParams(collective_id=2, has_side_effects=True, vmem_limit_bytes=VMEM_BYTES),
    )(context, tokens, d_out, params, ffb, all3, all_ff2)


def leave_kernel(
    repeat, groups,
    d_query, d_window, tokens, d_mid, sum_rows, all3, grad_o3, grad_ff2_in,
    d_tokens, g_qkv, g_out, g_ff1, g_ff2, g_rows,
    w_qkv, grad3, grad_ff2, land_qkv, land_out, land_ff1, land_ff2,
    near_land, side_land, stretch_sum, kv_parts, q_parts, joined, swap_out, swap_in, rows_mine, rows_land,
    grad_send, grad_recv, near_send, near_recv, side_send, side_recv, kv_send, kv_recv,
    q_send, q_recv, swap_send, swap_recv, rows_send, rows_recv, local,
):
    place = Place(repeat, groups)
    tok, dim = tokens.shape
    ff = grad_ff2.shape[0]
    unit_rows = dim // 32
    loads = [
        pltpu.make_async_copy(grad_o3, grad3.at[:, pl.ds(3 * dim, dim + ff)], local.at[0]),
        pltpu.make_async_copy(grad_ff2_in, grad_ff2, local.at[1]),
        pltpu.make_async_copy(all3.at[:, pl.ds(0, 3 * dim)], w_qkv, local.at[2]),
    ]
    for load in loads:
        load.start()
    place.greet()
    sibling = place.member(place.x, 1 - place.core, place.y)

    def stretch(slot, half, core):
        return rows_at(4 * tok * half + 2 * tok * core, 2 * tok)

    def near(slot, half):
        at = 2 * slot + half
        return remote(
            d_window.at[slot].at[stretch(slot, half, 1 - place.core)], near_land.at[at],
            near_send.at[at], near_recv.at[at], sibling,
        )

    order = (0, 2, 1)
    for slot in order:
        for half in range(2):
            near(slot, half).start()
    to_tokens(place, d_query, q_parts, q_send, q_recv)
    cuts = matrices(dim, ff)
    slab = 2 * unit_rows
    scatters = {
        name: Scatter(place, grad3, slab, first, width, RS_PLAN[name], True) for name, first, width in cuts
    }
    scatters["ff2"] = Scatter(place, grad_ff2, ff // 16, 0, dim, RS_PLAN["ff2"], False)
    lands = dict(qkv=land_qkv, out=land_out, ff1=land_ff1, ff2=land_ff2)

    def begin(name, at):
        scatters[name].begin(lands[name], grad_send.at[at], grad_recv.at[at])

    def side(slot, half):
        at = slot + half
        return remote(
            stretch_sum.at[at], side_land.at[at], side_send.at[at], side_recv.at[at],
            place.beside(-1 if slot == 0 else 1),
        )

    def add_near(slot, half, target):
        near(slot, half).wait_recv()
        at = 2 * slot + half
        mine = d_window[slot, stretch(slot, half, place.core)].astype(F32) + near_land[at].astype(F32)
        target[...] = mine.astype(BF16)

    loads[0].wait()
    loads[1].wait()
    begin("ff2", 3)
    for slot in (0, 2):
        for half in range(2):
            add_near(slot, half, stretch_sum.at[slot + half])
            side(slot, half).start()
    begin("ff1", 2)
    begin("out", 1)
    for phase in range(2):
        for name in ("ff2", "ff1", "out"):
            scatters[name].step(phase)

    def kv_copy(dx, dy):
        tx, ty = rem(place.x + dx, 2), rem(place.y + dy, 2)
        at = 2 * dx + dy
        return remote(
            stretch_sum.at[4 + tx].at[rows_at(tok * ty, tok)], kv_parts.at[2 * place.x + place.y],
            kv_send.at[at], kv_recv.at[at], place.member(tx, place.core, ty),
        )

    for half in range(2):
        near(1, half).wait_recv()
        at = 2 + half
        total = d_window[1, stretch(1, half, place.core)].astype(F32) + near_land[at].astype(F32)
        for slot in (0, 2):
            side(slot, half).wait_recv()
            total = total + side_land[slot + half].astype(F32)
        stretch_sum[4 + half] = total.astype(BF16)
    for dx, dy in ((1, 1), (1, 0), (0, 1)):
        kv_copy(dx, dy).start()
    kv_parts[2 * place.x + place.y] = stretch_sum[4 + place.x, rows_at(tok * place.y, tok)]
    to_tokens_wait(place, d_query, q_parts, q_send, q_recv)
    joined[:, 0:dim] = jnp.concatenate(
        [q_parts[chip][:, :HW].astype(F32) for chip in range(CHIPS)], axis=1
    ).astype(BF16)
    for dx, dy in ((1, 1), (1, 0), (0, 1)):
        kv_copy(dx, dy).wait_recv()
    for at in range(2):
        joined[:, (1 + at) * dim:(2 + at) * dim] = jnp.concatenate(
            [kv_parts[chip][:, HW * at:HW * (at + 1)].astype(F32) for chip in range(CHIPS)], axis=1
        ).astype(BF16)
    for part in range(3):
        cut = slice(part * dim, (part + 1) * dim)
        grad3[:, cut] = tn(tokens[...], joined[:, cut]).astype(BF16)
    begin("qkv", 0)
    rows_mine[0] = sum_rows[...]
    rows_mine[0, 4:5, :] = column_sum(joined[:, 0:dim])
    rows_mine[0, 5:6, :] = column_sum(joined[:, 2 * dim:3 * dim])

    def rows_copy(phase):
        return remote(
            rows_mine.at[phase], rows_land.at[phase], rows_send.at[phase], rows_recv.at[phase], place.partner(phase)
        )

    def rows_add(phase):
        rows_copy(phase).wait_recv()
        rows_mine[phase + 1] = rows_mine[phase] + rows_land[phase]
        if phase < 4:
            rows_copy(phase + 1).start()

    rows_copy(0).start()

    def swap(at):
        name, first, width = cuts[at]
        part = (slice(None), pl.ds(first // 2, width // 2))
        return remote(swap_out.at[part], swap_in.at[part], swap_send.at[at], swap_recv.at[at], place.partner(0))

    def finish_half(at):
        name, first, width = cuts[at]
        target = (g_qkv, g_out, g_ff1)[at]
        total = scatters[name].last()
        high = place.bit(0) == 1
        keep = jnp.where(high, total[unit_rows:], total[:unit_rows])
        give = jnp.where(high, total[:unit_rows], total[unit_rows:])
        pad = jnp.zeros((swap_out.shape[0] - unit_rows, give.shape[1]), F32)
        swap_out[:, first // 2:(first + width) // 2] = jnp.concatenate([give, pad], axis=0).astype(BF16)
        swap(at).start()
        target[:, rows_at(place.bit(0) * (width // 2), width // 2, 128)] = keep

    def finish_swap(at):
        name, first, width = cuts[at]
        target = (g_qkv, g_out, g_ff1)[at]
        swap(at).wait_recv()
        other = swap_in[:, first // 2:(first + width) // 2].astype(F32)[:unit_rows]
        target[:, rows_at((1 - place.bit(0)) * (width // 2), width // 2, 128)] = other

    loads[2].wait()
    d_tokens[...] = (d_mid[...] + nt(joined[...], w_qkv[...])).astype(BF16)
    for phase in range(4):
        if phase >= 2:
            for name in ("ff2", "ff1", "out"):
                scatters[name].step(phase)
        scatters["qkv"].step(phase)
        rows_add(phase)
    rows_add(4)
    g_ff2[...] = scatters["ff2"].last()
    for at in (2, 1, 0):
        finish_half(at)
    for at in (2, 1, 0):
        finish_swap(at)
    g_rows[...] = rows_mine[5]
    for phase in range(5):
        rows_copy(phase).wait_send()
    for scatter in scatters.values():
        scatter.finish()
    for at in range(3):
        swap(at).wait_send()
    for slot in range(3):
        for half in range(2):
            near(slot, half).wait_send()
    for slot in (0, 2):
        for half in range(2):
            side(slot, half).wait_send()
    for dx, dy in ((1, 1), (1, 0), (0, 1)):
        kv_copy(dx, dy).wait_send()
    to_tokens_drain(place, d_query, q_parts, q_send, q_recv)


def leave(repeat, groups, d_query, d_window, tokens, d_mid, sum_rows, all3, grad_o3, grad_ff2):
    tok, dim = tokens.shape
    ff = grad_ff2.shape[0]
    unit = dim // 32
    slab = 2 * unit
    shape = jax.ShapeDtypeStruct
    vm = pltpu.VMEM
    return pl.pallas_call(
        functools.partial(leave_kernel, repeat, groups),
        out_shape=(
            shape((tok, dim), BF16), shape((unit, 3 * dim), F32), shape((unit, dim), F32), shape((unit, ff), F32),
            shape((ff // 32, dim), F32), shape((16, dim), F32),
        ),
        in_specs=[VM] * 5 + [HBM] * 3,
        out_specs=(VM,) * 6,
        scratch_shapes=[
            vm((dim, 3 * dim), BF16), vm((dim, 4 * dim + ff), BF16), vm((ff, dim), BF16),
            vm((31, slab, 3 * dim // 2), BF16), vm((31, slab, dim // 2), BF16), vm((31, slab, ff // 2), BF16),
            vm((31, ff // 32, dim), BF16),
            vm((6, 2 * tok, KW), BF16), vm((4, 2 * tok, KW), BF16), vm((6, 2 * tok, KW), BF16),
            vm((CHIPS, tok, KW), BF16), vm((CHIPS, tok, QW), BF16), vm((tok, 3 * dim), BF16),
            vm((-(-unit // 16) * 16, (4 * dim + ff) // 2), BF16), vm((-(-unit // 16) * 16, (4 * dim + ff) // 2), BF16),
            vm((6, 16, dim), F32), vm((5, 16, dim), F32),
            DMA((4, 31)), DMA((4, 31)), DMA((6,)), DMA((6,)), DMA((4,)), DMA((4,)), DMA((4,)), DMA((4,)),
            DMA((4,)), DMA((4,)), DMA((3,)), DMA((3,)), DMA((5,)), DMA((5,)), DMA((3,)),
        ],
        compiler_params=pltpu.CompilerParams(collective_id=3, has_side_effects=True, vmem_limit_bytes=VMEM_BYTES),
    )(d_query, d_window, tokens, d_mid, sum_rows, all3, grad_o3, grad_ff2)


def gather_repeat(value, repeat, axis):
    if repeat == 1:
        return value
    count = repeat // 2
    sets = [list(range(at, at + count)) for at in range(0, lax.axis_size("blk"), count)]
    value = lax.all_gather(value, "head", axis=axis, tiled=True)
    if count == 1:
        return value
    return lax.all_gather(value, "blk", axis=axis, tiled=True, axis_index_groups=sets)


def own_share(value, repeat, axis):
    if repeat == 1:
        return value
    count = repeat // 2
    sets = [list(range(at, at + count)) for at in range(0, lax.axis_size("blk"), count)]
    value = lax.psum(value, "head")
    if count > 1:
        value = lax.psum(value, "blk", axis_index_groups=sets)
    size = value.shape[axis] // repeat
    at = jnp.mod(lax.axis_index("blk") * 2 + lax.axis_index("head"), repeat)
    return lax.dynamic_slice_in_dim(value, at * size, size, axis)


def body(tokens, w_qkv, w_out, w_ff1, w_ff2, norm_gains, norm_biases, proj_biases, ff_bias, doc_starts, d_out):
    blks = lax.axis_size("blk")
    repeat = blks * 2 // 32
    groups = blks // GROUP
    tok, dim = tokens.shape
    half_rows = 4 * tok
    total_rows = blks * 2 * tok
    blk = lax.axis_index("blk")
    joined = gather_repeat(jnp.concatenate([w_qkv, w_out, w_ff1], axis=1), repeat, 0)
    joined = jnp.pad(joined, ((0, -joined.shape[0] % 16), (0, 0)))
    shard_ff2 = gather_repeat(w_ff2, repeat, 0)
    small = pack_small(
        gather_repeat(norm_gains, repeat, 1), gather_repeat(norm_biases, repeat, 1),
        gather_repeat(proj_biases, repeat, 1), gather_repeat(ff_bias, repeat, 0),
    )
    bounds, query_ids, key_ids = doc_tables(
        doc_starts, lax.rem(blk, 2), lax.div(blk, GROUP), half_rows, total_rows
    )
    all3, all_ff2, params, ffb, queries, window = enter(repeat, groups, joined, shard_ff2, small, tokens)
    window = window.reshape(6 * half_rows, KW)
    context, sums = forward(bounds, queries, window, query_ids, key_ids)
    out, d_mid, grads, grad_o3, grad_ff2, sum_rows = middle(
        repeat, groups, context, tokens, d_out, params, ffb, all3, all_ff2
    )
    d_query, d_window = backward(bounds, queries, window, query_ids, key_ids, context, grads, sums)
    d_tokens, g_qkv, g_out, g_ff1, g_ff2, g_rows = leave(
        repeat, groups, d_query, d_window.reshape(3, 2 * half_rows, KW), tokens, d_mid, sum_rows, all3, grad_o3, grad_ff2
    )
    unit = lax.div(blk * 2 + lax.axis_index("head"), repeat)
    width = dim // 32
    rows = g_rows
    g_small = lax.dynamic_slice_in_dim(rows[:8], unit * width, width, 1)
    g_hidden = lax.dynamic_slice_in_dim(rows[8:].reshape(-1), unit * shard_ff2.shape[0], shard_ff2.shape[0], 0)
    g_small, g_hidden = own_share(g_small, repeat, 1), own_share(g_hidden, repeat, 0)
    return (
        out, d_tokens, own_share(g_qkv, repeat, 0), own_share(g_out, repeat, 0), own_share(g_ff1, repeat, 0),
        own_share(g_ff2, repeat, 0), g_small[0:2], g_small[2:4], g_small[4:8], g_hidden,
    )


def solution(mesh):
    rows, columns, flat = P(("blk", "head"), None), P(None, ("blk", "head")), P(("blk", "head"))
    return jax.shard_map(
        body,
        mesh=mesh,
        in_specs=(rows,) * 5 + (columns,) * 3 + (flat, P(), rows),
        out_specs=(rows,) * 6 + (columns,) * 3 + (flat,),
        check_vma=False,
    )
```

```python
import functools

import jax
import jax.numpy as jnp
from jax import lax
from jax.experimental import pallas as pl
from jax.experimental.pallas import tpu as pltpu
from jax.sharding import PartitionSpec as P

H = 12
HD = 64
DOC_MOST = 2048
EPSILON = 1e-06
NEGATIVE = -1e30
MESH = pl.DeviceIdType.MESH
F32 = jnp.float32
BF16 = jnp.bfloat16
VMEM_BYTES = 60 * 1024 * 1024
CHIPS = 4
GROUP = 4
QW = 256
KW = 384
HW = (H // CHIPS) * HD
PW = QW + KW


def div(a, b):
    return lax.div(a, jnp.int32(b))


def rem(a, b):
    return lax.rem(a, jnp.int32(b))


def nn(a, b):
    return lax.dot_general(a, b, (((1,), (0,)), ((), ())), preferred_element_type=F32)


def nt(a, b):
    return lax.dot_general(a, b, (((1,), (1,)), ((), ())), preferred_element_type=F32)


def tn(a, b):
    return lax.dot_general(a, b, (((0,), (0,)), ((), ())), preferred_element_type=F32)


def rows_at(start, count, unit=16):
    return pl.ds(pl.multiple_of(start, unit), count)


class Place:
    def __init__(self, repeat, groups):
        self.repeat = repeat
        blk, head = lax.axis_index("blk"), lax.axis_index("head")
        self.index = blk * 2 + head
        self.unit = div(self.index, repeat)
        self.core, self.x, self.y = rem(blk, 2), rem(div(blk, 2), 2), head
        self.group, self.groups = div(blk, GROUP), groups
        self.bits = [rem(div(self.unit, 1 << k), 2) for k in range(5)]
        others = [self.index + (1 - 2 * self.bits[k]) * (repeat << k) for k in range(5)]
        self.partners = [{"blk": div(other, 2), "head": rem(other, 2)} for other in others]

    def bit(self, k):
        return self.bits[k]

    def partner(self, k):
        return self.partners[k]

    def member(self, x, core, y):
        return {"blk": self.group * GROUP + 2 * x + core, "head": y}

    def beside(self, step):
        group = rem(self.group + self.groups + step, self.groups)
        return {"blk": group * GROUP + 2 * self.x + self.core, "head": self.y}

    def greet(self, cube=True, group=True, beside=True):
        barrier = pltpu.get_barrier_semaphore()
        partners = []
        if cube:
            partners += [self.partner(k) for k in range(5)]
        if group:
            partners += [
                self.member(
                    rem(self.x + dx, 2), rem(self.core + dc, 2), rem(self.y + dy, 2)
                )
                for dx in range(2)
                for dc in range(2)
                for dy in range(2)
                if dx + dc + dy
            ]
        if beside:
            partners += [self.beside(1), self.beside(-1)]
        for partner in partners:
            pl.semaphore_signal(barrier, inc=1, device_id=partner, device_id_type=MESH)
        pl.semaphore_wait(barrier, len(partners))


def remote(src, dst, send, recv, device):
    return pltpu.make_async_remote_copy(
        src_ref=src, dst_ref=dst, send_sem=send, recv_sem=recv, device_id=device, device_id_type=MESH
    )


class Pieces:
    def __init__(self, place, ref, rows, first, width, order, by_columns):
        self.place, self.ref, self.rows, self.first, self.width = place, ref, rows, first, width
        self.order, self.by_columns = order, by_columns
        if by_columns is not None:
            self.shape = (rows, width // 2) if by_columns else (rows // 2, width)
        self.deltas = [(1 - 2 * place.bit(k)) * (1 << k) for k in order]
        self.units = {0: place.unit}
        self.own = self.piece(0)

    def unit_of(self, mask):
        if mask not in self.units:
            at = mask.bit_length() - 1
            self.units[mask] = self.unit_of(mask - (1 << at)) + self.deltas[at]
        return self.units[mask]

    def region(self, unit):
        slab, half = div(unit, 2), rem(unit, 2)
        if self.by_columns:
            return (
                rows_at(slab * self.rows, self.rows),
                rows_at(self.first + half * self.shape[1], self.shape[1], 128),
            )
        return (rows_at(unit * self.shape[0], self.shape[0]), pl.ds(self.first, self.width))

    def piece(self, mask):
        return self.ref.at[self.region(self.unit_of(mask))]


class Gather(Pieces):
    def begin(self, send, recv, until=5):
        self.send, self.recv = send, recv
        self.feed(0, 0, until)

    def copy(self, phase, mask, ref):
        at = (1 << phase) - 1 + mask
        return remote(ref, ref, self.send.at[at], self.recv.at[at], self.place.partner(self.order[phase]))

    def feed(self, mask, phase, until=5):
        if phase < until:
            ref = self.piece(mask)
            for later in range(phase, until):
                self.copy(later, mask, ref).start()

    def release(self, phase):
        for mask in range(1 << phase):
            self.feed(mask, phase)

    def step(self, phase, until=5):
        for mask in range(1 << phase):
            self.copy(phase, mask, self.own).wait_recv()
            self.feed(mask + (1 << phase), phase + 1, until)

    def finish(self):
        for phase in range(5):
            for mask in range(1 << phase):
                self.copy(phase, mask, self.own).wait_send()


class Scatter(Pieces):
    def begin(self, landing, send, recv):
        self.landing, self.send, self.recv = landing, send, recv
        for j in range(16):
            self.give(0, j)

    def slot(self, phase, j):
        return 32 - (1 << (5 - phase)) + j

    def copy(self, phase, j, ref):
        at = self.slot(phase, j)
        return remote(
            ref, self.landing.at[at], self.send.at[at], self.recv.at[at], self.place.partner(self.order[phase])
        )

    def give(self, phase, j):
        self.copy(phase, j, self.piece((2 * j + 1) * (1 << phase))).start()

    def absorb(self, phase, j):
        self.copy(phase, j, self.own).wait_recv()
        rows, columns = self.region(self.unit_of(j * (2 << phase)))
        total = self.ref[rows, columns].astype(F32) + self.landing[self.slot(phase, j)].astype(F32)
        self.ref[rows, columns] = total.astype(BF16)
        return total

    def step(self, phase):
        half = 1 << (3 - phase)
        for jj in range(half):
            self.absorb(phase, 2 * jj + 1)
            self.give(phase + 1, jj)
        for jj in range(half):
            self.absorb(phase, 2 * jj)

    def last(self):
        return self.absorb(4, 0)

    def finish(self):
        for phase in range(5):
            for j in range(1 << (4 - phase)):
                self.copy(phase, j, self.own).wait_send()


class GatherBlocks(Gather):
    def __init__(self, place, ref, order):
        self.shape = ref.shape[1:]
        Pieces.__init__(self, place, ref, 0, 0, 0, order, None)

    def piece(self, mask):
        return self.ref.at[self.unit_of(mask)]


class ScatterBlocks(Scatter):
    def __init__(self, place, ref, order, until):
        Pieces.__init__(self, place, ref, 0, 0, 0, order, None)
        self.until = until

    def piece(self, mask):
        return self.ref.at[self.unit_of(mask)]

    def give(self, phase, j):
        if phase < self.until:
            Scatter.give(self, phase, j)

    def absorb(self, phase, j):
        self.copy(phase, j, self.own).wait_recv()
        unit = self.unit_of(j * (2 << phase))
        total = self.ref[unit].astype(F32) + self.landing[self.slot(phase, j)].astype(F32)
        self.ref[unit] = total.astype(BF16)
        return total

    def finish(self):
        for phase in range(self.until):
            for j in range(1 << (4 - phase)):
                self.copy(phase, j, self.own).wait_send()


def to_heads(place, packed, landed, send, recv, part=None):
    tok = packed.shape[1] if part is None else part.shape[0]
    mine = rows_at(2 * tok * place.core + tok * place.y, tok)
    slot = 2 * place.core + place.y
    alone = place.core == place.x
    for dx, dy in ((0, 0), (1, 0), (0, 1), (1, 1)):
        if True:
            tx, ty = rem(place.x + dx, 2), rem(place.y + dy, 2)
            copy = remote(
                packed.at[2 * tx + ty] if part is None else part,
                landed.at[mine],
                send.at[2 * dx + dy],
                recv.at[slot],
                place.member(tx, place.x, ty),
            )
            if dx + dy:
                copy.start()
            else:
                pl.when(jnp.logical_not(alone))(copy.start)

                @pl.when(alone)
                def _(tx=tx, ty=ty):
                    landed[mine] = packed[2 * tx + ty] if part is None else part[...]


def to_heads_wait_one(place, landed, send, recv, cs, ys):
    tok = landed.shape[0] // 4
    part = landed.at[pl.ds(0, tok)]
    copy = remote(part, part, send.at[0], recv.at[2 * cs + ys], place.member(place.x, 1 - place.core, place.y))
    own = (place.core == place.x) & (place.core == cs) & (place.y == ys)
    pl.when(jnp.logical_not(own))(copy.wait_recv)


def to_heads_wait(place, landed, send, recv):
    for cs in range(2):
        for ys in range(2):
            to_heads_wait_one(place, landed, send, recv, cs, ys)


def to_heads_drain(place, landed, send, recv):
    part = landed.at[pl.ds(0, landed.shape[0] // 4)]
    for at in range(4):
        copy = remote(part, part, send.at[at], recv.at[0], place.member(place.x, 1 - place.core, place.y))
        if at:
            copy.wait_send()
        else:
            pl.when(place.core != place.x)(copy.wait_send)


def to_tokens(place, rows, landed, send, recv):
    tok = landed.shape[1]
    chip = 2 * place.x + place.y
    for cs in range(2):
        for ys in range(2):
            part = pl.ds(2 * tok * cs + tok * ys, tok)
            own = (place.core == place.x) & (place.core == cs) & (place.y == ys)
            copy = remote(
                rows.at[part], landed.at[chip], send.at[2 * cs + ys], recv.at[chip], place.member(place.core, cs, ys)
            )
            pl.when(jnp.logical_not(own))(copy.start)

            @pl.when(own)
            def _(part=part):
                landed[chip] = rows[part]


def to_tokens_wait(place, rows, landed, send, recv):
    for xs in range(2):
        for ys in range(2):
            at = 2 * xs + ys
            own = (place.core == place.x) & (place.x == xs) & (place.y == ys)
            copy = remote(
                landed.at[at], landed.at[at], send.at[at], recv.at[at], place.member(place.x, 1 - place.core, place.y)
            )
            pl.when(jnp.logical_not(own))(copy.wait_recv)


def to_tokens_drain(place, rows, landed, send, recv):
    for cs in range(2):
        for ys in range(2):
            own = (place.core == place.x) & (place.core == cs) & (place.y == ys)
            at = 2 * cs + ys
            copy = remote(
                landed.at[at], landed.at[at], send.at[at], recv.at[at], place.member(place.x, 1 - place.core, place.y)
            )
            pl.when(jnp.logical_not(own))(copy.wait_send)


def spread_rows(small, per, width, rows):
    lane = lax.broadcasted_iota(jnp.int32, (128, width), 1).astype(F32)
    spot = lane - per * jnp.floor((lane + 0.5) * (1.0 / per))
    pick = (spot == lax.broadcasted_iota(jnp.int32, (128, width), 0).astype(F32)).astype(BF16)
    wide = nn(small.astype(BF16), pick).reshape(32, rows, width)
    low = lax.broadcasted_iota(jnp.int32, wide.shape, 0) * per
    column = lax.broadcasted_iota(jnp.int32, wide.shape, 2)
    return jnp.sum(jnp.where((column >= low) & (column < low + per), wide, 0.0), axis=0)


AG_PLAN = dict(out=(4, 3, 0, 2, 1), ff1=(4, 3, 0, 2, 1), ff2=(4, 3, 2, 0, 1))
AG_HEADS = (2, 0, 4, 3, 1)
RS_PLAN = dict(out=(1, 2, 0, 3, 4), ff1=(1, 2, 0, 3, 4), ff2=(1, 0, 2, 3, 4))
RS_HEADS = (1, 3, 4, 2, 0)
REST = ("ff2", "ff1", "out")


def matrices(dim, ff):
    return (("out", 0, dim), ("ff1", dim, ff))


def plane(place, dx, dy):
    tx, ty = rem(place.x + dx, 2), rem(place.y + dy, 2)
    return 2 * tx + ty, place.member(tx, place.core, ty)


def enter_kernel(
    repeat, groups,
    shard_qkv, shard2, shard_ff2, small, tokens,
    all2_out, ff2_out, params_out, ffb_out, q_out, kv_out, rows_out, heads_out,
    stage, all2, all_ff2, q_rows, window, rows, pack_w, blocks, heads,
    y_sems, gather_send, gather_recv, block_send, block_recv, plane_send, plane_recv,
    row_send, row_recv, near_send, near_recv, side_send, side_recv, local,
):
    place = Place(repeat, groups)
    dim = all2.shape[0]
    ff = all_ff2.shape[0]
    tok = tokens.shape[0]
    unit_rows = dim // 32
    slab = 2 * unit_rows
    half = 4 * tok
    own_ff2 = pltpu.make_async_copy(
        shard_ff2, all_ff2.at[rows_at(place.unit * (ff // 32), ff // 32)], local.at[0]
    )
    own_ff2.start()
    wide = shard_qkv[...].astype(F32)
    for chip in range(CHIPS):
        cut = [wide[:, part * dim + HW * chip:part * dim + HW * (chip + 1)] for part in range(3)]
        block = jnp.concatenate([cut[0], jnp.zeros((unit_rows, QW - HW), F32), cut[1], cut[2]], axis=1)
        pack_w[chip] = jnp.concatenate([block, small[...].astype(F32)], axis=0).astype(BF16)
    role = 2 * place.x + place.y
    blocks[place.unit] = pack_w[role]
    place.greet()
    plane_copies = []
    if repeat == 1:
        for dx, dy in ((1, 1), (1, 0), (0, 1)):
            chip, device = plane(place, dx, dy)
            at = 2 * dx + dy
            copy = remote(pack_w.at[chip], blocks.at[place.unit], plane_send.at[at], plane_recv.at[at], device)
            copy.start()
            plane_copies.append(copy)
    to_heads(place, None, rows, row_send, row_recv, tokens)
    cuts = matrices(dim, ff)
    y_copies = []

    def half_columns(at, which):
        name, first, width = cuts[at]
        return (slice(None), rows_at(first + which * (width // 2), width // 2, 128))

    for at in range(2):
        mine, other = half_columns(at, place.bit(0)), half_columns(at, 1 - place.bit(0))
        out = remote(shard2.at[other], stage.at[other], y_sems.at[at], y_sems.at[2 + at], place.partner(0))
        back = remote(shard2.at[mine], stage.at[mine], y_sems.at[at], y_sems.at[2 + at], place.partner(0))
        out.start()
        y_copies.append((out, back))

    by_heads = GatherBlocks(place, blocks, AG_HEADS)
    gathers = {name: Gather(place, all2, slab, first, width, AG_PLAN[name], True) for name, first, width in cuts}
    gathers["ff2"] = Gather(place, all_ff2, ff // 16, 0, dim, AG_PLAN["ff2"], False)
    here = rows_at(div(place.unit, 2) * slab, slab)

    def merge(at):
        y_copies[at][1].wait_recv()
        name, first, width = cuts[at]
        low = place.bit(0) == 0
        for column in range(0, width // 2, 256):
            size = min(256, width // 2 - column)
            part = rows_at(first + place.bit(0) * (width // 2) + column, size, 128)
            mine, other = shard2[:unit_rows, part].astype(F32), stage[:unit_rows, part].astype(F32)
            whole = jnp.concatenate([jnp.where(low, mine, other), jnp.where(low, other, mine)], axis=0)
            all2[here, part] = whole.astype(BF16)
        gathers[name].begin(gather_send.at[at], gather_recv.at[at])

    by_heads.send, by_heads.recv = block_send, block_recv
    if repeat == 1:
        for copy in plane_copies:
            copy.wait_recv()
        by_heads.release(2)
    else:
        by_heads.feed(0, 0)
        by_heads.step(0)
        by_heads.step(1)
    own_ff2.wait()
    by_heads.step(2)
    gathers["ff2"].begin(gather_send.at[2], gather_recv.at[2])
    merge(1)
    merge(0)
    by_heads.step(3)
    for name in REST:
        gathers[name].step(0)
    by_heads.step(4)

    def compact(pair, carry):
        whole = jnp.concatenate(
            [blocks[2 * pair][:unit_rows].astype(F32), blocks[2 * pair + 1][:unit_rows].astype(F32)], axis=0
        )
        heads[rows_at(pair * slab, slab)] = whole.astype(BF16)
        return carry

    lax.fori_loop(0, 16, compact, 0)
    params_out[...] = spread_rows(blocks[:, unit_rows:, 0:128].astype(F32).reshape(-1, 128), unit_rows, dim, 8)
    bias = jnp.zeros((2, PW), F32)
    for chip in range(CHIPS):
        cut = params_out[4:6, HW * chip:HW * (chip + 1)]
        query = jnp.concatenate([cut[0:1], jnp.zeros((1, PW - HW), F32)], axis=1)
        value = jnp.concatenate([jnp.zeros((1, PW - HW), F32), cut[1:2]], axis=1)
        bias = jnp.where(role == chip, query + value, bias)
    sibling = place.member(place.x, 1 - place.core, place.y)

    def stretch(slot, core):
        return window.at[slot].at[rows_at(half * core, half)]

    def part_of(slot, at):
        return window.at[slot].at[rows_at(half * place.core + tok * at, tok)]

    def side(to, at):
        return remote(
            part_of(1, at), part_of(2 * to, at), side_send.at[to, at], side_recv.at[to, at], place.beside(1 - 2 * to)
        )

    def near(at):
        ref = stretch(1, place.core) if at == 0 else stretch(2 - 2 * place.core, place.core)
        return remote(ref, ref, near_send.at[at], near_recv.at[at], sibling)

    for ys in (place.y, 1 - place.y):
        for cs in range(2):
            to_heads_wait_one(place, rows, row_send, row_recv, cs, ys)
            at = 2 * cs + ys
            part = rows_at(at * tok, tok)
            made = nn(rows[part, :], heads[...]) + bias[0:1]
            window[1, rows_at(half * place.core + at * tok, tok)] = made[:, QW:].astype(BF16)
            side(0, at).start()
            side(1, at).start()
            q_rows[part, :] = made[:, :QW].astype(BF16)
    near(0).start()
    hidden = blocks[:, unit_rows:, 128:256].astype(F32).reshape(-1, 128)
    ffb_out[...] = spread_rows(hidden, ff // 32, ff, 8)
    for name in REST:
        gathers[name].step(1)
    first_copies = [
        pltpu.make_async_copy(q_rows, q_out, local.at[2]),
        pltpu.make_async_copy(rows, rows_out, local.at[3]),
        pltpu.make_async_copy(heads, heads_out, local.at[4]),
    ]
    for copy in first_copies:
        copy.start()
    for phase in range(2, 5):
        for name in REST:
            gathers[name].step(phase)
    for gather in gathers.values():
        gather.finish()
    copies = [
        pltpu.make_async_copy(all2, all2_out, local.at[0]),
        pltpu.make_async_copy(all_ff2, ff2_out, local.at[1]),
    ]
    for copy in copies:
        copy.start()
    for at in range(4):
        side(0, at).wait_recv()
        side(1, at).wait_recv()
    near(1).start()
    near(0).wait_recv()
    near(1).wait_recv()
    last = pltpu.make_async_copy(window, kv_out, local.at[5])
    last.start()
    for at in range(2):
        y_copies[at][0].wait_send()
        near(at).wait_send()
        for part in range(4):
            side(at, part).wait_send()
    for copy in plane_copies:
        copy.wait_send()
    for phase in range(2 if repeat == 1 else 0, 5):
        for mask in range(1 << phase):
            by_heads.copy(phase, mask, by_heads.own).wait_send()
    to_heads_drain(place, rows, row_send, row_recv)
    for copy in first_copies + copies + [last]:
        copy.wait()


VM = pl.BlockSpec(memory_space=pltpu.VMEM)
HBM = pl.BlockSpec(memory_space=pl.ANY)
SM = pl.BlockSpec(memory_space=pltpu.SMEM)
DMA = pltpu.SemaphoreType.DMA


def enter(repeat, groups, shard_qkv, shard2, shard_ff2, small, tokens):
    tok, dim = tokens.shape
    joined = shard2.shape[1]
    ff = shard_ff2.shape[0] * 32
    shape = jax.ShapeDtypeStruct
    vm = pltpu.VMEM
    return pl.pallas_call(
        functools.partial(enter_kernel, repeat, groups),
        out_shape=(
            shape((dim, joined), BF16), shape((ff, dim), BF16), shape((8, dim), F32), shape((8, ff), F32),
            shape((4 * tok, QW), BF16), shape((3, 8 * tok, KW), BF16), shape((4 * tok, dim), BF16),
            shape((dim, PW), BF16),
        ),
        in_specs=[VM] * 5,
        out_specs=(HBM, HBM, VM, VM, HBM, HBM, HBM, HBM),
        scratch_shapes=[
            vm(shard2.shape, BF16), vm((dim, joined), BF16), vm((ff, dim), BF16),
            vm((4 * tok, QW), BF16), vm((3, 8 * tok, KW), BF16), vm((4 * tok, dim), BF16),
            vm((CHIPS, shard2.shape[0], PW), BF16), vm((32, shard2.shape[0], PW), BF16), vm((dim, PW), BF16),
            DMA((4,)), DMA((3, 31)), DMA((3, 31)), DMA((31,)), DMA((31,)), DMA((4,)), DMA((4,)),
            DMA((4,)), DMA((4,)), DMA((2,)), DMA((2,)), DMA((2, 4)), DMA((2, 4)), DMA((6,)),
        ],
        compiler_params=pltpu.CompilerParams(
            collective_id=1, has_side_effects=True, vmem_limit_bytes=VMEM_BYTES
        ),
    )(shard_qkv, shard2, shard_ff2, small, tokens)


def pack_small(norm_gains, norm_biases, proj_biases, ff_bias):
    rows = jnp.concatenate([norm_gains, norm_biases, proj_biases], axis=0)
    rows = jnp.pad(rows, ((0, 0), (0, 128 - rows.shape[1])))
    hidden = jnp.pad(ff_bias[None], ((0, 7), (0, PW - 128 - ff_bias.shape[0])))
    return jnp.concatenate([rows, hidden], axis=1)


QT = 512
KT = 512


def lane_mask(shape, low, high, axis):
    lane = lax.broadcasted_iota(jnp.int32, shape, axis)
    return (lane >= low) & (lane < high)


HEAD_QUERY = ((0, 0), (0, 64), (128, 0))
HEAD_VALUE = ((128, 64), (256, 0), (256, 64))
HEAD_CONTEXT = ((0, 64), (128, 0), (128, 64))


def head_rows(ref, rows, spot):
    tile, place = spot
    part = ref[rows, tile:tile + 128]
    return jnp.where(lane_mask(part.shape, place, place + HD, 1), part, jnp.zeros_like(part))


def doc_spans(starts, spans, total_rows):
    half = spans.shape[1]
    blk = lax.axis_index("blk")
    origin = (div(blk, GROUP) - 1) * 2 * half
    first = origin + (2 + rem(blk, 2)) * half
    far = jnp.int32(1 << 30)
    shape = (half // 128, 128)
    places = first + 128 * lax.broadcasted_iota(jnp.int32, shape, 0) + lax.broadcasted_iota(jnp.int32, shape, 1)
    edges = range(0, half, QT)

    def one(at, state):
        low, high, last, lows, highs = state
        start = starts[at]
        live = start < total_rows
        below = jnp.where(live, start, -far)
        above = jnp.where(live, start, far)
        low = jnp.where(below <= places, jnp.maximum(low, below), low)
        high = jnp.where(above > places, jnp.minimum(high, above), high)
        lows = tuple(jnp.where(below <= first + edge, jnp.maximum(old, below), old) for edge, old in zip(edges, lows))
        highs = tuple(
            jnp.where(above > first + edge + QT - 1, jnp.minimum(old, above), old) for edge, old in zip(edges, highs)
        )
        return low, high, jnp.maximum(last, below), lows, highs

    low, high, last, lows, highs = lax.fori_loop(
        0, starts.shape[0], one,
        (
            jnp.full(shape, -far), jnp.full(shape, far), -far,
            tuple(-far for _ in edges), tuple(far for _ in edges),
        ),
    )
    start, end = last - total_rows, starts[0] + total_rows
    low = jnp.where(low == -far, start, low) - origin
    high = jnp.where(high == far, end, high) - origin
    for at in range(shape[0]):
        spans[0:1, at * 128:(at + 1) * 128] = low[at:at + 1]
        spans[1:2, at * 128:(at + 1) * 128] = high[at:at + 1]
    tiles = []
    for old_low, old_high in zip(lows, highs):
        begin = jnp.where(old_low == -far, start, old_low) - origin
        finish = jnp.where(old_high == far, end, old_high) - origin
        tiles.append((div(begin, KT), div(finish + (KT - 1), KT)))
    return tiles


def meets(spans, columns, j):
    key = j * KT + lax.broadcasted_iota(jnp.int32, (KT, QT), 0)
    inside = (key >= spans[0:1, columns]) & (key < spans[1:2, columns])
    return jnp.where(inside, 0.0, NEGATIVE)


def forward_kernel(total_rows, starts, queries, window, context_out, sums_out, spans):
    count = queries.shape[0]
    scale = HD ** (-0.5)
    tiles = doc_spans(starts, spans, total_rows)

    for at, (begin, finish) in enumerate(tiles):
        rows = slice(at * QT, (at + 1) * QT)
        columns = rows
        scaled = [head_rows(queries, rows, HEAD_QUERY[head]) * jnp.asarray(scale, BF16) for head in range(3)]

        def visit(j, state, columns=columns, scaled=scaled):
            keys = rows_at(j * KT, KT)
            bias = meets(spans, columns, j)
            tops, terms, fresh = [], [], []
            scores = [
                nt(window[keys, tile_at:tile_at + 128], scaled[head]) + bias
                for head, (tile_at, place) in enumerate(HEAD_QUERY)
            ]
            for head in range(3):
                tops.append(jnp.maximum(state[3 * head], jnp.max(scores[head], axis=0, keepdims=True)))
            for head in range(3):
                terms.append(jnp.exp(scores[head] - tops[head]))
            for head in range(3):
                highest, total, weighted = state[3 * head:3 * head + 3]
                tile_at = HEAD_VALUE[head][0]
                factor = jnp.exp(highest - tops[head])
                total = total * factor + jnp.sum(terms[head], axis=0, keepdims=True)
                weighted = weighted * factor + tn(window[keys, tile_at:tile_at + 128], terms[head].astype(BF16))
                fresh += [tops[head], total, weighted]
            return tuple(fresh)

        start = []
        for head in range(3):
            start += [jnp.full((1, QT), NEGATIVE, F32), jnp.zeros((1, QT), F32), jnp.zeros((128, QT), F32)]
        state = lax.fori_loop(begin, finish, visit, tuple(start))
        made = []
        for head in range(3):
            highest, total, weighted = state[3 * head:3 * head + 3]
            whole = weighted / total
            place = HEAD_CONTEXT[head][1]
            made.append(jnp.where(lane_mask(whole.shape, place, place + HD, 0), whole, 0.0))
            sums_out[head:head + 1, columns] = highest + jnp.log(total)
        context_out[rows, 0:128] = made[0].T
        context_out[rows, 128:256] = (made[1] + made[2]).T


def forward(total_rows, starts, queries, window):
    count = queries.shape[0]
    shape = jax.ShapeDtypeStruct
    return pl.pallas_call(
        functools.partial(forward_kernel, total_rows),
        out_shape=(shape((count, QW), F32), shape((8, count), F32)),
        in_specs=[SM] + [VM] * 2,
        out_specs=(VM, VM),
        scratch_shapes=[pltpu.VMEM((8, count), jnp.int32)],
        compiler_params=pltpu.CompilerParams(vmem_limit_bytes=VMEM_BYTES),
    )(starts, queries, window)


def backward_kernel(total_rows, starts, queries, window, context, grads, sums, query_out, window_out, acc, spans):
    count = queries.shape[0]
    scale = HD ** (-0.5)
    acc[...] = jnp.zeros_like(acc)
    tiles = doc_spans(starts, spans, total_rows)

    for at, (begin, finish) in enumerate(tiles):
        rows = slice(at * QT, (at + 1) * QT)
        columns = rows
        scaled, grad, delta, sum_rows = [], [], [], []
        for head in range(3):
            scaled.append(head_rows(queries, rows, HEAD_QUERY[head]) * jnp.asarray(scale, BF16))
            mine = head_rows(grads, rows, HEAD_CONTEXT[head])
            tile_at = HEAD_CONTEXT[head][0]
            product = mine.astype(F32) * context[rows, tile_at:tile_at + 128]
            grad.append(mine)
            delta.append(
                lax.dot_general(
                    jnp.ones((8, 128), F32), product, (((1,), (1,)), ((), ())),
                    precision=lax.Precision.HIGHEST, preferred_element_type=F32,
                )[0:1]
            )
            sum_rows.append(sums[head:head + 1, columns])

        def visit(j, state, columns=columns, scaled=scaled, grad=grad, delta=delta, sum_rows=sum_rows):
            keys = rows_at(j * KT, KT)
            bias = meets(spans, columns, j)
            fresh, key_grads, value_grads = [], [], []
            for head in range(3):
                key = window[keys, HEAD_QUERY[head][0]:HEAD_QUERY[head][0] + 128]
                value = window[keys, HEAD_VALUE[head][0]:HEAD_VALUE[head][0] + 128]
                probs = jnp.exp((nt(key, scaled[head]) + bias) - sum_rows[head])
                spread = nt(value, grad[head])
                steps = (probs * (spread - delta[head])).astype(BF16)
                value_grads.append(nn(probs.astype(BF16), grad[head]))
                key_grads.append(nn(steps, scaled[head]))
                fresh.append(state[head] + tn(key, steps))
            acc[keys, 0:128] += key_grads[0] + key_grads[1]
            acc[keys, 128:256] += key_grads[2] + value_grads[0]
            acc[keys, 256:384] += value_grads[1] + value_grads[2]
            return tuple(fresh)

        state = lax.fori_loop(
            begin, finish, visit, tuple(jnp.zeros((128, QT), F32) for _ in range(3))
        )
        made = []
        for head in range(3):
            place = HEAD_QUERY[head][1]
            made.append(jnp.where(lane_mask(state[head].shape, place, place + HD, 0), state[head] * scale, 0.0))
        query_out[rows, 0:128] = (made[0] + made[1]).T.astype(BF16)
        query_out[rows, 128:256] = made[2].T.astype(BF16)

    def store(at, carry):
        rows = rows_at(at * KT, KT)
        window_out[rows, :] = acc[rows, :].astype(BF16)
        return carry

    lax.fori_loop(0, acc.shape[0] // KT, store, 0)


def backward(total_rows, starts, queries, window, context, grads, sums):
    shape = jax.ShapeDtypeStruct
    return pl.pallas_call(
        functools.partial(backward_kernel, total_rows),
        out_shape=(shape(queries.shape, BF16), shape(window.shape, BF16)),
        in_specs=[SM] + [VM] * 5,
        out_specs=(VM, VM),
        scratch_shapes=[pltpu.VMEM(window.shape, F32), pltpu.VMEM((8, queries.shape[0]), jnp.int32)],
        compiler_params=pltpu.CompilerParams(vmem_limit_bytes=VMEM_BYTES),
    )(starts, queries, window, context, grads, sums)


def norm_forward(values):
    center = values - jnp.mean(values, axis=-1, keepdims=True)
    scale = lax.rsqrt(jnp.mean(center * center, axis=-1, keepdims=True) + EPSILON)
    return center * scale, scale


def norm_backward(grad, unit_rows, scale, gain):
    inner = grad * gain
    gain_row = jnp.sum(grad * unit_rows, axis=0, keepdims=True)
    shift_row = jnp.sum(grad, axis=0, keepdims=True)
    back = scale * (
        inner
        - jnp.mean(inner, axis=-1, keepdims=True)
        - unit_rows * jnp.mean(inner * unit_rows, axis=-1, keepdims=True)
    )
    return back, gain_row, shift_row


def column_sum(values):
    return jnp.sum(values.astype(F32), axis=0, keepdims=True)


def middle_kernel(
    repeat, groups,
    context, tokens, d_out, params, ffb, all2, all_ff2,
    out, d_mid_out, grads_out, grad_o3, grad_ff2, sum_rows,
    w_out, w_ff1, w_ff2, ctx_rows, parts, pack, grad_rows, act, slope, d_pre,
    send, recv, back_send, back_recv, local,
):
    place = Place(repeat, groups)
    tok, dim = tokens.shape
    ff = w_ff1.shape[1]
    loads = [
        pltpu.make_async_copy(all2.at[:, pl.ds(0, dim)], w_out, local.at[0]),
        pltpu.make_async_copy(all2.at[:, pl.ds(dim, ff)], w_ff1, local.at[1]),
        pltpu.make_async_copy(all_ff2, w_ff2, local.at[2]),
    ]
    for load in loads:
        load.start()
    ctx_rows[...] = context[...].astype(BF16)
    place.greet(cube=False, beside=False)
    to_tokens(place, ctx_rows, parts, send, recv)
    to_tokens_wait(place, ctx_rows, parts, send, recv)
    joined = jnp.concatenate([parts[chip][:, QW - HW:].astype(F32) for chip in range(CHIPS)], axis=1).astype(BF16)
    loads[0].wait()
    gains, shifts = [params[at:at + 1, :] for at in (0, 1)], [params[at:at + 1, :] for at in (2, 3)]
    mid = tokens[...].astype(F32) + (nn(joined, w_out[...]) + params[6:7, :])
    unit_first, scale_first = norm_forward(mid)
    hidden = unit_first * gains[0] + shifts[0]
    low = hidden.astype(BF16)
    loads[1].wait()
    loads[2].wait()
    ff_out = jnp.zeros((tok, dim), F32)
    for first in range(0, ff, dim):
        cut = slice(first, first + dim)
        pre = nn(low, w_ff1[:, cut]) + ffb[0:1, cut]
        bell = 0.5 * (1.0 + lax.erf(pre * 0.7071067811865476))
        made = (pre * bell).astype(BF16)
        act[:, cut] = made
        slope[:, cut] = bell + pre * jnp.exp(-0.5 * pre * pre) * 0.3989422804014327
        ff_out = ff_out + nn(made, w_ff2[cut, :])
    unit_second, scale_second = norm_forward(hidden + (ff_out + params[7:8, :]))
    out[...] = (unit_second * gains[1] + shifts[1]).astype(BF16)
    d_sum, gain_second, shift_second = norm_backward(d_out[...].astype(F32), unit_second, scale_second, gains[1])
    d_ff = d_sum.astype(BF16)
    d_hidden = d_sum
    for first in range(0, ff, dim):
        cut = slice(first, first + dim)
        made = (nt(d_ff, w_ff2[cut, :]) * slope[:, cut]).astype(BF16)
        d_pre[:, cut] = made
        d_hidden = d_hidden + nt(made, w_ff1[:, cut])
    d_mid, gain_first, shift_first = norm_backward(d_hidden, unit_first, scale_first, gains[0])
    d_mid_out[...] = d_mid
    d_attn = d_mid.astype(BF16)
    d_context = nt(d_attn, w_out[...])
    for chip in range(CHIPS):
        pack[chip] = jnp.concatenate(
            [jnp.zeros((tok, QW - HW), F32), d_context[:, HW * chip:HW * (chip + 1)]], axis=1
        ).astype(BF16)
    to_heads(place, pack, grad_rows, back_send, back_recv)
    for first in range(0, ff, dim):
        cut = slice(first, first + dim)
        grad_ff2[cut, :] = tn(act[:, cut], d_ff).astype(BF16)
        grad_o3[:, dim + first:2 * dim + first] = tn(low, d_pre[:, cut]).astype(BF16)
        sum_rows[8 + first // dim:9 + first // dim, :] = column_sum(d_pre[:, cut])
    grad_o3[:, 0:dim] = tn(joined, d_attn).astype(BF16)
    for at, row in enumerate(
        (
            gain_first, gain_second, shift_first, shift_second,
            jnp.zeros((1, dim), F32), jnp.zeros((1, dim), F32), column_sum(d_attn), column_sum(d_ff),
        )
    ):
        sum_rows[at:at + 1, :] = row
    sum_rows[8 + ff // dim:, :] = jnp.zeros((8 - ff // dim, dim), F32)
    to_heads_wait(place, grad_rows, back_send, back_recv)
    grads_out[...] = grad_rows[...]
    to_tokens_drain(place, ctx_rows, parts, send, recv)
    to_heads_drain(place, grad_rows, back_send, back_recv)


def middle(repeat, groups, context, tokens, d_out, params, ffb, all2, all_ff2):
    tok, dim = tokens.shape
    ff = all_ff2.shape[0]
    shape = jax.ShapeDtypeStruct
    vm = pltpu.VMEM
    return pl.pallas_call(
        functools.partial(middle_kernel, repeat, groups),
        out_shape=(
            shape((tok, dim), BF16), shape((tok, dim), F32), shape((4 * tok, QW), BF16),
            shape((dim, dim + ff), BF16), shape((ff, dim), BF16), shape((16, dim), F32),
        ),
        in_specs=[VM] * 5 + [HBM] * 2,
        out_specs=(VM,) * 6,
        scratch_shapes=[
            vm((dim, dim), BF16), vm((dim, ff), BF16), vm((ff, dim), BF16), vm((4 * tok, QW), BF16),
            vm((CHIPS, tok, QW), BF16), vm((CHIPS, tok, QW), BF16), vm((4 * tok, QW), BF16),
            vm((tok, ff), BF16), vm((tok, ff), F32), vm((tok, ff), BF16),
            DMA((4,)), DMA((4,)), DMA((4,)), DMA((4,)), DMA((4,)),
        ],
        compiler_params=pltpu.CompilerParams(collective_id=2, has_side_effects=True, vmem_limit_bytes=VMEM_BYTES),
    )(context, tokens, d_out, params, ffb, all2, all_ff2)


def leave_kernel(
    repeat, groups,
    d_query, d_window, rows, heads, d_mid, sum_rows, grad_o2, grad_ff2_in,
    d_tokens, g_qkv, g_out, g_ff1, g_ff2, g_rows,
    grad2, grad_ff2, land_out, land_ff1, land_ff2, blocks, land_blocks, role_land,
    near_land, side_land, joint, joined, partial, parts, swap_out, swap_in, rows_mine, rows_land,
    grad_send, grad_recv, block_send, block_recv, plane_send, plane_recv, near_send, near_recv, side_send, side_recv,
    part_send, part_recv, swap_send, swap_recv, rows_send, rows_recv, local,
):
    place = Place(repeat, groups)
    tok, dim = d_mid.shape
    ff = grad_ff2.shape[0]
    unit_rows = dim // 32
    half = 4 * tok
    role = 2 * place.x + place.y
    loads = [
        pltpu.make_async_copy(grad_o2, grad2, local.at[0]),
        pltpu.make_async_copy(grad_ff2_in, grad_ff2, local.at[1]),
    ]
    for load in loads:
        load.start()
    place.greet()
    sibling = place.member(place.x, 1 - place.core, place.y)

    def stretch(slot, core):
        return d_window.at[slot].at[rows_at(half * core, half)]

    def near(at):
        ref = stretch(2 * place.core, 1 - place.core) if at == 0 else stretch(1, 1 - place.core)
        return remote(ref, near_land.at[at], near_send.at[at], near_recv.at[at], sibling)

    solo = remote(
        stretch(2 * place.core, place.core), side_land.at[place.core], side_send.at[place.core],
        side_recv.at[place.core], place.beside(2 * place.core - 1),
    )
    shared = remote(
        joint, side_land.at[1 - place.core], side_send.at[1 - place.core], side_recv.at[1 - place.core],
        place.beside(1 - 2 * place.core),
    )
    near(0).start()
    solo.start()
    near(1).start()
    cuts = matrices(dim, ff)
    scatters = {
        name: Scatter(place, grad2, 2 * unit_rows, first, width, RS_PLAN[name], True) for name, first, width in cuts
    }
    scatters["ff2"] = Scatter(place, grad_ff2, ff // 16, 0, dim, RS_PLAN["ff2"], False)
    loads[0].wait()
    loads[1].wait()
    near(0).wait_recv()
    joint[...] = (
        d_window[2 - 2 * place.core, rows_at(half * place.core, half)].astype(F32) + near_land[0].astype(F32)
    ).astype(BF16)
    shared.start()
    scatters["ff2"].begin(land_ff2, grad_send.at[2], grad_recv.at[2])
    scatters["ff1"].begin(land_ff1, grad_send.at[1], grad_recv.at[1])
    scatters["out"].begin(land_out, grad_send.at[0], grad_recv.at[0])
    for phase in range(SPLIT):
        for name in REST:
            scatters[name].step(phase)
    near(1).wait_recv()
    own = d_window[1, rows_at(half * place.core, half)].astype(F32) + near_land[1].astype(F32)
    for at in range(2):
        remote(joint, side_land.at[at], side_send.at[at], side_recv.at[at], sibling).wait_recv()
    joined[:, QW:] = (own + side_land[0].astype(F32) + side_land[1].astype(F32)).astype(BF16)
    joined[:, :QW] = d_query[...]
    for at in range(4):
        part = slice(at * tok, (at + 1) * tok)
        partial[part, :] = nt(joined[part, :], heads[...]).astype(BF16)
    to_tokens(place, partial, parts, part_send, part_recv)
    whole = tn(rows[...], joined[...])
    for unit in range(32):
        block = whole[unit * unit_rows:(unit + 1) * unit_rows]
        pad = jnp.zeros((blocks.shape[1] - unit_rows, PW), F32)
        blocks[unit] = jnp.concatenate([block, pad], axis=0).astype(BF16)
    until = 3 if repeat == 1 else 5
    by_heads = ScatterBlocks(place, blocks, RS_HEADS, until)
    by_heads.begin(land_blocks, block_send, block_recv)
    sums = column_sum(joined[...])
    rows_mine[0] = sum_rows[...]
    for row, first in ((4, 0), (5, PW - HW)):
        line = [jnp.where(role == chip, sums[:, first:first + HW], 0.0) for chip in range(CHIPS)]
        rows_mine[0, row:row + 1, :] = jnp.concatenate(line, axis=1)

    def rows_copy(phase):
        return remote(
            rows_mine.at[phase], rows_land.at[phase], rows_send.at[phase], rows_recv.at[phase],
            place.partner(RS_HEADS[phase]),
        )

    def rows_add(phase):
        rows_copy(phase).wait_recv()
        rows_mine[phase + 1] = rows_mine[phase] + rows_land[phase]
        if phase < 4:
            rows_copy(phase + 1).start()

    rows_copy(0).start()
    by_heads.step(0)
    rows_add(0)
    by_heads.step(1)
    rows_add(1)
    for phase in range(SPLIT, 4):
        for name in REST:
            scatters[name].step(phase)
    by_heads.step(2)
    rows_add(2)

    def role_copy(dx, dy):
        chip, device = plane(place, dx, dy)
        at = 2 * dx + dy
        there = place.unit + dx * 4 * (1 - 2 * place.bit(2)) + dy * (1 - 2 * place.bit(0))
        return remote(blocks.at[there], role_land.at[role], plane_send.at[at], plane_recv.at[at], device)

    if repeat == 1:
        for dx, dy in ((1, 1), (1, 0), (0, 1)):
            role_copy(dx, dy).start()
    else:
        by_heads.step(3)
        by_heads.last()
        role_land[...] = jnp.zeros_like(role_land)
    role_land[role] = blocks[place.unit]
    rows_add(3)

    def swap(at):
        name, first, width = cuts[at]
        part = (slice(None), pl.ds(first // 2, width // 2))
        return remote(swap_out.at[part], swap_in.at[part], swap_send.at[at], swap_recv.at[at], place.partner(0))

    def finish_half(at):
        name, first, width = cuts[at]
        target = (g_out, g_ff1)[at]
        total = scatters[name].last()
        high = place.bit(0) == 1
        keep = jnp.where(high, total[unit_rows:], total[:unit_rows])
        give = jnp.where(high, total[:unit_rows], total[unit_rows:])
        pad = jnp.zeros((swap_out.shape[0] - unit_rows, give.shape[1]), F32)
        swap_out[:, first // 2:(first + width) // 2] = jnp.concatenate([give, pad], axis=0).astype(BF16)
        swap(at).start()
        target[:, rows_at(place.bit(0) * (width // 2), width // 2, 128)] = keep

    def finish_swap(at):
        name, first, width = cuts[at]
        target = (g_out, g_ff1)[at]
        swap(at).wait_recv()
        other = swap_in[:, first // 2:(first + width) // 2].astype(F32)[:unit_rows]
        target[:, rows_at((1 - place.bit(0)) * (width // 2), width // 2, 128)] = other

    for at in (1, 0):
        finish_half(at)
    g_ff2[...] = scatters["ff2"].last()
    rows_add(4)
    g_rows[...] = rows_mine[5]
    to_tokens_wait(place, partial, parts, part_send, part_recv)
    d_tokens[...] = (
        d_mid[...] + (parts[0].astype(F32) + parts[1].astype(F32)) + (parts[2].astype(F32) + parts[3].astype(F32))
    ).astype(BF16)
    for at in (1, 0):
        finish_swap(at)
    if repeat == 1:
        for dx, dy in ((1, 1), (1, 0), (0, 1)):
            role_copy(dx, dy).wait_recv()
    for part, first in ((0, 0), (1, QW), (2, QW + HW)):
        line = [role_land[chip][:unit_rows, first:first + HW].astype(F32) for chip in range(CHIPS)]
        g_qkv[:, part * dim:(part + 1) * dim] = jnp.concatenate(line, axis=1)
    for scatter in scatters.values():
        scatter.finish()
    by_heads.finish()
    if repeat == 1:
        for dx, dy in ((1, 1), (1, 0), (0, 1)):
            role_copy(dx, dy).wait_send()
    for at in range(2):
        swap(at).wait_send()
        near(at).wait_send()
    solo.wait_send()
    shared.wait_send()
    for phase in range(5):
        rows_copy(phase).wait_send()
    to_tokens_drain(place, partial, parts, part_send, part_recv)


SPLIT = 2


def leave(repeat, groups, d_query, d_window, rows, heads, d_mid, sum_rows, grad_o2, grad_ff2):
    tok, dim = d_mid.shape
    ff = grad_ff2.shape[0]
    unit = dim // 32
    slab = 2 * unit
    half = 4 * tok
    wide = -(-unit // 16) * 16
    shape = jax.ShapeDtypeStruct
    vm = pltpu.VMEM
    return pl.pallas_call(
        functools.partial(leave_kernel, repeat, groups),
        out_shape=(
            shape((tok, dim), BF16), shape((unit, 3 * dim), F32), shape((unit, dim), F32), shape((unit, ff), F32),
            shape((ff // 32, dim), F32), shape((16, dim), F32),
        ),
        in_specs=[VM] * 6 + [HBM] * 2,
        out_specs=(VM,) * 6,
        scratch_shapes=[
            vm((dim, dim + ff), BF16), vm((ff, dim), BF16),
            vm((31, slab, dim // 2), BF16), vm((31, slab, ff // 2), BF16), vm((31, ff // 32, dim), BF16),
            vm((32, wide, PW), BF16), vm((31, wide, PW), BF16), vm((CHIPS, wide, PW), BF16),
            vm((2, half, KW), BF16), vm((2, half, KW), BF16), vm((half, KW), BF16), vm((half, PW), BF16),
            vm((half, dim), BF16), vm((CHIPS, tok, dim), BF16),
            vm((wide, (dim + ff) // 2), BF16), vm((wide, (dim + ff) // 2), BF16),
            vm((6, 16, dim), F32), vm((5, 16, dim), F32),
            DMA((3, 31)), DMA((3, 31)), DMA((31,)), DMA((31,)), DMA((4,)), DMA((4,)), DMA((2,)), DMA((2,)), DMA((2,)),
            DMA((2,)), DMA((4,)), DMA((4,)), DMA((2,)), DMA((2,)), DMA((5,)), DMA((5,)), DMA((2,)),
        ],
        compiler_params=pltpu.CompilerParams(collective_id=3, has_side_effects=True, vmem_limit_bytes=VMEM_BYTES),
    )(d_query, d_window, rows, heads, d_mid, sum_rows, grad_o2, grad_ff2)


def settle_kernel(
    repeat, out, d_tokens, g_qkv, g_out, g_ff1, g_ff2, g_rows,
    out_r, d_tokens_r, g_qkv_r, g_out_r, g_ff1_r, g_ff2_r, gains_r, shifts_r, biases_r, hidden_r,
):
    for source, target in (
        (out, out_r), (d_tokens, d_tokens_r), (g_qkv, g_qkv_r), (g_out, g_out_r), (g_ff1, g_ff1_r), (g_ff2, g_ff2_r)
    ):
        target[...] = source[...]
    width = g_rows.shape[1]
    per, hidden = gains_r.shape[1], hidden_r.shape[1]
    unit = div(lax.axis_index("blk") * 2 + lax.axis_index("head"), repeat)
    turned = pltpu.roll(g_rows[0:8, :], rem(width - unit * per, width), 1)
    gains_r[...] = turned[0:2, :per]
    shifts_r[...] = turned[2:4, :per]
    biases_r[...] = turned[4:8, :per]
    lines = g_rows[8:16, :]
    row = lax.broadcasted_iota(jnp.int32, lines.shape, 0)
    mine = jnp.sum(jnp.where(row == div(unit * hidden, width), lines, 0.0), axis=0, keepdims=True)
    turned = pltpu.roll(jnp.broadcast_to(mine, lines.shape), rem(width - rem(unit * hidden, width), width), 1)
    hidden_r[...] = turned[0:1, :hidden]


def settle(repeat, results):
    shape = jax.ShapeDtypeStruct
    per, hidden = results[2].shape[0], results[5].shape[0]
    small = [shape((count, per), F32) for count in (2, 2, 4)] + [shape((1, hidden), F32)]
    return pl.pallas_call(
        functools.partial(settle_kernel, repeat),
        out_shape=[shape(value.shape, value.dtype) for value in results[:6]] + small,
        in_specs=[VM] * 7,
        out_specs=[VM] * 10,
        compiler_params=pltpu.CompilerParams(vmem_limit_bytes=VMEM_BYTES),
    )(*results)


def gather_repeat(value, repeat, axis):
    if repeat == 1:
        return value
    count = repeat // 2
    sets = [list(range(at, at + count)) for at in range(0, lax.axis_size("blk"), count)]
    value = lax.all_gather(value, "head", axis=axis, tiled=True)
    if count == 1:
        return value
    return lax.all_gather(value, "blk", axis=axis, tiled=True, axis_index_groups=sets)


def own_share(value, repeat, axis):
    if repeat == 1:
        return value
    count = repeat // 2
    sets = [list(range(at, at + count)) for at in range(0, lax.axis_size("blk"), count)]
    value = lax.psum(value, "head")
    if count > 1:
        value = lax.psum(value, "blk", axis_index_groups=sets)
    size = value.shape[axis] // repeat
    at = jnp.mod(lax.axis_index("blk") * 2 + lax.axis_index("head"), repeat)
    return lax.dynamic_slice_in_dim(value, at * size, size, axis)


def body(tokens, w_qkv, w_out, w_ff1, w_ff2, norm_gains, norm_biases, proj_biases, ff_bias, doc_starts, d_out):
    blks = lax.axis_size("blk")
    repeat = blks * 2 // 32
    groups = blks // GROUP
    tok, dim = tokens.shape
    half_rows = 4 * tok
    total_rows = blks * 2 * tok
    shard_qkv = gather_repeat(w_qkv, repeat, 0)
    shard2 = gather_repeat(jnp.concatenate([w_out, w_ff1], axis=1), repeat, 0)
    shard2 = jnp.pad(shard2, ((0, -shard2.shape[0] % 16), (0, 0)))
    shard_ff2 = gather_repeat(w_ff2, repeat, 0)
    small = pack_small(
        gather_repeat(norm_gains, repeat, 1), gather_repeat(norm_biases, repeat, 1),
        gather_repeat(proj_biases, repeat, 1), gather_repeat(ff_bias, repeat, 0),
    )
    all2, all_ff2, params, ffb, queries, window, rows, heads = enter(
        repeat, groups, shard_qkv, shard2, shard_ff2, small, tokens
    )
    window = window.reshape(6 * half_rows, KW)
    context, sums = forward(total_rows, doc_starts, queries, window)
    out, d_mid, grads, grad_o2, grad_ff2, sum_rows = middle(
        repeat, groups, context, tokens, d_out, params, ffb, all2, all_ff2
    )
    d_query, d_window = backward(total_rows, doc_starts, queries, window, context, grads, sums)
    d_tokens, g_qkv, g_out, g_ff1, g_ff2, g_rows = leave(
        repeat, groups, d_query, d_window.reshape(3, 2 * half_rows, KW), rows, heads, d_mid, sum_rows, grad_o2, grad_ff2
    )
    results = settle(repeat, (out, d_tokens, g_qkv, g_out, g_ff1, g_ff2, g_rows))
    axes = (None, None, 0, 0, 0, 0, 1, 1, 1, 0)
    results = list(results[:9]) + [results[9].reshape(-1)]
    return tuple(
        value if axis is None else own_share(value, repeat, axis) for value, axis in zip(results, axes)
    )


def solution(mesh):
    rows, columns, flat = P(("blk", "head"), None), P(None, ("blk", "head")), P(("blk", "head"))
    return jax.shard_map(
        body,
        mesh=mesh,
        in_specs=(rows,) * 5 + (columns,) * 3 + (flat, P(), rows),
        out_specs=(rows,) * 6 + (columns,) * 3 + (flat,),
        check_vma=False,
    )
```

```python
import functools

import jax
import jax.numpy as jnp
from jax import lax
from jax.experimental import pallas as pl
from jax.experimental.pallas import tpu as pltpu
from jax.sharding import PartitionSpec as P

H = 12
HD = 64
DOC_MOST = 2048
EPSILON = 1e-06
NEGATIVE = -1e30
MESH = pl.DeviceIdType.MESH
F32 = jnp.float32
BF16 = jnp.bfloat16
VMEM_BYTES = 62 * 1024 * 1024
CHIPS = 4
GROUP = 4
QW = 256
KW = 384
HW = (H // CHIPS) * HD
PW = QW + KW


def div(a, b):
    return lax.div(a, jnp.int32(b))


def rem(a, b):
    return lax.rem(a, jnp.int32(b))


def nn(a, b):
    return lax.dot_general(a, b, (((1,), (0,)), ((), ())), preferred_element_type=F32)


def nt(a, b):
    return lax.dot_general(a, b, (((1,), (1,)), ((), ())), preferred_element_type=F32)


def tn(a, b):
    return lax.dot_general(a, b, (((0,), (0,)), ((), ())), preferred_element_type=F32)


def rows_at(start, count, unit=16):
    return pl.ds(pl.multiple_of(start, unit), count)


class Place:
    def __init__(self, repeat, groups):
        self.repeat = repeat
        blk, head = lax.axis_index("blk"), lax.axis_index("head")
        self.index = blk * 2 + head
        self.unit = div(self.index, repeat)
        self.core, self.x, self.y = rem(blk, 2), rem(div(blk, 2), 2), head
        self.group, self.groups = div(blk, GROUP), groups
        self.bits = [rem(div(self.unit, 1 << k), 2) for k in range(5)]
        others = [self.index + (1 - 2 * self.bits[k]) * (repeat << k) for k in range(5)]
        self.partners = [{"blk": div(other, 2), "head": rem(other, 2)} for other in others]

    def bit(self, k):
        return self.bits[k]

    def partner(self, k):
        return self.partners[k]

    def member(self, x, core, y):
        return {"blk": self.group * GROUP + 2 * x + core, "head": y}

    def beside(self, step):
        group = rem(self.group + self.groups + step, self.groups)
        return {"blk": group * GROUP + 2 * self.x + self.core, "head": self.y}

    def greet(self, cube=True, group=True, beside=True):
        barrier = pltpu.get_barrier_semaphore()
        partners = []
        if cube:
            partners += [self.partner(k) for k in range(5)]
        if group:
            partners += [
                self.member(
                    rem(self.x + dx, 2), rem(self.core + dc, 2), rem(self.y + dy, 2)
                )
                for dx in range(2)
                for dc in range(2)
                for dy in range(2)
                if dx + dc + dy
            ]
        if beside:
            partners += [self.beside(1), self.beside(-1)]
        for partner in partners:
            pl.semaphore_signal(barrier, inc=1, device_id=partner, device_id_type=MESH)
        pl.semaphore_wait(barrier, len(partners))


def remote(src, dst, send, recv, device):
    return pltpu.make_async_remote_copy(
        src_ref=src, dst_ref=dst, send_sem=send, recv_sem=recv, device_id=device, device_id_type=MESH
    )


class Pieces:
    def __init__(self, place, ref, rows, first, width, order, by_columns):
        self.place, self.ref, self.rows, self.first, self.width = place, ref, rows, first, width
        self.order, self.by_columns = order, by_columns
        if by_columns is not None:
            self.shape = (rows, width // 2) if by_columns else (rows // 2, width)
        self.deltas = [(1 - 2 * place.bit(k)) * (1 << k) for k in order]
        self.units = {0: place.unit}
        self.own = self.piece(0)

    def unit_of(self, mask):
        if mask not in self.units:
            at = mask.bit_length() - 1
            self.units[mask] = self.unit_of(mask - (1 << at)) + self.deltas[at]
        return self.units[mask]

    def region(self, unit):
        slab, half = div(unit, 2), rem(unit, 2)
        if self.by_columns:
            return (
                rows_at(slab * self.rows, self.rows),
                rows_at(self.first + half * self.shape[1], self.shape[1], 128),
            )
        return (rows_at(unit * self.shape[0], self.shape[0]), pl.ds(self.first, self.width))

    def piece(self, mask):
        return self.ref.at[self.region(self.unit_of(mask))]


class Gather(Pieces):
    def begin(self, send, recv, until=5):
        self.send, self.recv = send, recv
        self.feed(0, 0, until)

    def copy(self, phase, mask, ref):
        at = (1 << phase) - 1 + mask
        return remote(ref, ref, self.send.at[at], self.recv.at[at], self.place.partner(self.order[phase]))

    def feed(self, mask, phase, until=5):
        if phase < until:
            ref = self.piece(mask)
            for later in range(phase, until):
                self.copy(later, mask, ref).start()

    def release(self, phase):
        for mask in range(1 << phase):
            self.feed(mask, phase)

    def step(self, phase, until=5):
        for mask in range(1 << phase):
            self.copy(phase, mask, self.own).wait_recv()
            self.feed(mask + (1 << phase), phase + 1, until)

    def finish(self):
        for phase in range(5):
            for mask in range(1 << phase):
                self.copy(phase, mask, self.own).wait_send()


class Scatter(Pieces):
    def begin(self, landing, send, recv):
        self.landing, self.send, self.recv = landing, send, recv
        for j in range(16):
            self.give(0, j)

    def slot(self, phase, j):
        return 32 - (1 << (5 - phase)) + j

    def copy(self, phase, j, ref):
        at = self.slot(phase, j)
        return remote(
            ref, self.landing.at[at], self.send.at[at], self.recv.at[at], self.place.partner(self.order[phase])
        )

    def give(self, phase, j):
        self.copy(phase, j, self.piece((2 * j + 1) * (1 << phase))).start()

    def absorb(self, phase, j):
        self.copy(phase, j, self.own).wait_recv()
        rows, columns = self.region(self.unit_of(j * (2 << phase)))
        total = self.ref[rows, columns].astype(F32) + self.landing[self.slot(phase, j)].astype(F32)
        self.ref[rows, columns] = total.astype(BF16)
        return total

    def step(self, phase):
        half = 1 << (3 - phase)
        for jj in range(half):
            self.absorb(phase, 2 * jj + 1)
            self.give(phase + 1, jj)
        for jj in range(half):
            self.absorb(phase, 2 * jj)

    def last(self):
        return self.absorb(4, 0)

    def finish(self):
        for phase in range(5):
            for j in range(1 << (4 - phase)):
                self.copy(phase, j, self.own).wait_send()


class GatherBlocks(Gather):
    def __init__(self, place, ref, order):
        self.shape = ref.shape[1:]
        Pieces.__init__(self, place, ref, 0, 0, 0, order, None)

    def piece(self, mask):
        return self.ref.at[self.unit_of(mask)]


class ScatterBlocks(Scatter):
    def __init__(self, place, ref, order, until):
        Pieces.__init__(self, place, ref, 0, 0, 0, order, None)
        self.until = until

    def piece(self, mask):
        return self.ref.at[self.unit_of(mask)]

    def give(self, phase, j):
        if phase < self.until:
            Scatter.give(self, phase, j)

    def absorb(self, phase, j):
        self.copy(phase, j, self.own).wait_recv()
        unit = self.unit_of(j * (2 << phase))
        total = self.ref[unit].astype(F32) + self.landing[self.slot(phase, j)].astype(F32)
        self.ref[unit] = total.astype(BF16)
        return total

    def finish(self):
        for phase in range(self.until):
            for j in range(1 << (4 - phase)):
                self.copy(phase, j, self.own).wait_send()


def to_heads(place, packed, landed, send, recv, part=None):
    tok = packed.shape[1] if part is None else part.shape[0]
    mine = rows_at(2 * tok * place.core + tok * place.y, tok)
    slot = 2 * place.core + place.y
    alone = place.core == place.x
    for dx, dy in ((0, 0), (1, 0), (0, 1), (1, 1)):
        if True:
            tx, ty = rem(place.x + dx, 2), rem(place.y + dy, 2)
            copy = remote(
                packed.at[2 * tx + ty] if part is None else part,
                landed.at[mine],
                send.at[2 * dx + dy],
                recv.at[slot],
                place.member(tx, place.x, ty),
            )
            if dx + dy:
                copy.start()
            else:
                pl.when(jnp.logical_not(alone))(copy.start)

                @pl.when(alone)
                def _(tx=tx, ty=ty):
                    landed[mine] = packed[2 * tx + ty] if part is None else part[...]


def to_heads_wait_one(place, landed, send, recv, cs, ys):
    tok = landed.shape[0] // 4
    part = landed.at[pl.ds(0, tok)]
    copy = remote(part, part, send.at[0], recv.at[2 * cs + ys], place.member(place.x, 1 - place.core, place.y))
    own = (place.core == place.x) & (place.core == cs) & (place.y == ys)
    pl.when(jnp.logical_not(own))(copy.wait_recv)


def to_heads_wait(place, landed, send, recv):
    for cs in range(2):
        for ys in range(2):
            to_heads_wait_one(place, landed, send, recv, cs, ys)


def to_heads_drain(place, landed, send, recv):
    part = landed.at[pl.ds(0, landed.shape[0] // 4)]
    for at in range(4):
        copy = remote(part, part, send.at[at], recv.at[0], place.member(place.x, 1 - place.core, place.y))
        if at:
            copy.wait_send()
        else:
            pl.when(place.core != place.x)(copy.wait_send)


def to_tokens(place, rows, landed, send, recv):
    tok = landed.shape[1]
    chip = 2 * place.x + place.y
    for cs in range(2):
        for ys in range(2):
            part = pl.ds(2 * tok * cs + tok * ys, tok)
            own = (place.core == place.x) & (place.core == cs) & (place.y == ys)
            copy = remote(
                rows.at[part], landed.at[chip], send.at[2 * cs + ys], recv.at[chip], place.member(place.core, cs, ys)
            )
            pl.when(jnp.logical_not(own))(copy.start)

            @pl.when(own)
            def _(part=part):
                landed[chip] = rows[part]


def to_tokens_wait(place, rows, landed, send, recv):
    for xs in range(2):
        for ys in range(2):
            at = 2 * xs + ys
            own = (place.core == place.x) & (place.x == xs) & (place.y == ys)
            copy = remote(
                landed.at[at], landed.at[at], send.at[at], recv.at[at], place.member(place.x, 1 - place.core, place.y)
            )
            pl.when(jnp.logical_not(own))(copy.wait_recv)


def to_tokens_drain(place, rows, landed, send, recv):
    for cs in range(2):
        for ys in range(2):
            own = (place.core == place.x) & (place.core == cs) & (place.y == ys)
            at = 2 * cs + ys
            copy = remote(
                landed.at[at], landed.at[at], send.at[at], recv.at[at], place.member(place.x, 1 - place.core, place.y)
            )
            pl.when(jnp.logical_not(own))(copy.wait_send)


def spread_rows(small, per, width, rows):
    lane = lax.broadcasted_iota(jnp.int32, (128, width), 1).astype(F32)
    spot = lane - per * jnp.floor((lane + 0.5) * (1.0 / per))
    pick = (spot == lax.broadcasted_iota(jnp.int32, (128, width), 0).astype(F32)).astype(BF16)
    wide = nn(small.astype(BF16), pick).reshape(32, rows, width)
    low = lax.broadcasted_iota(jnp.int32, wide.shape, 0) * per
    column = lax.broadcasted_iota(jnp.int32, wide.shape, 2)
    return jnp.sum(jnp.where((column >= low) & (column < low + per), wide, 0.0), axis=0)


AG_PLAN = dict(out=(4, 3, 0, 2, 1), ff1=(4, 3, 0, 2, 1), ff2=(4, 3, 2, 0, 1))
AG_HEADS = (2, 0, 4, 3, 1)
RS_PLAN = dict(out=(1, 2, 0, 3, 4), ff1=(1, 2, 0, 3, 4), ff2=(1, 0, 2, 3, 4))
RS_HEADS = (1, 3, 4, 2, 0)
REST = ("ff2", "ff1", "out")


def matrices(dim, ff):
    return (("out", 0, dim), ("ff1", dim, ff))


def plane(place, dx, dy):
    tx, ty = rem(place.x + dx, 2), rem(place.y + dy, 2)
    return 2 * tx + ty, place.member(tx, place.core, ty)


def enter_kernel(
    repeat, groups,
    shard_qkv, shard2, shard_ff2, small, tokens,
    all2_out, ff2_out, params_out, ffb_out, q_out, kv_out, rows_out, heads_out,
    stage, all2, all_ff2, q_rows, window, rows, pack_w, blocks, heads,
    y_sems, gather_send, gather_recv, block_send, block_recv, plane_send, plane_recv,
    row_send, row_recv, near_send, near_recv, side_send, side_recv, local,
):
    place = Place(repeat, groups)
    dim = all2.shape[0]
    ff = all_ff2.shape[0]
    tok = tokens.shape[0]
    unit_rows = dim // 32
    slab = 2 * unit_rows
    half = 4 * tok
    own_ff2 = pltpu.make_async_copy(
        shard_ff2, all_ff2.at[rows_at(place.unit * (ff // 32), ff // 32)], local.at[0]
    )
    own_ff2.start()
    wide = shard_qkv[...].astype(F32)
    for chip in range(CHIPS):
        cut = [wide[:, part * dim + HW * chip:part * dim + HW * (chip + 1)] for part in range(3)]
        block = jnp.concatenate([cut[0], jnp.zeros((unit_rows, QW - HW), F32), cut[1], cut[2]], axis=1)
        pack_w[chip] = jnp.concatenate([block, small[...].astype(F32)], axis=0).astype(BF16)
    role = 2 * place.x + place.y
    blocks[place.unit] = pack_w[role]
    place.greet()
    plane_copies = []
    if repeat == 1:
        for dx, dy in ((1, 1), (1, 0), (0, 1)):
            chip, device = plane(place, dx, dy)
            at = 2 * dx + dy
            copy = remote(pack_w.at[chip], blocks.at[place.unit], plane_send.at[at], plane_recv.at[at], device)
            copy.start()
            plane_copies.append(copy)
    to_heads(place, None, rows, row_send, row_recv, tokens)
    cuts = matrices(dim, ff)
    y_copies = []

    def half_columns(at, which):
        name, first, width = cuts[at]
        return (slice(None), rows_at(first + which * (width // 2), width // 2, 128))

    for at in range(2):
        mine, other = half_columns(at, place.bit(0)), half_columns(at, 1 - place.bit(0))
        out = remote(shard2.at[other], stage.at[other], y_sems.at[at], y_sems.at[2 + at], place.partner(0))
        back = remote(shard2.at[mine], stage.at[mine], y_sems.at[at], y_sems.at[2 + at], place.partner(0))
        out.start()
        y_copies.append((out, back))

    by_heads = GatherBlocks(place, blocks, AG_HEADS)
    gathers = {name: Gather(place, all2, slab, first, width, AG_PLAN[name], True) for name, first, width in cuts}
    gathers["ff2"] = Gather(place, all_ff2, ff // 16, 0, dim, AG_PLAN["ff2"], False)
    here = rows_at(div(place.unit, 2) * slab, slab)

    def merge(at):
        y_copies[at][1].wait_recv()
        name, first, width = cuts[at]
        low = place.bit(0) == 0
        for column in range(0, width // 2, 256):
            size = min(256, width // 2 - column)
            part = rows_at(first + place.bit(0) * (width // 2) + column, size, 128)
            mine, other = shard2[:unit_rows, part].astype(F32), stage[:unit_rows, part].astype(F32)
            whole = jnp.concatenate([jnp.where(low, mine, other), jnp.where(low, other, mine)], axis=0)
            all2[here, part] = whole.astype(BF16)
        gathers[name].begin(gather_send.at[at], gather_recv.at[at])

    by_heads.send, by_heads.recv = block_send, block_recv
    if repeat == 1:
        for copy in plane_copies:
            copy.wait_recv()
        by_heads.release(2)
    else:
        by_heads.feed(0, 0)
        by_heads.step(0)
        by_heads.step(1)
    own_ff2.wait()
    by_heads.step(2)
    gathers["ff2"].begin(gather_send.at[2], gather_recv.at[2])
    merge(1)
    merge(0)
    by_heads.step(3)
    for name in REST:
        gathers[name].step(0)
    by_heads.step(4)

    def compact(pair, carry):
        whole = jnp.concatenate(
            [blocks[2 * pair][:unit_rows].astype(F32), blocks[2 * pair + 1][:unit_rows].astype(F32)], axis=0
        )
        heads[rows_at(pair * slab, slab)] = whole.astype(BF16)
        return carry

    lax.fori_loop(0, 16, compact, 0)
    params_out[...] = spread_rows(blocks[:, unit_rows:, 0:128].astype(F32).reshape(-1, 128), unit_rows, dim, 8)
    bias = jnp.zeros((2, PW), F32)
    for chip in range(CHIPS):
        cut = params_out[4:6, HW * chip:HW * (chip + 1)]
        query = jnp.concatenate([cut[0:1], jnp.zeros((1, PW - HW), F32)], axis=1)
        value = jnp.concatenate([jnp.zeros((1, PW - HW), F32), cut[1:2]], axis=1)
        bias = jnp.where(role == chip, query + value, bias)
    sibling = place.member(place.x, 1 - place.core, place.y)

    def stretch(slot, core):
        return window.at[slot].at[rows_at(half * core, half)]

    def part_of(slot, at):
        return window.at[slot].at[rows_at(half * place.core + tok * at, tok)]

    def side(to, at):
        return remote(
            part_of(1, at), part_of(2 * to, at), side_send.at[to, at], side_recv.at[to, at], place.beside(1 - 2 * to)
        )

    def near(at):
        ref = stretch(1, place.core) if at == 0 else stretch(2 - 2 * place.core, place.core)
        return remote(ref, ref, near_send.at[at], near_recv.at[at], sibling)

    for ys in (place.y, 1 - place.y):
        for cs in range(2):
            to_heads_wait_one(place, rows, row_send, row_recv, cs, ys)
            at = 2 * cs + ys
            part = rows_at(at * tok, tok)
            made = nn(rows[part, :], heads[...]) + bias[0:1]
            window[1, rows_at(half * place.core + at * tok, tok)] = made[:, QW:].astype(BF16)
            side(0, at).start()
            side(1, at).start()
            q_rows[part, :] = made[:, :QW].astype(BF16)
    near(0).start()
    hidden = blocks[:, unit_rows:, 128:256].astype(F32).reshape(-1, 128)
    ffb_out[...] = spread_rows(hidden, ff // 32, ff, 8)
    for name in REST:
        gathers[name].step(1)
    first_copies = [
        pltpu.make_async_copy(q_rows, q_out, local.at[2]),
        pltpu.make_async_copy(rows, rows_out, local.at[3]),
        pltpu.make_async_copy(heads, heads_out, local.at[4]),
    ]
    for copy in first_copies:
        copy.start()
    for phase in range(2, 5):
        for name in REST:
            gathers[name].step(phase)
    for gather in gathers.values():
        gather.finish()
    copies = [
        pltpu.make_async_copy(all2, all2_out, local.at[0]),
        pltpu.make_async_copy(all_ff2, ff2_out, local.at[1]),
    ]
    for copy in copies:
        copy.start()
    for at in range(4):
        side(0, at).wait_recv()
        side(1, at).wait_recv()
    near(1).start()
    near(0).wait_recv()
    near(1).wait_recv()
    last = pltpu.make_async_copy(window, kv_out, local.at[5])
    last.start()
    for at in range(2):
        y_copies[at][0].wait_send()
        near(at).wait_send()
        for part in range(4):
            side(at, part).wait_send()
    for copy in plane_copies:
        copy.wait_send()
    for phase in range(2 if repeat == 1 else 0, 5):
        for mask in range(1 << phase):
            by_heads.copy(phase, mask, by_heads.own).wait_send()
    to_heads_drain(place, rows, row_send, row_recv)
    for copy in first_copies + copies + [last]:
        copy.wait()


VM = pl.BlockSpec(memory_space=pltpu.VMEM)
HBM = pl.BlockSpec(memory_space=pl.ANY)
SM = pl.BlockSpec(memory_space=pltpu.SMEM)
DMA = pltpu.SemaphoreType.DMA


def enter(repeat, groups, shard_qkv, shard2, shard_ff2, small, tokens):
    tok, dim = tokens.shape
    joined = shard2.shape[1]
    ff = shard_ff2.shape[0] * 32
    shape = jax.ShapeDtypeStruct
    vm = pltpu.VMEM
    return pl.pallas_call(
        functools.partial(enter_kernel, repeat, groups),
        out_shape=(
            shape((dim, joined), BF16), shape((ff, dim), BF16), shape((8, dim), F32), shape((8, ff), F32),
            shape((4 * tok, QW), BF16), shape((3, 8 * tok, KW), BF16), shape((4 * tok, dim), BF16),
            shape((dim, PW), BF16),
        ),
        in_specs=[VM] * 5,
        out_specs=(HBM, HBM, VM, VM, HBM, HBM, HBM, HBM),
        scratch_shapes=[
            vm(shard2.shape, BF16), vm((dim, joined), BF16), vm((ff, dim), BF16),
            vm((4 * tok, QW), BF16), vm((3, 8 * tok, KW), BF16), vm((4 * tok, dim), BF16),
            vm((CHIPS, shard2.shape[0], PW), BF16), vm((32, shard2.shape[0], PW), BF16), vm((dim, PW), BF16),
            DMA((4,)), DMA((3, 31)), DMA((3, 31)), DMA((31,)), DMA((31,)), DMA((4,)), DMA((4,)),
            DMA((4,)), DMA((4,)), DMA((2,)), DMA((2,)), DMA((2, 4)), DMA((2, 4)), DMA((6,)),
        ],
        compiler_params=pltpu.CompilerParams(
            collective_id=1, has_side_effects=True, vmem_limit_bytes=VMEM_BYTES
        ),
    )(shard_qkv, shard2, shard_ff2, small, tokens)


def pack_small(norm_gains, norm_biases, proj_biases, ff_bias):
    rows = jnp.concatenate([norm_gains, norm_biases, proj_biases], axis=0)
    rows = jnp.pad(rows, ((0, 0), (0, 128 - rows.shape[1])))
    hidden = jnp.pad(ff_bias[None], ((0, 7), (0, PW - 128 - ff_bias.shape[0])))
    return jnp.concatenate([rows, hidden], axis=1)


QT = 512
KT = 512


def lane_mask(shape, low, high, axis):
    lane = lax.broadcasted_iota(jnp.int32, shape, axis)
    return (lane >= low) & (lane < high)


HEAD_QUERY = ((0, 0), (0, 64), (128, 0))
HEAD_VALUE = ((128, 64), (256, 0), (256, 64))
HEAD_CONTEXT = ((0, 64), (128, 0), (128, 64))


def head_rows(ref, rows, spot):
    tile, place = spot
    part = ref[rows, tile:tile + 128]
    return jnp.where(lane_mask(part.shape, place, place + HD, 1), part, jnp.zeros_like(part))


def doc_spans(starts, spans, total_rows):
    half = spans.shape[1]
    blk = lax.axis_index("blk")
    origin = (div(blk, GROUP) - 1) * 2 * half
    first = origin + (2 + rem(blk, 2)) * half
    far = jnp.int32(1 << 30)
    shape = (half // 128, 128)
    places = first + 128 * lax.broadcasted_iota(jnp.int32, shape, 0) + lax.broadcasted_iota(jnp.int32, shape, 1)
    edges = range(0, half, QT)

    def one(at, state):
        low, high, last, lows, highs = state
        start = starts[at]
        live = start < total_rows
        below = jnp.where(live, start, -far)
        above = jnp.where(live, start, far)
        low = jnp.where(below <= places, jnp.maximum(low, below), low)
        high = jnp.where(above > places, jnp.minimum(high, above), high)
        lows = tuple(jnp.where(below <= first + edge, jnp.maximum(old, below), old) for edge, old in zip(edges, lows))
        highs = tuple(
            jnp.where(above > first + edge + QT - 1, jnp.minimum(old, above), old) for edge, old in zip(edges, highs)
        )
        return low, high, jnp.maximum(last, below), lows, highs

    low, high, last, lows, highs = lax.fori_loop(
        0, starts.shape[0], one,
        (
            jnp.full(shape, -far), jnp.full(shape, far), -far,
            tuple(-far for _ in edges), tuple(far for _ in edges),
        ),
    )
    start, end = last - total_rows, starts[0] + total_rows
    low = jnp.where(low == -far, start, low) - origin
    high = jnp.where(high == far, end, high) - origin
    for at in range(shape[0]):
        spans[0:1, at * 128:(at + 1) * 128] = low[at:at + 1]
        spans[1:2, at * 128:(at + 1) * 128] = high[at:at + 1]
    tiles = []
    for old_low, old_high in zip(lows, highs):
        begin = jnp.where(old_low == -far, start, old_low) - origin
        finish = jnp.where(old_high == far, end, old_high) - origin
        tiles.append((div(begin, KT), div(finish + (KT - 1), KT)))
    return tiles


def meets(spans, columns, j):
    key = j * KT + lax.broadcasted_iota(jnp.int32, (KT, QT), 0)
    inside = (key >= spans[0:1, columns]) & (key < spans[1:2, columns])
    return jnp.where(inside, 0.0, NEGATIVE)


def forward_kernel(total_rows, starts, queries, window, context_out, sums_out, spans):
    spans[...] = jnp.zeros_like(spans)
    count = queries.shape[0]
    scale = HD ** (-0.5)
    tiles = doc_spans(starts, spans, total_rows)

    for at, (begin, finish) in enumerate(tiles):
        rows = slice(at * QT, (at + 1) * QT)
        columns = rows
        scaled = [head_rows(queries, rows, HEAD_QUERY[head]) * jnp.asarray(scale, BF16) for head in range(3)]

        def visit(j, state, columns=columns, scaled=scaled):
            keys = rows_at(j * KT, KT)
            bias = meets(spans, columns, j)
            tops, terms, fresh = [], [], []
            scores = [
                nt(window[keys, tile_at:tile_at + 128], scaled[head]) + bias
                for head, (tile_at, place) in enumerate(HEAD_QUERY)
            ]
            for head in range(3):
                tops.append(jnp.maximum(state[3 * head], jnp.max(scores[head], axis=0, keepdims=True)))
            for head in range(3):
                terms.append(jnp.exp(scores[head] - tops[head]))
            for head in range(3):
                highest, total, weighted = state[3 * head:3 * head + 3]
                tile_at = HEAD_VALUE[head][0]
                factor = jnp.exp(highest - tops[head])
                total = total * factor + jnp.sum(terms[head], axis=0, keepdims=True)
                weighted = weighted * factor + tn(window[keys, tile_at:tile_at + 128], terms[head].astype(BF16))
                fresh += [tops[head], total, weighted]
            return tuple(fresh)

        start = []
        for head in range(3):
            start += [jnp.full((1, QT), NEGATIVE, F32), jnp.zeros((1, QT), F32), jnp.zeros((128, QT), F32)]
        state = lax.fori_loop(begin, finish, visit, tuple(start))
        made = []
        for head in range(3):
            highest, total, weighted = state[3 * head:3 * head + 3]
            whole = weighted / total
            place = HEAD_CONTEXT[head][1]
            made.append(jnp.where(lane_mask(whole.shape, place, place + HD, 0), whole, 0.0))
            sums_out[head:head + 1, columns] = highest + jnp.log(total)
        context_out[rows, 0:128] = made[0].T
        context_out[rows, 128:256] = (made[1] + made[2]).T


def forward(total_rows, starts, queries, window):
    count = queries.shape[0]
    shape = jax.ShapeDtypeStruct
    return pl.pallas_call(
        functools.partial(forward_kernel, total_rows),
        out_shape=(shape((count, QW), F32), shape((8, count), F32), shape((8, count), jnp.int32)),
        in_specs=[SM] + [VM] * 2,
        out_specs=(VM, VM, VM),
        compiler_params=pltpu.CompilerParams(vmem_limit_bytes=VMEM_BYTES),
    )(starts, queries, window)


class Backward:
    def __init__(self, skip, queries, window, context, grads, sums, spans, by_query, by_grad, deltas, query_acc, acc):
        self.skip = skip
        self.window, self.sums, self.spans = window, sums, spans
        self.by_query, self.by_grad, self.deltas, self.query_acc, self.acc = by_query, by_grad, deltas, query_acc, acc
        scale = jnp.asarray(HD ** (-0.5), BF16)
        for head in range(3):
            every = slice(None)
            by_query[head] = head_rows(queries, every, HEAD_QUERY[head]) * scale
            mine = head_rows(grads, every, HEAD_CONTEXT[head])
            by_grad[head] = mine
            tile = HEAD_CONTEXT[head][0]
            product = mine.astype(F32) * context[:, tile:tile + 128]
            deltas[head:head + 1, :] = lax.dot_general(
                jnp.ones((8, 128), F32), product, (((1,), (1,)), ((), ())),
                precision=lax.Precision.HIGHEST, preferred_element_type=F32,
            )[0:1]
        acc[...] = jnp.zeros_like(acc)
        query_acc[...] = jnp.zeros_like(query_acc)

    def visit(self, at, j):
        rows, columns, keys = rows_at(at * QT, QT), rows_at(at * QT, QT, 128), rows_at(j * KT, KT)
        window, acc = self.window, self.acc.at[rows_at(j * KT - self.skip, KT)]
        bias = meets(self.spans, columns, j)
        key_grads, value_grads = [], []
        for head in range(3):
            key = window[keys, HEAD_QUERY[head][0]:HEAD_QUERY[head][0] + 128]
            value = window[keys, HEAD_VALUE[head][0]:HEAD_VALUE[head][0] + 128]
            query, grad = self.by_query[head, rows, :], self.by_grad[head, rows, :]
            probs = jnp.exp((nt(key, query) + bias) - self.sums[head:head + 1, columns])
            steps = (probs * (nt(value, grad) - self.deltas[head:head + 1, columns])).astype(BF16)
            value_grads.append(nn(probs.astype(BF16), grad))
            key_grads.append(nn(steps, query))
            self.query_acc[3 * at + head] += tn(key, steps)
        acc[:, 0:128] += key_grads[0] + key_grads[1]
        acc[:, 128:256] += key_grads[2] + value_grads[0]
        acc[:, 256:384] += value_grads[1] + value_grads[2]

    def run(self, count, where):
        def one(n, carry):
            self.visit(*where(n))
            return carry

        lax.fori_loop(0, count, one, 0)

    def query_rows(self, target):
        scale = HD ** (-0.5)
        for at in range(target.shape[0] // QT):
            made = []
            for head in range(3):
                place = HEAD_QUERY[head][1]
                mine = self.query_acc[3 * at + head]
                made.append(jnp.where(lane_mask(mine.shape, place, place + HD, 0), mine * scale, 0.0))
            rows = slice(at * QT, (at + 1) * QT)
            target[rows, 0:128] = (made[0] + made[1]).T.astype(BF16)
            target[rows, 128:256] = made[2].T.astype(BF16)


def norm_forward(values):
    center = values - jnp.mean(values, axis=-1, keepdims=True)
    scale = lax.rsqrt(jnp.mean(center * center, axis=-1, keepdims=True) + EPSILON)
    return center * scale, scale


def norm_backward(grad, unit_rows, scale, gain):
    inner = grad * gain
    gain_row = jnp.sum(grad * unit_rows, axis=0, keepdims=True)
    shift_row = jnp.sum(grad, axis=0, keepdims=True)
    back = scale * (
        inner
        - jnp.mean(inner, axis=-1, keepdims=True)
        - unit_rows * jnp.mean(inner * unit_rows, axis=-1, keepdims=True)
    )
    return back, gain_row, shift_row


def column_sum(values):
    return jnp.sum(values.astype(F32), axis=0, keepdims=True)


def middle_kernel(
    repeat, groups,
    context, tokens, d_out, params, ffb, all2, all_ff2,
    out, d_mid_out, grads_out, grad_o3, grad_ff2, sum_rows,
    w_out, w_ff1, w_ff2, ctx_rows, parts, pack, grad_rows, act, slope, d_pre,
    send, recv, back_send, back_recv, local,
):
    place = Place(repeat, groups)
    tok, dim = tokens.shape
    ff = w_ff1.shape[1]
    loads = [
        pltpu.make_async_copy(all2.at[:, pl.ds(0, dim)], w_out, local.at[0]),
        pltpu.make_async_copy(all2.at[:, pl.ds(dim, ff)], w_ff1, local.at[1]),
        pltpu.make_async_copy(all_ff2, w_ff2, local.at[2]),
    ]
    for load in loads:
        load.start()
    ctx_rows[...] = context[...].astype(BF16)
    place.greet(cube=False, beside=False)
    to_tokens(place, ctx_rows, parts, send, recv)
    to_tokens_wait(place, ctx_rows, parts, send, recv)
    joined = jnp.concatenate([parts[chip][:, QW - HW:].astype(F32) for chip in range(CHIPS)], axis=1).astype(BF16)
    loads[0].wait()
    gains, shifts = [params[at:at + 1, :] for at in (0, 1)], [params[at:at + 1, :] for at in (2, 3)]
    mid = tokens[...].astype(F32) + (nn(joined, w_out[...]) + params[6:7, :])
    unit_first, scale_first = norm_forward(mid)
    hidden = unit_first * gains[0] + shifts[0]
    low = hidden.astype(BF16)
    loads[1].wait()
    loads[2].wait()
    ff_out = jnp.zeros((tok, dim), F32)
    for first in range(0, ff, dim):
        cut = slice(first, first + dim)
        pre = nn(low, w_ff1[:, cut]) + ffb[0:1, cut]
        bell = 0.5 * (1.0 + lax.erf(pre * 0.7071067811865476))
        made = (pre * bell).astype(BF16)
        act[:, cut] = made
        slope[:, cut] = bell + pre * jnp.exp(-0.5 * pre * pre) * 0.3989422804014327
        ff_out = ff_out + nn(made, w_ff2[cut, :])
    unit_second, scale_second = norm_forward(hidden + (ff_out + params[7:8, :]))
    out[...] = (unit_second * gains[1] + shifts[1]).astype(BF16)
    d_sum, gain_second, shift_second = norm_backward(d_out[...].astype(F32), unit_second, scale_second, gains[1])
    d_ff = d_sum.astype(BF16)
    d_hidden = d_sum
    for first in range(0, ff, dim):
        cut = slice(first, first + dim)
        made = (nt(d_ff, w_ff2[cut, :]) * slope[:, cut]).astype(BF16)
        d_pre[:, cut] = made
        d_hidden = d_hidden + nt(made, w_ff1[:, cut])
    d_mid, gain_first, shift_first = norm_backward(d_hidden, unit_first, scale_first, gains[0])
    d_mid_out[...] = d_mid
    d_attn = d_mid.astype(BF16)
    d_context = nt(d_attn, w_out[...])
    for chip in range(CHIPS):
        pack[chip] = jnp.concatenate(
            [jnp.zeros((tok, QW - HW), F32), d_context[:, HW * chip:HW * (chip + 1)]], axis=1
        ).astype(BF16)
    to_heads(place, pack, grad_rows, back_send, back_recv)
    for first in range(0, ff, dim):
        cut = slice(first, first + dim)
        grad_ff2[cut, :] = tn(act[:, cut], d_ff).astype(BF16)
        grad_o3[:, dim + first:2 * dim + first] = tn(low, d_pre[:, cut]).astype(BF16)
        sum_rows[8 + first // dim:9 + first // dim, :] = column_sum(d_pre[:, cut])
    grad_o3[:, 0:dim] = tn(joined, d_attn).astype(BF16)
    for at, row in enumerate(
        (
            gain_first, gain_second, shift_first, shift_second,
            jnp.zeros((1, dim), F32), jnp.zeros((1, dim), F32), column_sum(d_attn), column_sum(d_ff),
        )
    ):
        sum_rows[at:at + 1, :] = row
    sum_rows[8 + ff // dim:, :] = jnp.zeros((8 - ff // dim, dim), F32)
    to_heads_wait(place, grad_rows, back_send, back_recv)
    grads_out[...] = grad_rows[...]
    to_tokens_drain(place, ctx_rows, parts, send, recv)
    to_heads_drain(place, grad_rows, back_send, back_recv)


def middle(repeat, groups, context, tokens, d_out, params, ffb, all2, all_ff2):
    tok, dim = tokens.shape
    ff = all_ff2.shape[0]
    shape = jax.ShapeDtypeStruct
    vm = pltpu.VMEM
    return pl.pallas_call(
        functools.partial(middle_kernel, repeat, groups),
        out_shape=(
            shape((tok, dim), BF16), shape((tok, dim), F32), shape((4 * tok, QW), BF16),
            shape((dim, dim + ff), BF16), shape((ff, dim), BF16), shape((16, dim), F32),
        ),
        in_specs=[VM] * 5 + [HBM] * 2,
        out_specs=(VM,) * 6,
        scratch_shapes=[
            vm((dim, dim), BF16), vm((dim, ff), BF16), vm((ff, dim), BF16), vm((4 * tok, QW), BF16),
            vm((CHIPS, tok, QW), BF16), vm((CHIPS, tok, QW), BF16), vm((4 * tok, QW), BF16),
            vm((tok, ff), BF16), vm((tok, ff), F32), vm((tok, ff), BF16),
            DMA((4,)), DMA((4,)), DMA((4,)), DMA((4,)), DMA((4,)),
        ],
        compiler_params=pltpu.CompilerParams(collective_id=2, has_side_effects=True, vmem_limit_bytes=VMEM_BYTES),
    )(context, tokens, d_out, params, ffb, all2, all_ff2)


def leave_kernel(
    repeat, groups,
    queries, window, context, grads, sums, spans, rows, heads, d_mid, sum_rows, grad_o2, grad_ff2_in,
    d_tokens, g_qkv, g_out, g_ff1, g_ff2, g_rows,
    by_query, by_grad, deltas, query_acc, acc,
    grad2, grad_ff2, land_out, land_ff1, land_ff2, blocks, land_blocks, role_land,
    near_out, near_land, side_land, solo_out, joint, joined, partial, parts, swap_out, swap_in, rows_mine, rows_land,
    grad_send, grad_recv, block_send, block_recv, plane_send, plane_recv, near_send, near_recv, side_send, side_recv,
    part_send, part_recv, swap_send, swap_recv, rows_send, rows_recv, local,
):
    place = Place(repeat, groups)
    tok, dim = d_mid.shape
    ff = grad_ff2.shape[0]
    unit_rows = dim // 32
    half = 4 * tok
    role = 2 * place.x + place.y
    core = place.core
    loads = [
        pltpu.make_async_copy(grad_o2, grad2, local.at[0]),
        pltpu.make_async_copy(grad_ff2_in, grad_ff2, local.at[1]),
    ]
    for load in loads:
        load.start()
    place.greet()
    sibling = place.member(place.x, 1 - core, place.y)

    def near(at):
        return remote(near_out, near_land.at[at], near_send.at[at], near_recv.at[at], sibling)

    solo = remote(
        solo_out, side_land.at[core], side_send.at[core], side_recv.at[core], place.beside(2 * core - 1)
    )
    shared = remote(
        joint, side_land.at[1 - core], side_send.at[1 - core], side_recv.at[1 - core], place.beside(1 - 2 * core)
    )
    cuts = matrices(dim, ff)
    scatters = {
        name: Scatter(place, grad2, 2 * unit_rows, first, width, RS_PLAN[name], True) for name, first, width in cuts
    }
    scatters["ff2"] = Scatter(place, grad_ff2, ff // 16, 0, dim, RS_PLAN["ff2"], False)
    loads[0].wait()
    loads[1].wait()
    scatters["ff2"].begin(land_ff2, grad_send.at[2], grad_recv.at[2])
    scatters["ff1"].begin(land_ff1, grad_send.at[1], grad_recv.at[1])
    scatters["out"].begin(land_out, grad_send.at[0], grad_recv.at[0])
    back = Backward(core * half, queries, window, context, grads, sums, spans, by_query, by_grad, deltas, query_acc, acc)

    def made(slot, which):
        return acc[rows_at(2 * half * slot + half * which - half * core, half), :]

    back.run(4, lambda n: (rem(n, 2), 2 + 6 * core + div(n, 2)))
    near_out[...] = made(2 * core, 1 - core).astype(BF16)
    near(0).start()
    for name in REST:
        scatters[name].step(0)

    def solo_tile(n):
        single = div(n, 2)
        return single * core + (1 - single) * n, single * (11 * core) + (1 - single) * (1 + 9 * core)

    def shared_tile(n):
        single = div(n, 2)
        return single * (1 - core) + (1 - single) * n, single * (9 - 7 * core) + (1 - single) * (8 - 5 * core)

    back.run(3, solo_tile)
    solo_out[...] = made(2 * core, core).astype(BF16)
    solo.start()
    back.run(3, shared_tile)
    near(0).wait_recv()
    joint[...] = (made(2 - 2 * core, core) + near_land[0].astype(F32)).astype(BF16)
    shared.start()
    back.run(4, lambda n: (rem(n, 2), 6 - 2 * core + div(n, 2)))
    near(0).wait_send()
    near_out[...] = made(1, 1 - core).astype(BF16)
    near(1).start()
    for name in REST:
        scatters[name].step(1)
    back.run(4, lambda n: (rem(n, 2), 4 + 2 * core + div(n, 2)))
    back.query_rows(joined)
    near(1).wait_recv()
    own = made(1, core) + near_land[1].astype(F32)
    for at in range(2):
        remote(joint, side_land.at[at], side_send.at[at], side_recv.at[at], sibling).wait_recv()
    joined[:, QW:] = (own + side_land[0].astype(F32) + side_land[1].astype(F32)).astype(BF16)
    for at in range(4):
        part = slice(at * tok, (at + 1) * tok)
        partial[part, :] = nt(joined[part, :], heads[...]).astype(BF16)
    to_tokens(place, partial, parts, part_send, part_recv)
    whole = tn(rows[...], joined[...])
    for unit in range(32):
        block = whole[unit * unit_rows:(unit + 1) * unit_rows]
        pad = jnp.zeros((blocks.shape[1] - unit_rows, PW), F32)
        blocks[unit] = jnp.concatenate([block, pad], axis=0).astype(BF16)
    until = 3 if repeat == 1 else 5
    by_heads = ScatterBlocks(place, blocks, RS_HEADS, until)
    by_heads.begin(land_blocks, block_send, block_recv)
    sums = column_sum(joined[...])
    rows_mine[0] = sum_rows[...]
    for row, first in ((4, 0), (5, PW - HW)):
        line = [jnp.where(role == chip, sums[:, first:first + HW], 0.0) for chip in range(CHIPS)]
        rows_mine[0, row:row + 1, :] = jnp.concatenate(line, axis=1)

    def rows_copy(phase):
        return remote(
            rows_mine.at[phase], rows_land.at[phase], rows_send.at[phase], rows_recv.at[phase],
            place.partner(RS_HEADS[phase]),
        )

    def rows_add(phase):
        rows_copy(phase).wait_recv()
        rows_mine[phase + 1] = rows_mine[phase] + rows_land[phase]
        if phase < 4:
            rows_copy(phase + 1).start()

    rows_copy(0).start()
    by_heads.step(0)
    rows_add(0)
    by_heads.step(1)
    rows_add(1)
    for phase in range(SPLIT, 4):
        for name in REST:
            scatters[name].step(phase)
    by_heads.step(2)
    rows_add(2)

    def role_copy(dx, dy):
        chip, device = plane(place, dx, dy)
        at = 2 * dx + dy
        there = place.unit + dx * 4 * (1 - 2 * place.bit(2)) + dy * (1 - 2 * place.bit(0))
        return remote(blocks.at[there], role_land.at[role], plane_send.at[at], plane_recv.at[at], device)

    if repeat == 1:
        for dx, dy in ((1, 1), (1, 0), (0, 1)):
            role_copy(dx, dy).start()
    else:
        by_heads.step(3)
        by_heads.last()
        role_land[...] = jnp.zeros_like(role_land)
    role_land[role] = blocks[place.unit]
    rows_add(3)

    def swap(at):
        name, first, width = cuts[at]
        part = (slice(None), pl.ds(first // 2, width // 2))
        return remote(swap_out.at[part], swap_in.at[part], swap_send.at[at], swap_recv.at[at], place.partner(0))

    def finish_half(at):
        name, first, width = cuts[at]
        target = (g_out, g_ff1)[at]
        total = scatters[name].last()
        high = place.bit(0) == 1
        keep = jnp.where(high, total[unit_rows:], total[:unit_rows])
        give = jnp.where(high, total[:unit_rows], total[unit_rows:])
        pad = jnp.zeros((swap_out.shape[0] - unit_rows, give.shape[1]), F32)
        swap_out[:, first // 2:(first + width) // 2] = jnp.concatenate([give, pad], axis=0).astype(BF16)
        swap(at).start()
        target[:, rows_at(place.bit(0) * (width // 2), width // 2, 128)] = keep

    def finish_swap(at):
        name, first, width = cuts[at]
        target = (g_out, g_ff1)[at]
        swap(at).wait_recv()
        other = swap_in[:, first // 2:(first + width) // 2].astype(F32)[:unit_rows]
        target[:, rows_at((1 - place.bit(0)) * (width // 2), width // 2, 128)] = other

    for at in (1, 0):
        finish_half(at)
    g_ff2[...] = scatters["ff2"].last()
    rows_add(4)
    g_rows[...] = rows_mine[5]
    to_tokens_wait(place, partial, parts, part_send, part_recv)
    d_tokens[...] = (
        d_mid[...] + (parts[0].astype(F32) + parts[1].astype(F32)) + (parts[2].astype(F32) + parts[3].astype(F32))
    ).astype(BF16)
    for at in (1, 0):
        finish_swap(at)
    if repeat == 1:
        for dx, dy in ((1, 1), (1, 0), (0, 1)):
            role_copy(dx, dy).wait_recv()
    for part, first in ((0, 0), (1, QW), (2, QW + HW)):
        line = [role_land[chip][:unit_rows, first:first + HW].astype(F32) for chip in range(CHIPS)]
        g_qkv[:, part * dim:(part + 1) * dim] = jnp.concatenate(line, axis=1)
    for scatter in scatters.values():
        scatter.finish()
    by_heads.finish()
    if repeat == 1:
        for dx, dy in ((1, 1), (1, 0), (0, 1)):
            role_copy(dx, dy).wait_send()
    for at in range(2):
        swap(at).wait_send()
    near(1).wait_send()
    solo.wait_send()
    shared.wait_send()
    for phase in range(5):
        rows_copy(phase).wait_send()
    to_tokens_drain(place, partial, parts, part_send, part_recv)


SPLIT = 2


def leave(repeat, groups, attention, rows, heads, d_mid, sum_rows, grad_o2, grad_ff2):
    tok, dim = d_mid.shape
    ff = grad_ff2.shape[0]
    unit = dim // 32
    slab = 2 * unit
    half = 4 * tok
    wide = -(-unit // 16) * 16
    shape = jax.ShapeDtypeStruct
    vm = pltpu.VMEM
    return pl.pallas_call(
        functools.partial(leave_kernel, repeat, groups),
        out_shape=(
            shape((tok, dim), BF16), shape((unit, 3 * dim), F32), shape((unit, dim), F32), shape((unit, ff), F32),
            shape((ff // 32, dim), F32), shape((16, dim), F32),
        ),
        in_specs=[VM] * 10 + [HBM] * 2,
        out_specs=(VM,) * 6,
        scratch_shapes=[
            vm((3, half, 128), BF16), vm((3, half, 128), BF16), vm((8, half), F32), vm((3 * half // QT, 128, QT), F32),
            vm((5 * half, KW), F32),
            vm((dim, dim + ff), BF16), vm((ff, dim), BF16),
            vm((31, slab, dim // 2), BF16), vm((31, slab, ff // 2), BF16), vm((31, ff // 32, dim), BF16),
            vm((32, wide, PW), BF16), vm((31, wide, PW), BF16), vm((CHIPS, wide, PW), BF16),
            vm((half, KW), BF16), vm((2, half, KW), BF16), vm((2, half, KW), BF16), vm((half, KW), BF16),
            vm((half, KW), BF16), vm((half, PW), BF16),
            vm((half, dim), BF16), vm((CHIPS, tok, dim), BF16),
            vm((wide, (dim + ff) // 2), BF16), vm((wide, (dim + ff) // 2), BF16),
            vm((6, 16, dim), F32), vm((5, 16, dim), F32),
            DMA((3, 31)), DMA((3, 31)), DMA((31,)), DMA((31,)), DMA((4,)), DMA((4,)), DMA((2,)), DMA((2,)), DMA((2,)),
            DMA((2,)), DMA((4,)), DMA((4,)), DMA((2,)), DMA((2,)), DMA((5,)), DMA((5,)), DMA((2,)),
        ],
        compiler_params=pltpu.CompilerParams(collective_id=3, has_side_effects=True, vmem_limit_bytes=VMEM_BYTES),
    )(*attention, rows, heads, d_mid, sum_rows, grad_o2, grad_ff2)


def settle_kernel(
    repeat, out, d_tokens, g_qkv, g_out, g_ff1, g_ff2, g_rows,
    out_r, d_tokens_r, g_qkv_r, g_out_r, g_ff1_r, g_ff2_r, gains_r, shifts_r, biases_r, hidden_r,
):
    for source, target in (
        (out, out_r), (d_tokens, d_tokens_r), (g_qkv, g_qkv_r), (g_out, g_out_r), (g_ff1, g_ff1_r), (g_ff2, g_ff2_r)
    ):
        target[...] = source[...]
    width = g_rows.shape[1]
    per, hidden = gains_r.shape[1], hidden_r.shape[1]
    unit = div(lax.axis_index("blk") * 2 + lax.axis_index("head"), repeat)
    turned = pltpu.roll(g_rows[0:8, :], rem(width - unit * per, width), 1)
    gains_r[...] = turned[0:2, :per]
    shifts_r[...] = turned[2:4, :per]
    biases_r[...] = turned[4:8, :per]
    lines = g_rows[8:16, :]
    row = lax.broadcasted_iota(jnp.int32, lines.shape, 0)
    mine = jnp.sum(jnp.where(row == div(unit * hidden, width), lines, 0.0), axis=0, keepdims=True)
    turned = pltpu.roll(jnp.broadcast_to(mine, lines.shape), rem(width - rem(unit * hidden, width), width), 1)
    hidden_r[...] = turned[0:1, :hidden]


def settle(repeat, results):
    shape = jax.ShapeDtypeStruct
    per, hidden = results[2].shape[0], results[5].shape[0]
    small = [shape((count, per), F32) for count in (2, 2, 4)] + [shape((1, hidden), F32)]
    return pl.pallas_call(
        functools.partial(settle_kernel, repeat),
        out_shape=[shape(value.shape, value.dtype) for value in results[:6]] + small,
        in_specs=[VM] * 7,
        out_specs=[VM] * 10,
        compiler_params=pltpu.CompilerParams(vmem_limit_bytes=VMEM_BYTES),
    )(*results)


def gather_repeat(value, repeat, axis):
    if repeat == 1:
        return value
    count = repeat // 2
    sets = [list(range(at, at + count)) for at in range(0, lax.axis_size("blk"), count)]
    value = lax.all_gather(value, "head", axis=axis, tiled=True)
    if count == 1:
        return value
    return lax.all_gather(value, "blk", axis=axis, tiled=True, axis_index_groups=sets)


def own_share(value, repeat, axis):
    if repeat == 1:
        return value
    count = repeat // 2
    sets = [list(range(at, at + count)) for at in range(0, lax.axis_size("blk"), count)]
    value = lax.psum(value, "head")
    if count > 1:
        value = lax.psum(value, "blk", axis_index_groups=sets)
    size = value.shape[axis] // repeat
    at = jnp.mod(lax.axis_index("blk") * 2 + lax.axis_index("head"), repeat)
    return lax.dynamic_slice_in_dim(value, at * size, size, axis)


def body(tokens, w_qkv, w_out, w_ff1, w_ff2, norm_gains, norm_biases, proj_biases, ff_bias, doc_starts, d_out):
    blks = lax.axis_size("blk")
    repeat = blks * 2 // 32
    groups = blks // GROUP
    tok, dim = tokens.shape
    half_rows = 4 * tok
    total_rows = blks * 2 * tok
    shard_qkv = gather_repeat(w_qkv, repeat, 0)
    shard2 = gather_repeat(jnp.concatenate([w_out, w_ff1], axis=1), repeat, 0)
    shard2 = jnp.pad(shard2, ((0, -shard2.shape[0] % 16), (0, 0)))
    shard_ff2 = gather_repeat(w_ff2, repeat, 0)
    small = pack_small(
        gather_repeat(norm_gains, repeat, 1), gather_repeat(norm_biases, repeat, 1),
        gather_repeat(proj_biases, repeat, 1), gather_repeat(ff_bias, repeat, 0),
    )
    all2, all_ff2, params, ffb, queries, window, rows, heads = enter(
        repeat, groups, shard_qkv, shard2, shard_ff2, small, tokens
    )
    window = window.reshape(6 * half_rows, KW)
    context, sums, spans = forward(total_rows, doc_starts, queries, window)
    out, d_mid, grads, grad_o2, grad_ff2, sum_rows = middle(
        repeat, groups, context, tokens, d_out, params, ffb, all2, all_ff2
    )
    d_tokens, g_qkv, g_out, g_ff1, g_ff2, g_rows = leave(
        repeat, groups, (queries, window, context, grads, sums, spans), rows, heads, d_mid, sum_rows, grad_o2, grad_ff2
    )
    results = settle(repeat, (out, d_tokens, g_qkv, g_out, g_ff1, g_ff2, g_rows))
    axes = (None, None, 0, 0, 0, 0, 1, 1, 1, 0)
    results = list(results[:9]) + [results[9].reshape(-1)]
    return tuple(
        value if axis is None else own_share(value, repeat, axis) for value, axis in zip(results, axes)
    )


def solution(mesh):
    rows, columns, flat = P(("blk", "head"), None), P(None, ("blk", "head")), P(("blk", "head"))
    return jax.shard_map(
        body,
        mesh=mesh,
        in_specs=(rows,) * 5 + (columns,) * 3 + (flat, P(), rows),
        out_specs=(rows,) * 6 + (columns,) * 3 + (flat,),
        check_vma=False,
    )
```

```python
import functools

import jax
import jax.numpy as jnp
from jax import lax
from jax.experimental import pallas as pl
from jax.experimental.pallas import tpu as pltpu
from jax.sharding import PartitionSpec as P

H = 12
HD = 64
DOC_MOST = 2048
EPSILON = 1e-06
NEGATIVE = -1e30
MESH = pl.DeviceIdType.MESH
F32 = jnp.float32
BF16 = jnp.bfloat16
VMEM_BYTES = 62 * 1024 * 1024
CHIPS = 4
GROUP = 4
QW = 256
KW = 384
HW = (H // CHIPS) * HD
PW = QW + KW


def div(a, b):
    return lax.div(a, jnp.int32(b))


def rem(a, b):
    return lax.rem(a, jnp.int32(b))


def nn(a, b):
    return lax.dot_general(a, b, (((1,), (0,)), ((), ())), preferred_element_type=F32)


def nt(a, b):
    return lax.dot_general(a, b, (((1,), (1,)), ((), ())), preferred_element_type=F32)


def tn(a, b):
    return lax.dot_general(a, b, (((0,), (0,)), ((), ())), preferred_element_type=F32)


def rows_at(start, count, unit=16):
    return pl.ds(pl.multiple_of(start, unit), count)


class Place:
    def __init__(self, repeat, groups):
        self.repeat = repeat
        blk, head = lax.axis_index("blk"), lax.axis_index("head")
        self.index = blk * 2 + head
        self.unit = div(self.index, repeat)
        self.core, self.x, self.y = rem(blk, 2), rem(div(blk, 2), 2), head
        self.group, self.groups = div(blk, GROUP), groups
        self.bits = [rem(div(self.unit, 1 << k), 2) for k in range(5)]
        others = [self.index + (1 - 2 * self.bits[k]) * (repeat << k) for k in range(5)]
        self.partners = [{"blk": div(other, 2), "head": rem(other, 2)} for other in others]

    def bit(self, k):
        return self.bits[k]

    def partner(self, k):
        return self.partners[k]

    def member(self, x, core, y):
        return {"blk": self.group * GROUP + 2 * x + core, "head": y}

    def beside(self, step):
        group = rem(self.group + self.groups + step, self.groups)
        return {"blk": group * GROUP + 2 * self.x + self.core, "head": self.y}

    def greet(self, cube=True, group=True, beside=True):
        barrier = pltpu.get_barrier_semaphore()
        partners = []
        if cube:
            partners += [self.partner(k) for k in range(5)]
        if group:
            partners += [
                self.member(
                    rem(self.x + dx, 2), rem(self.core + dc, 2), rem(self.y + dy, 2)
                )
                for dx in range(2)
                for dc in range(2)
                for dy in range(2)
                if dx + dc + dy
            ]
        if beside:
            partners += [self.beside(1), self.beside(-1)]
        for partner in partners:
            pl.semaphore_signal(barrier, inc=1, device_id=partner, device_id_type=MESH)
        pl.semaphore_wait(barrier, len(partners))


def remote(src, dst, send, recv, device):
    return pltpu.make_async_remote_copy(
        src_ref=src, dst_ref=dst, send_sem=send, recv_sem=recv, device_id=device, device_id_type=MESH
    )


class Pieces:
    def __init__(self, place, ref, rows, first, width, order, by_columns):
        self.place, self.ref, self.rows, self.first, self.width = place, ref, rows, first, width
        self.order, self.by_columns = order, by_columns
        if by_columns is not None:
            self.shape = (rows, width // 2) if by_columns else (rows // 2, width)
        self.deltas = [(1 - 2 * place.bit(k)) * (1 << k) for k in order]
        self.units = {0: place.unit}
        self.own = self.piece(0)

    def unit_of(self, mask):
        if mask not in self.units:
            at = mask.bit_length() - 1
            self.units[mask] = self.unit_of(mask - (1 << at)) + self.deltas[at]
        return self.units[mask]

    def region(self, unit):
        slab, half = div(unit, 2), rem(unit, 2)
        if self.by_columns:
            return (
                rows_at(slab * self.rows, self.rows),
                rows_at(self.first + half * self.shape[1], self.shape[1], 128),
            )
        return (rows_at(unit * self.shape[0], self.shape[0]), pl.ds(self.first, self.width))

    def piece(self, mask):
        return self.ref.at[self.region(self.unit_of(mask))]


class Gather(Pieces):
    def begin(self, send, recv, until=5):
        self.send, self.recv = send, recv
        self.feed(0, 0, until)

    def copy(self, phase, mask, ref):
        at = (1 << phase) - 1 + mask
        return remote(ref, ref, self.send.at[at], self.recv.at[at], self.place.partner(self.order[phase]))

    def feed(self, mask, phase, until=5):
        if phase < until:
            ref = self.piece(mask)
            for later in range(phase, until):
                self.copy(later, mask, ref).start()

    def release(self, phase):
        for mask in range(1 << phase):
            self.feed(mask, phase)

    def step(self, phase, until=5):
        for mask in range(1 << phase):
            self.copy(phase, mask, self.own).wait_recv()
            self.feed(mask + (1 << phase), phase + 1, until)

    def finish(self):
        for phase in range(5):
            for mask in range(1 << phase):
                self.copy(phase, mask, self.own).wait_send()


def soonest(count):
    return sorted(range(count), key=lambda j: (j & -j) if j else count)


class Scatter(Pieces):
    def begin(self, landing, send, recv, since=0):
        self.landing, self.send, self.recv, self.since = landing, send, recv, since
        for j in soonest(16 >> since):
            self.give(since, j)

    def slot(self, phase, j):
        return (32 >> self.since) - (1 << (5 - phase)) + j

    def copy(self, phase, j, ref):
        at = self.slot(phase, j)
        return remote(
            ref, self.landing.at[at], self.send.at[at], self.recv.at[at], self.place.partner(self.order[phase])
        )

    def give(self, phase, j):
        self.copy(phase, j, self.piece((2 * j + 1) * (1 << phase))).start()

    def absorb(self, phase, j):
        self.copy(phase, j, self.own).wait_recv()
        rows, columns = self.region(self.unit_of(j * (2 << phase)))
        if phase == 4:
            return self.ref[rows, columns].astype(F32) + self.landing[self.slot(phase, j)].astype(F32)
        self.ref[rows, columns] = self.ref[rows, columns] + self.landing[self.slot(phase, j)]

    def step(self, phase):
        half = 1 << (3 - phase)
        for jj in soonest(half):
            self.absorb(phase, 2 * jj + 1)
            self.give(phase + 1, jj)
        for jj in soonest(half):
            self.absorb(phase, 2 * jj)

    def stage(self, at):
        for j in soonest(1 << (4 - at)):
            if at < 4 and j % 2 == 0:
                continue
            for phase in range(1, at + 1):
                if phase < 4:
                    self.absorb(phase, j << (at - phase))
            if at < 4:
                self.give(at + 1, j >> 1)

    def last(self):
        return self.absorb(4, 0)

    def finish(self, until=5):
        for phase in range(self.since, until):
            for j in range(1 << (4 - phase)):
                self.copy(phase, j, self.own).wait_send()


class GatherBlocks(Gather):
    def __init__(self, place, ref, order):
        self.shape = ref.shape[1:]
        Pieces.__init__(self, place, ref, 0, 0, 0, order, None)

    def piece(self, mask):
        return self.ref.at[self.unit_of(mask)]


class ScatterBlocks(Scatter):
    def __init__(self, place, ref, order, until):
        Pieces.__init__(self, place, ref, 0, 0, 0, order, None)
        self.until = until

    def piece(self, mask):
        return self.ref.at[self.unit_of(mask)]

    def give(self, phase, j):
        if phase < self.until:
            Scatter.give(self, phase, j)

    def absorb(self, phase, j):
        self.copy(phase, j, self.own).wait_recv()
        unit = self.unit_of(j * (2 << phase))
        self.ref[unit] = self.ref[unit] + self.landing[self.slot(phase, j)]

    def finish(self):
        for phase in range(self.until):
            for j in range(1 << (4 - phase)):
                self.copy(phase, j, self.own).wait_send()


def to_heads(place, packed, landed, send, recv, part=None):
    tok = packed.shape[1] if part is None else part.shape[0]
    mine = rows_at(2 * tok * place.core + tok * place.y, tok)
    slot = 2 * place.core + place.y
    alone = place.core == place.x
    for dx, dy in ((0, 0), (1, 0), (0, 1), (1, 1)):
        if True:
            tx, ty = rem(place.x + dx, 2), rem(place.y + dy, 2)
            copy = remote(
                packed.at[2 * tx + ty] if part is None else part,
                landed.at[mine],
                send.at[2 * dx + dy],
                recv.at[slot],
                place.member(tx, place.x, ty),
            )
            if dx + dy:
                copy.start()
            else:
                pl.when(jnp.logical_not(alone))(copy.start)

                @pl.when(alone)
                def _(tx=tx, ty=ty):
                    landed[mine] = packed[2 * tx + ty] if part is None else part[...]


def to_heads_wait_one(place, landed, send, recv, cs, ys):
    tok = landed.shape[0] // 4
    part = landed.at[pl.ds(0, tok)]
    copy = remote(part, part, send.at[0], recv.at[2 * cs + ys], place.member(place.x, 1 - place.core, place.y))
    own = (place.core == place.x) & (place.core == cs) & (place.y == ys)
    pl.when(jnp.logical_not(own))(copy.wait_recv)


def to_heads_wait(place, landed, send, recv):
    for cs in range(2):
        for ys in range(2):
            to_heads_wait_one(place, landed, send, recv, cs, ys)


def to_heads_drain(place, landed, send, recv):
    part = landed.at[pl.ds(0, landed.shape[0] // 4)]
    for at in range(4):
        copy = remote(part, part, send.at[at], recv.at[0], place.member(place.x, 1 - place.core, place.y))
        if at:
            copy.wait_send()
        else:
            pl.when(place.core != place.x)(copy.wait_send)


def to_tokens(place, rows, landed, send, recv):
    tok = landed.shape[1]
    chip = 2 * place.x + place.y
    for cs in range(2):
        for ys in range(2):
            part = pl.ds(2 * tok * cs + tok * ys, tok)
            own = (place.core == place.x) & (place.core == cs) & (place.y == ys)
            copy = remote(
                rows.at[part], landed.at[chip], send.at[2 * cs + ys], recv.at[chip], place.member(place.core, cs, ys)
            )
            pl.when(jnp.logical_not(own))(copy.start)

            @pl.when(own)
            def _(part=part):
                landed[chip] = rows[part]


def to_tokens_wait(place, rows, landed, send, recv):
    for xs in range(2):
        for ys in range(2):
            at = 2 * xs + ys
            own = (place.core == place.x) & (place.x == xs) & (place.y == ys)
            copy = remote(
                landed.at[at], landed.at[at], send.at[at], recv.at[at], place.member(place.x, 1 - place.core, place.y)
            )
            pl.when(jnp.logical_not(own))(copy.wait_recv)


def to_tokens_drain(place, rows, landed, send, recv):
    for cs in range(2):
        for ys in range(2):
            own = (place.core == place.x) & (place.core == cs) & (place.y == ys)
            at = 2 * cs + ys
            copy = remote(
                landed.at[at], landed.at[at], send.at[at], recv.at[at], place.member(place.x, 1 - place.core, place.y)
            )
            pl.when(jnp.logical_not(own))(copy.wait_send)


def spread_rows(small, per, width, rows):
    lane = lax.broadcasted_iota(jnp.int32, (128, width), 1).astype(F32)
    spot = lane - per * jnp.floor((lane + 0.5) * (1.0 / per))
    pick = (spot == lax.broadcasted_iota(jnp.int32, (128, width), 0).astype(F32)).astype(BF16)
    wide = nn(small.astype(BF16), pick).reshape(32, rows, width)
    low = lax.broadcasted_iota(jnp.int32, wide.shape, 0) * per
    column = lax.broadcasted_iota(jnp.int32, wide.shape, 2)
    return jnp.sum(jnp.where((column >= low) & (column < low + per), wide, 0.0), axis=0)


AG_PLAN = dict(out=(4, 3, 0, 2, 1), ff1=(4, 3, 0, 2, 1), ff2=(4, 3, 2, 0, 1))
AG_HEADS = (2, 0, 4, 3, 1)
RS_PLAN = dict(out=(1, 2, 0, 3, 4), ff1=(1, 2, 0, 3, 4), ff2=(1, 0, 2, 3, 4))
RS_HEADS = (1, 3, 4, 2, 0)
REST = ("ff2", "ff1", "out")


def matrices(dim, ff):
    return (("out", 0, dim), ("ff1", dim, ff))


def plane(place, dx, dy):
    tx, ty = rem(place.x + dx, 2), rem(place.y + dy, 2)
    return 2 * tx + ty, place.member(tx, place.core, ty)


def enter_kernel(
    repeat, groups,
    starts, shard_qkv, shard2, shard_ff2, small, tokens,
    all2_out, ff2_out, params_out, ffb_out, q_out, kv_out, rows_out, heads_out, context, sums, spans,
    by_query, stats, weighted, stage, all2, all_ff2, q_rows, window, rows, pack_w, blocks, heads,
    y_sems, gather_send, gather_recv, block_send, block_recv, plane_send, plane_recv,
    row_send, row_recv, near_send, near_recv, side_send, side_recv, local,
):
    place = Place(repeat, groups)
    dim = all2.shape[0]
    ff = all_ff2.shape[0]
    tok = tokens.shape[0]
    unit_rows = dim // 32
    slab = 2 * unit_rows
    half = 4 * tok
    own_ff2 = pltpu.make_async_copy(
        shard_ff2, all_ff2.at[rows_at(place.unit * (ff // 32), ff // 32)], local.at[0]
    )
    own_ff2.start()
    wide = shard_qkv[...].astype(F32)
    for chip in range(CHIPS):
        cut = [wide[:, part * dim + HW * chip:part * dim + HW * (chip + 1)] for part in range(3)]
        block = jnp.concatenate([cut[0], jnp.zeros((unit_rows, QW - HW), F32), cut[1], cut[2]], axis=1)
        pack_w[chip] = jnp.concatenate([block, small[...].astype(F32)], axis=0).astype(BF16)
    role = 2 * place.x + place.y
    blocks[place.unit] = pack_w[role]
    place.greet()
    plane_copies = []
    if repeat == 1:
        for dx, dy in ((1, 1), (1, 0), (0, 1)):
            chip, device = plane(place, dx, dy)
            at = 2 * dx + dy
            copy = remote(pack_w.at[chip], blocks.at[place.unit], plane_send.at[at], plane_recv.at[at], device)
            copy.start()
            plane_copies.append(copy)
    to_heads(place, None, rows, row_send, row_recv, tokens)
    cuts = matrices(dim, ff)
    y_copies = []

    def half_columns(at, which):
        name, first, width = cuts[at]
        return (slice(None), rows_at(first + which * (width // 2), width // 2, 128))

    for at in range(2):
        mine, other = half_columns(at, place.bit(0)), half_columns(at, 1 - place.bit(0))
        out = remote(shard2.at[other], stage.at[other], y_sems.at[at], y_sems.at[2 + at], place.partner(0))
        back = remote(shard2.at[mine], stage.at[mine], y_sems.at[at], y_sems.at[2 + at], place.partner(0))
        out.start()
        y_copies.append((out, back))

    by_heads = GatherBlocks(place, blocks, AG_HEADS)
    gathers = {name: Gather(place, all2, slab, first, width, AG_PLAN[name], True) for name, first, width in cuts}
    gathers["ff2"] = Gather(place, all_ff2, ff // 16, 0, dim, AG_PLAN["ff2"], False)
    here = rows_at(div(place.unit, 2) * slab, slab)

    def merge(at):
        y_copies[at][1].wait_recv()
        name, first, width = cuts[at]
        low = place.bit(0) == 0
        for column in range(0, width // 2, 256):
            size = min(256, width // 2 - column)
            part = rows_at(first + place.bit(0) * (width // 2) + column, size, 128)
            mine, other = shard2[:unit_rows, part].astype(F32), stage[:unit_rows, part].astype(F32)
            whole = jnp.concatenate([jnp.where(low, mine, other), jnp.where(low, other, mine)], axis=0)
            all2[here, part] = whole.astype(BF16)
        gathers[name].begin(gather_send.at[at], gather_recv.at[at])

    by_heads.send, by_heads.recv = block_send, block_recv
    if repeat == 1:
        for copy in plane_copies:
            copy.wait_recv()
        by_heads.release(2)
    else:
        by_heads.feed(0, 0)
        by_heads.step(0)
        by_heads.step(1)
    own_ff2.wait()
    by_heads.step(2)
    gathers["ff2"].begin(gather_send.at[2], gather_recv.at[2])
    merge(1)
    merge(0)
    by_heads.step(3)
    for name in REST:
        gathers[name].step(0)
    by_heads.step(4)

    def compact(pair, carry):
        whole = jnp.concatenate(
            [blocks[2 * pair][:unit_rows].astype(F32), blocks[2 * pair + 1][:unit_rows].astype(F32)], axis=0
        )
        heads[rows_at(pair * slab, slab)] = whole.astype(BF16)
        return carry

    lax.fori_loop(0, 16, compact, 0)
    params_out[...] = spread_rows(blocks[:, unit_rows:, 0:128].astype(F32).reshape(-1, 128), unit_rows, dim, 8)
    bias = jnp.zeros((2, PW), F32)
    for chip in range(CHIPS):
        cut = params_out[4:6, HW * chip:HW * (chip + 1)]
        query = jnp.concatenate([cut[0:1], jnp.zeros((1, PW - HW), F32)], axis=1)
        value = jnp.concatenate([jnp.zeros((1, PW - HW), F32), cut[1:2]], axis=1)
        bias = jnp.where(role == chip, query + value, bias)
    sibling = place.member(place.x, 1 - place.core, place.y)

    def stretch(slot, core):
        return window.at[rows_at(half * (2 * slot + core), half)]

    def part_of(slot, at):
        return window.at[rows_at(half * (2 * slot + place.core) + tok * at, tok)]

    def side(to, at):
        return remote(
            part_of(1, at), part_of(2 * to, at), side_send.at[to, at], side_recv.at[to, at], place.beside(1 - 2 * to)
        )

    def near(at):
        ref = stretch(1, place.core) if at == 0 else stretch(2 - 2 * place.core, place.core)
        return remote(ref, ref, near_send.at[at], near_recv.at[at], sibling)

    for ys in (place.y, 1 - place.y):
        for cs in range(2):
            to_heads_wait_one(place, rows, row_send, row_recv, cs, ys)
            at = 2 * cs + ys
            part = rows_at(at * tok, tok)
            made = nn(rows[part, :], heads[...]) + bias[0:1]
            window[rows_at(half * (2 + place.core) + at * tok, tok)] = made[:, QW:].astype(BF16)
            side(0, at).start()
            side(1, at).start()
            q_rows[part, :] = made[:, :QW].astype(BF16)
    near(0).start()
    hidden = blocks[:, unit_rows:, 128:256].astype(F32).reshape(-1, 128)
    ffb_out[...] = spread_rows(hidden, ff // 32, ff, 8)
    first_copies = [
        pltpu.make_async_copy(q_rows, q_out, local.at[2]),
        pltpu.make_async_copy(rows, rows_out, local.at[3]),
        pltpu.make_async_copy(heads, heads_out, local.at[4]),
    ]
    for copy in first_copies:
        copy.start()

    def rest(slot):
        for phase, at in enumerate(ENTER_PLAN):
            if at == slot:
                for name in REST:
                    gathers[name].step(phase + 1)

    core = place.core
    doc_spans(starts, spans, 2 * half * groups)
    ahead = Forward(q_rows, window, spans, by_query, stats, weighted)
    rest(0)
    ahead.run(4, lambda n: (rem(n, 2), 4 + 2 * core + div(n, 2)))
    rest(1)
    near(0).wait_recv()
    ahead.run(4, lambda n: (rem(n, 2), 6 - 2 * core + div(n, 2)))
    rest(2)
    for at in range(4):
        side(0, at).wait_recv()
        side(1, at).wait_recv()
    near(1).start()
    rest(3)
    ahead.run(3, solo_tile(core))
    ahead.run(3, shared_tile(core))
    rest(4)
    near(1).wait_recv()
    ahead.run(4, lambda n: (rem(n, 2), 2 + 6 * core + div(n, 2)))
    ahead.finish(context, sums)
    rest(5)
    for gather in gathers.values():
        gather.finish()
    copies = [
        pltpu.make_async_copy(all2, all2_out, local.at[0]),
        pltpu.make_async_copy(all_ff2, ff2_out, local.at[1]),
    ]
    for copy in copies:
        copy.start()
    last = pltpu.make_async_copy(window, kv_out, local.at[5])
    last.start()
    for at in range(2):
        y_copies[at][0].wait_send()
        near(at).wait_send()
        for part in range(4):
            side(at, part).wait_send()
    for copy in plane_copies:
        copy.wait_send()
    for phase in range(2 if repeat == 1 else 0, 5):
        for mask in range(1 << phase):
            by_heads.copy(phase, mask, by_heads.own).wait_send()
    to_heads_drain(place, rows, row_send, row_recv)
    for copy in first_copies + copies + [last]:
        copy.wait()


VM = pl.BlockSpec(memory_space=pltpu.VMEM)
HBM = pl.BlockSpec(memory_space=pl.ANY)
SM = pl.BlockSpec(memory_space=pltpu.SMEM)
DMA = pltpu.SemaphoreType.DMA


ENTER_PLAN = (0, 2, 3, 4)


def enter(repeat, groups, starts, shard_qkv, shard2, shard_ff2, small, tokens):
    tok, dim = tokens.shape
    joined = shard2.shape[1]
    ff = shard_ff2.shape[0] * 32
    shape = jax.ShapeDtypeStruct
    vm = pltpu.VMEM
    return pl.pallas_call(
        functools.partial(enter_kernel, repeat, groups),
        out_shape=(
            shape((dim, joined), BF16), shape((ff, dim), BF16), shape((8, dim), F32), shape((8, ff), F32),
            shape((4 * tok, QW), BF16), shape((24 * tok, KW), BF16), shape((4 * tok, dim), BF16),
            shape((dim, PW), BF16), shape((4 * tok, QW), F32), shape((8, 4 * tok), F32), shape((8, 4 * tok), jnp.int32),
        ),
        in_specs=[SM] + [VM] * 5,
        out_specs=(HBM, HBM, VM, VM, HBM, HBM, HBM, HBM, VM, VM, VM),
        scratch_shapes=[
            vm((3, 4 * tok, 128), BF16), vm((4 * tok // QT, 8, QT), F32), vm((12 * tok // QT, 128, QT), F32),
            vm(shard2.shape, BF16), vm((dim, joined), BF16), vm((ff, dim), BF16),
            vm((4 * tok, QW), BF16), vm((24 * tok, KW), BF16), vm((4 * tok, dim), BF16),
            vm((CHIPS, shard2.shape[0], PW), BF16), vm((32, shard2.shape[0], PW), BF16), vm((dim, PW), BF16),
            DMA((4,)), DMA((3, 31)), DMA((3, 31)), DMA((31,)), DMA((31,)), DMA((4,)), DMA((4,)),
            DMA((4,)), DMA((4,)), DMA((2,)), DMA((2,)), DMA((2, 4)), DMA((2, 4)), DMA((6,)),
        ],
        compiler_params=pltpu.CompilerParams(
            collective_id=1, has_side_effects=True, vmem_limit_bytes=VMEM_BYTES
        ),
    )(starts, shard_qkv, shard2, shard_ff2, small, tokens)


def pack_small(norm_gains, norm_biases, proj_biases, ff_bias):
    rows = jnp.concatenate([norm_gains, norm_biases, proj_biases], axis=0)
    rows = jnp.pad(rows, ((0, 0), (0, 128 - rows.shape[1])))
    hidden = jnp.pad(ff_bias[None], ((0, 7), (0, PW - 128 - ff_bias.shape[0])))
    return jnp.concatenate([rows, hidden], axis=1)


QT = 512
KT = 512


def lane_mask(shape, low, high, axis):
    lane = lax.broadcasted_iota(jnp.int32, shape, axis)
    return (lane >= low) & (lane < high)


HEAD_QUERY = ((0, 0), (0, 64), (128, 0))
HEAD_VALUE = ((128, 64), (256, 0), (256, 64))
HEAD_CONTEXT = ((0, 64), (128, 0), (128, 64))


def head_rows(ref, rows, spot):
    tile, place = spot
    part = ref[rows, tile:tile + 128]
    return jnp.where(lane_mask(part.shape, place, place + HD, 1), part, jnp.zeros_like(part))


def doc_spans(starts, spans, total_rows):
    half = spans.shape[1]
    blk = lax.axis_index("blk")
    origin = (div(blk, GROUP) - 1) * 2 * half
    first = origin + (2 + rem(blk, 2)) * half
    far = jnp.int32(1 << 30)
    shape = (half // 128, 128)
    places = first + 128 * lax.broadcasted_iota(jnp.int32, shape, 0) + lax.broadcasted_iota(jnp.int32, shape, 1)

    def one(at, state):
        low, high, last = state
        start = starts[at]
        live = start < total_rows
        below = jnp.where(live, start, -far)
        above = jnp.where(live, start, far)
        low = jnp.where(below <= places, jnp.maximum(low, below), low)
        high = jnp.where(above > places, jnp.minimum(high, above), high)
        return low, high, jnp.maximum(last, below)

    low, high, last = lax.fori_loop(
        0, starts.shape[0], one, (jnp.full(shape, -far), jnp.full(shape, far), -far)
    )
    low = jnp.where(low == -far, last - total_rows, low) - origin
    high = jnp.where(high == far, starts[0] + total_rows, high) - origin
    spans[...] = jnp.zeros_like(spans)
    for at in range(shape[0]):
        spans[0:1, at * 128:(at + 1) * 128] = low[at:at + 1]
        spans[1:2, at * 128:(at + 1) * 128] = high[at:at + 1]


def meets(spans, columns, j):
    key = j * KT + lax.broadcasted_iota(jnp.int32, (KT, QT), 0)
    inside = (key >= spans[0:1, columns]) & (key < spans[1:2, columns])
    return jnp.where(inside, 0.0, NEGATIVE)


def solo_tile(core):
    def where(n):
        single = div(n, 2)
        return single * core + (1 - single) * n, single * (11 * core) + (1 - single) * (1 + 9 * core)

    return where


def shared_tile(core):
    def where(n):
        single = div(n, 2)
        return single * (1 - core) + (1 - single) * n, single * (9 - 7 * core) + (1 - single) * (8 - 5 * core)

    return where


class Forward:
    def __init__(self, queries, window, spans, by_query, stats, weighted):
        self.window, self.spans, self.by_query, self.stats, self.weighted = window, spans, by_query, stats, weighted
        scale = jnp.asarray(HD ** (-0.5), BF16)
        for head in range(3):
            by_query[head] = head_rows(queries, slice(None), HEAD_QUERY[head]) * scale
        stats[:, 0:3, :] = jnp.full(stats[:, 0:3, :].shape, NEGATIVE, F32)
        stats[:, 3:6, :] = jnp.zeros(stats[:, 3:6, :].shape, F32)
        weighted[...] = jnp.zeros_like(weighted)

    def visit(self, at, j):
        rows, columns, keys = rows_at(at * QT, QT), rows_at(at * QT, QT, 128), rows_at(j * KT, KT)
        bias = meets(self.spans, columns, j)
        heads = range(3)
        old = [self.stats[at, head:head + 1, :] for head in heads]
        scores = [
            nt(self.window[keys, tile:tile + 128], self.by_query[head, rows, :]) + bias
            for head, (tile, place) in enumerate(HEAD_QUERY)
        ]
        tops = [jnp.maximum(old[head], jnp.max(scores[head], axis=0, keepdims=True)) for head in heads]
        terms = [jnp.exp(scores[head] - tops[head]) for head in heads]
        for head in heads:
            tile = HEAD_VALUE[head][0]
            factor = jnp.exp(old[head] - tops[head])
            self.stats[at, head:head + 1, :] = tops[head]
            self.stats[at, 3 + head:4 + head, :] = (
                self.stats[at, 3 + head:4 + head, :] * factor + jnp.sum(terms[head], axis=0, keepdims=True)
            )
            self.weighted[3 * at + head] = self.weighted[3 * at + head] * factor + tn(
                self.window[keys, tile:tile + 128], terms[head].astype(BF16)
            )

    def run(self, count, where):
        def one(n, carry):
            self.visit(*where(n))
            return carry

        lax.fori_loop(0, count, one, 0)

    def finish(self, context, sums):
        sums[...] = jnp.zeros_like(sums)
        for at in range(context.shape[0] // QT):
            made = []
            rows = slice(at * QT, (at + 1) * QT)
            for head in range(3):
                total = self.stats[at, 3 + head:4 + head, :]
                whole = self.weighted[3 * at + head] / total
                place = HEAD_CONTEXT[head][1]
                made.append(jnp.where(lane_mask(whole.shape, place, place + HD, 0), whole, 0.0))
                sums[head:head + 1, rows] = self.stats[at, head:head + 1, :] + jnp.log(total)
            context[rows, 0:128] = made[0].T
            context[rows, 128:256] = (made[1] + made[2]).T


class Backward:
    def __init__(self, skip, queries, window, context, grads, sums, spans, by_query, by_grad, deltas, query_acc, acc):
        self.skip = skip
        self.window, self.sums, self.spans = window, sums, spans
        self.by_query, self.by_grad, self.deltas, self.query_acc, self.acc = by_query, by_grad, deltas, query_acc, acc
        scale = jnp.asarray(HD ** (-0.5), BF16)
        for head in range(3):
            every = slice(None)
            by_query[head] = head_rows(queries, every, HEAD_QUERY[head]) * scale
            mine = head_rows(grads, every, HEAD_CONTEXT[head])
            by_grad[head] = mine
            tile = HEAD_CONTEXT[head][0]
            product = mine.astype(F32) * context[:, tile:tile + 128]
            deltas[head:head + 1, :] = lax.dot_general(
                jnp.ones((8, 128), F32), product, (((1,), (1,)), ((), ())),
                precision=lax.Precision.HIGHEST, preferred_element_type=F32,
            )[0:1]
        acc[...] = jnp.zeros_like(acc)
        query_acc[...] = jnp.zeros_like(query_acc)

    def visit(self, at, j):
        rows, columns, keys = rows_at(at * QT, QT), rows_at(at * QT, QT, 128), rows_at(j * KT, KT)
        window, acc = self.window, self.acc.at[rows_at(j * KT - self.skip, KT)]
        bias = meets(self.spans, columns, j)
        key_grads, value_grads = [], []
        for head in range(3):
            key = window[keys, HEAD_QUERY[head][0]:HEAD_QUERY[head][0] + 128]
            value = window[keys, HEAD_VALUE[head][0]:HEAD_VALUE[head][0] + 128]
            query, grad = self.by_query[head, rows, :], self.by_grad[head, rows, :]
            probs = jnp.exp((nt(key, query) + bias) - self.sums[head:head + 1, columns])
            steps = (probs * (nt(value, grad) - self.deltas[head:head + 1, columns])).astype(BF16)
            value_grads.append(nn(probs.astype(BF16), grad))
            key_grads.append(nn(steps, query))
            self.query_acc[3 * at + head] += tn(key, steps)
        acc[:, 0:128] += key_grads[0] + key_grads[1]
        acc[:, 128:256] += key_grads[2] + value_grads[0]
        acc[:, 256:384] += value_grads[1] + value_grads[2]

    def run(self, count, where):
        def one(n, carry):
            self.visit(*where(n))
            return carry

        lax.fori_loop(0, count, one, 0)

    def query_rows(self, target):
        scale = HD ** (-0.5)
        for at in range(target.shape[0] // QT):
            made = []
            for head in range(3):
                place = HEAD_QUERY[head][1]
                mine = self.query_acc[3 * at + head]
                made.append(jnp.where(lane_mask(mine.shape, place, place + HD, 0), mine * scale, 0.0))
            rows = slice(at * QT, (at + 1) * QT)
            target[rows, 0:128] = (made[0] + made[1]).T.astype(BF16)
            target[rows, 128:256] = made[2].T.astype(BF16)


def norm_forward(values):
    center = values - jnp.mean(values, axis=-1, keepdims=True)
    scale = lax.rsqrt(jnp.mean(center * center, axis=-1, keepdims=True) + EPSILON)
    return center * scale, scale


def norm_backward(grad, unit_rows, scale, gain):
    inner = grad * gain
    gain_row = jnp.sum(grad * unit_rows, axis=0, keepdims=True)
    shift_row = jnp.sum(grad, axis=0, keepdims=True)
    back = scale * (
        inner
        - jnp.mean(inner, axis=-1, keepdims=True)
        - unit_rows * jnp.mean(inner * unit_rows, axis=-1, keepdims=True)
    )
    return back, gain_row, shift_row


def column_sum(values):
    return jnp.sum(values.astype(F32), axis=0, keepdims=True)


def middle_kernel(
    repeat, groups,
    context, tokens, d_out, params, ffb, all2, all_ff2,
    out, d_mid_out, grads_out, grad_o2, grad_ff2, sum_rows,
    w_out, w_ff1, w_ff2, ctx_rows, parts, pack, grad_rows, act, slope, d_pre,
    land_out, land_ff1, land_ff2,
    send, recv, back_send, back_recv, grad_send, grad_recv, local,
):
    place = Place(repeat, groups)
    tok, dim = tokens.shape
    ff = w_ff1.shape[1]
    scatters = {
        name: Scatter(place, grad_o2, dim // 16, first, width, RS_PLAN[name], True)
        for name, first, width in matrices(dim, ff)
    }
    scatters["ff2"] = Scatter(place, grad_ff2, ff // 16, 0, dim, RS_PLAN["ff2"], False)
    loads = [
        pltpu.make_async_copy(all2.at[:, pl.ds(0, dim)], w_out, local.at[0]),
        pltpu.make_async_copy(all2.at[:, pl.ds(dim, ff)], w_ff1, local.at[1]),
        pltpu.make_async_copy(all_ff2, w_ff2, local.at[2]),
    ]
    for load in loads:
        load.start()
    ctx_rows[...] = context[...].astype(BF16)
    place.greet(beside=False)
    to_tokens(place, ctx_rows, parts, send, recv)
    to_tokens_wait(place, ctx_rows, parts, send, recv)
    joined = jnp.concatenate([parts[chip][:, QW - HW:].astype(F32) for chip in range(CHIPS)], axis=1).astype(BF16)
    loads[0].wait()
    gains, shifts = [params[at:at + 1, :] for at in (0, 1)], [params[at:at + 1, :] for at in (2, 3)]
    mid = tokens[...].astype(F32) + (nn(joined, w_out[...]) + params[6:7, :])
    unit_first, scale_first = norm_forward(mid)
    hidden = unit_first * gains[0] + shifts[0]
    low = hidden.astype(BF16)
    loads[1].wait()
    loads[2].wait()
    ff_out = jnp.zeros((tok, dim), F32)
    for first in range(0, ff, dim):
        cut = slice(first, first + dim)
        pre = nn(low, w_ff1[:, cut]) + ffb[0:1, cut]
        bell = 0.5 * (1.0 + lax.erf(pre * 0.7071067811865476))
        made = (pre * bell).astype(BF16)
        act[:, cut] = made
        slope[:, cut] = bell + pre * jnp.exp(-0.5 * pre * pre) * 0.3989422804014327
        ff_out = ff_out + nn(made, w_ff2[cut, :])
    unit_second, scale_second = norm_forward(hidden + (ff_out + params[7:8, :]))
    out[...] = (unit_second * gains[1] + shifts[1]).astype(BF16)
    d_sum, gain_second, shift_second = norm_backward(d_out[...].astype(F32), unit_second, scale_second, gains[1])
    d_ff = d_sum.astype(BF16)
    for first in range(0, ff, dim):
        cut = slice(first, first + dim)
        grad_ff2[cut, :] = tn(act[:, cut], d_ff).astype(BF16)
    scatters["ff2"].begin(land_ff2, grad_send.at[2], grad_recv.at[2])
    d_hidden = d_sum
    for first in range(0, ff, dim):
        cut = slice(first, first + dim)
        made = (nt(d_ff, w_ff2[cut, :]) * slope[:, cut]).astype(BF16)
        d_pre[:, cut] = made
        d_hidden = d_hidden + nt(made, w_ff1[:, cut])
    d_mid, gain_first, shift_first = norm_backward(d_hidden, unit_first, scale_first, gains[0])
    d_mid_out[...] = d_mid
    d_attn = d_mid.astype(BF16)
    d_context = nt(d_attn, w_out[...])
    for chip in range(CHIPS):
        pack[chip] = jnp.concatenate(
            [jnp.zeros((tok, QW - HW), F32), d_context[:, HW * chip:HW * (chip + 1)]], axis=1
        ).astype(BF16)
    to_heads(place, pack, grad_rows, back_send, back_recv)
    for first in range(0, ff, dim):
        cut = slice(first, first + dim)
        grad_o2[:, dim + first:2 * dim + first] = tn(low, d_pre[:, cut]).astype(BF16)
        sum_rows[8 + first // dim:9 + first // dim, :] = column_sum(d_pre[:, cut])
    scatters["ff1"].begin(land_ff1, grad_send.at[1], grad_recv.at[1])
    grad_o2[:, 0:dim] = tn(joined, d_attn).astype(BF16)
    scatters["out"].begin(land_out, grad_send.at[0], grad_recv.at[0])
    for at, row in enumerate(
        (
            gain_first, gain_second, shift_first, shift_second,
            jnp.zeros((1, dim), F32), jnp.zeros((1, dim), F32), column_sum(d_attn), column_sum(d_ff),
        )
    ):
        sum_rows[at:at + 1, :] = row
    sum_rows[8 + ff // dim:, :] = jnp.zeros((8 - ff // dim, dim), F32)
    for name in REST:
        for j in range(16):
            scatters[name].absorb(0, j)
    to_heads_wait(place, grad_rows, back_send, back_recv)
    grads_out[...] = grad_rows[...]
    to_tokens_drain(place, ctx_rows, parts, send, recv)
    to_heads_drain(place, grad_rows, back_send, back_recv)
    for scatter in scatters.values():
        scatter.finish(1)


def middle(repeat, groups, context, tokens, d_out, params, ffb, all2, all_ff2):
    tok, dim = tokens.shape
    ff = all_ff2.shape[0]
    shape = jax.ShapeDtypeStruct
    vm = pltpu.VMEM
    return pl.pallas_call(
        functools.partial(middle_kernel, repeat, groups),
        out_shape=(
            shape((tok, dim), BF16), shape((tok, dim), F32), shape((4 * tok, QW), BF16),
            shape((dim, dim + ff), BF16), shape((ff, dim), BF16), shape((16, dim), F32),
        ),
        in_specs=[VM] * 5 + [HBM] * 2,
        out_specs=(VM,) * 6,
        scratch_shapes=[
            vm((dim, dim), BF16), vm((dim, ff), BF16), vm((ff, dim), BF16), vm((4 * tok, QW), BF16),
            vm((CHIPS, tok, QW), BF16), vm((CHIPS, tok, QW), BF16), vm((4 * tok, QW), BF16),
            vm((tok, ff), BF16), vm((tok, ff), F32), vm((tok, ff), BF16),
            vm((16, dim // 16, dim // 2), BF16), vm((16, dim // 16, ff // 2), BF16), vm((16, ff // 32, dim), BF16),
            DMA((4,)), DMA((4,)), DMA((4,)), DMA((4,)), DMA((3, 16)), DMA((3, 16)), DMA((4,)),
        ],
        compiler_params=pltpu.CompilerParams(collective_id=2, has_side_effects=True, vmem_limit_bytes=VMEM_BYTES),
    )(context, tokens, d_out, params, ffb, all2, all_ff2)


def leave_kernel(
    repeat, groups,
    queries, window, context, grads, sums, spans, rows, heads, d_mid, sum_rows, grad_o2, grad_ff2_in,
    d_tokens, g_qkv, g_out, g_ff1, g_ff2, g_rows,
    by_query, by_grad, deltas, query_acc, acc,
    grad2, grad_ff2, land_out, land_ff1, land_ff2, blocks, land_blocks, role_land,
    near_out, near_land, side_land, solo_out, joint, joined, partial, parts, swap_out, swap_in, rows_mine, rows_land,
    grad_send, grad_recv, block_send, block_recv, plane_send, plane_recv, near_send, near_recv, side_send, side_recv,
    part_send, part_recv, swap_send, swap_recv, rows_send, rows_recv, local,
):
    place = Place(repeat, groups)
    tok, dim = d_mid.shape
    ff = grad_ff2.shape[0]
    unit_rows = dim // 32
    half = 4 * tok
    role = 2 * place.x + place.y
    core = place.core
    loads = [
        pltpu.make_async_copy(grad_o2, grad2, local.at[0]),
        pltpu.make_async_copy(grad_ff2_in, grad_ff2, local.at[1]),
    ]
    for load in loads:
        load.start()
    place.greet()
    sibling = place.member(place.x, 1 - core, place.y)

    def near(at):
        return remote(near_out, near_land.at[at], near_send.at[at], near_recv.at[at], sibling)

    solo = remote(
        solo_out, side_land.at[core], side_send.at[core], side_recv.at[core], place.beside(2 * core - 1)
    )
    shared = remote(
        joint, side_land.at[1 - core], side_send.at[1 - core], side_recv.at[1 - core], place.beside(1 - 2 * core)
    )
    cuts = matrices(dim, ff)
    scatters = {
        name: Scatter(place, grad2, 2 * unit_rows, first, width, RS_PLAN[name], True) for name, first, width in cuts
    }
    scatters["ff2"] = Scatter(place, grad_ff2, ff // 16, 0, dim, RS_PLAN["ff2"], False)
    loads[0].wait()
    loads[1].wait()
    scatters["ff2"].begin(land_ff2, grad_send.at[2], grad_recv.at[2], 1)
    scatters["ff1"].begin(land_ff1, grad_send.at[1], grad_recv.at[1], 1)
    scatters["out"].begin(land_out, grad_send.at[0], grad_recv.at[0], 1)
    back = Backward(core * half, queries, window, context, grads, sums, spans, by_query, by_grad, deltas, query_acc, acc)

    def rest(slot):
        for stage, at in enumerate(LEAVE_PLAN):
            if at == slot:
                for name in REST:
                    scatters[name].stage(stage + 1)

    def made(slot, which):
        return acc[rows_at(2 * half * slot + half * which - half * core, half), :]


    back.run(3, solo_tile(core))
    solo_out[...] = made(2 * core, core).astype(BF16)
    solo.start()
    rest(0)
    back.run(4, lambda n: (rem(n, 2), 2 + 6 * core + div(n, 2)))
    near_out[...] = made(2 * core, 1 - core).astype(BF16)
    near(0).start()
    rest(1)
    back.run(3, shared_tile(core))
    near(0).wait_recv()
    joint[...] = (made(2 - 2 * core, core) + near_land[0].astype(F32)).astype(BF16)
    shared.start()
    rest(2)
    back.run(4, lambda n: (rem(n, 2), 6 - 2 * core + div(n, 2)))
    near(0).wait_send()
    near_out[...] = made(1, 1 - core).astype(BF16)
    near(1).start()
    rest(3)
    back.run(4, lambda n: (rem(n, 2), 4 + 2 * core + div(n, 2)))
    back.query_rows(joined)
    rest(4)
    near(1).wait_recv()
    own = made(1, core) + near_land[1].astype(F32)
    for at in range(2):
        remote(joint, side_land.at[at], side_send.at[at], side_recv.at[at], sibling).wait_recv()
    joined[:, QW:] = (own + side_land[0].astype(F32) + side_land[1].astype(F32)).astype(BF16)
    for at in range(4):
        part = slice(at * tok, (at + 1) * tok)
        partial[part, :] = nt(joined[part, :], heads[...]).astype(BF16)
    to_tokens(place, partial, parts, part_send, part_recv)
    whole = tn(rows[...], joined[...])
    for unit in range(32):
        block = whole[unit * unit_rows:(unit + 1) * unit_rows]
        pad = jnp.zeros((blocks.shape[1] - unit_rows, PW), F32)
        blocks[unit] = jnp.concatenate([block, pad], axis=0).astype(BF16)
    until = 3 if repeat == 1 else 5
    by_heads = ScatterBlocks(place, blocks, RS_HEADS, until)
    by_heads.begin(land_blocks, block_send, block_recv)
    rest(5)
    sums = column_sum(joined[...])
    rows_mine[0] = sum_rows[...]
    for row, first in ((4, 0), (5, PW - HW)):
        line = [jnp.where(role == chip, sums[:, first:first + HW], 0.0) for chip in range(CHIPS)]
        rows_mine[0, row:row + 1, :] = jnp.concatenate(line, axis=1)

    def rows_copy(phase):
        return remote(
            rows_mine.at[phase], rows_land.at[phase], rows_send.at[phase], rows_recv.at[phase],
            place.partner(RS_HEADS[phase]),
        )

    def rows_add(phase):
        rows_copy(phase).wait_recv()
        rows_mine[phase + 1] = rows_mine[phase] + rows_land[phase]
        if phase < 4:
            rows_copy(phase + 1).start()

    rows_copy(0).start()
    by_heads.step(0)
    rows_add(0)
    rest(6)
    by_heads.step(1)
    rows_add(1)
    rest(7)
    by_heads.step(2)
    rows_add(2)
    rest(8)

    def role_copy(dx, dy):
        chip, device = plane(place, dx, dy)
        at = 2 * dx + dy
        there = place.unit + dx * 4 * (1 - 2 * place.bit(2)) + dy * (1 - 2 * place.bit(0))
        return remote(blocks.at[there], role_land.at[role], plane_send.at[at], plane_recv.at[at], device)

    if repeat == 1:
        for dx, dy in ((1, 1), (1, 0), (0, 1)):
            role_copy(dx, dy).start()
    else:
        by_heads.step(3)
        by_heads.last()
        role_land[...] = jnp.zeros_like(role_land)
    role_land[role] = blocks[place.unit]
    rows_add(3)

    def swap(at):
        name, first, width = cuts[at]
        part = (slice(None), pl.ds(first // 2, width // 2))
        return remote(swap_out.at[part], swap_in.at[part], swap_send.at[at], swap_recv.at[at], place.partner(0))

    def finish_half(at):
        name, first, width = cuts[at]
        target = (g_out, g_ff1)[at]
        total = scatters[name].last()
        high = place.bit(0) == 1
        keep = jnp.where(high, total[unit_rows:], total[:unit_rows])
        give = jnp.where(high, total[:unit_rows], total[unit_rows:])
        pad = jnp.zeros((swap_out.shape[0] - unit_rows, give.shape[1]), F32)
        swap_out[:, first // 2:(first + width) // 2] = jnp.concatenate([give, pad], axis=0).astype(BF16)
        swap(at).start()
        target[:, rows_at(place.bit(0) * (width // 2), width // 2, 128)] = keep

    def finish_swap(at):
        name, first, width = cuts[at]
        target = (g_out, g_ff1)[at]
        swap(at).wait_recv()
        other = swap_in[:, first // 2:(first + width) // 2].astype(F32)[:unit_rows]
        target[:, rows_at((1 - place.bit(0)) * (width // 2), width // 2, 128)] = other

    for at in (1, 0):
        finish_half(at)
    g_ff2[...] = scatters["ff2"].last()
    rows_add(4)
    g_rows[...] = rows_mine[5]
    to_tokens_wait(place, partial, parts, part_send, part_recv)
    d_tokens[...] = (
        d_mid[...] + (parts[0].astype(F32) + parts[1].astype(F32)) + (parts[2].astype(F32) + parts[3].astype(F32))
    ).astype(BF16)
    for at in (1, 0):
        finish_swap(at)
    if repeat == 1:
        for dx, dy in ((1, 1), (1, 0), (0, 1)):
            role_copy(dx, dy).wait_recv()
    for part, first in ((0, 0), (1, QW), (2, QW + HW)):
        line = [role_land[chip][:unit_rows, first:first + HW].astype(F32) for chip in range(CHIPS)]
        g_qkv[:, part * dim:(part + 1) * dim] = jnp.concatenate(line, axis=1)
    for scatter in scatters.values():
        scatter.finish()
    by_heads.finish()
    if repeat == 1:
        for dx, dy in ((1, 1), (1, 0), (0, 1)):
            role_copy(dx, dy).wait_send()
    for at in range(2):
        swap(at).wait_send()
    near(1).wait_send()
    solo.wait_send()
    shared.wait_send()
    for phase in range(5):
        rows_copy(phase).wait_send()
    to_tokens_drain(place, partial, parts, part_send, part_recv)


LEAVE_PLAN = (3, 4, 7, 8)


def leave(repeat, groups, attention, rows, heads, d_mid, sum_rows, grad_o2, grad_ff2):
    tok, dim = d_mid.shape
    ff = grad_ff2.shape[0]
    unit = dim // 32
    slab = 2 * unit
    half = 4 * tok
    wide = -(-unit // 16) * 16
    shape = jax.ShapeDtypeStruct
    vm = pltpu.VMEM
    return pl.pallas_call(
        functools.partial(leave_kernel, repeat, groups),
        out_shape=(
            shape((tok, dim), BF16), shape((unit, 3 * dim), F32), shape((unit, dim), F32), shape((unit, ff), F32),
            shape((ff // 32, dim), F32), shape((16, dim), F32),
        ),
        in_specs=[VM] * 10 + [HBM] * 2,
        out_specs=(VM,) * 6,
        scratch_shapes=[
            vm((3, half, 128), BF16), vm((3, half, 128), BF16), vm((8, half), F32), vm((3 * half // QT, 128, QT), F32),
            vm((5 * half, KW), F32),
            vm((dim, dim + ff), BF16), vm((ff, dim), BF16),
            vm((15, slab, dim // 2), BF16), vm((15, slab, ff // 2), BF16), vm((15, ff // 32, dim), BF16),
            vm((32, wide, PW), BF16), vm((31, wide, PW), BF16), vm((CHIPS, wide, PW), BF16),
            vm((half, KW), BF16), vm((2, half, KW), BF16), vm((2, half, KW), BF16), vm((half, KW), BF16),
            vm((half, KW), BF16), vm((half, PW), BF16),
            vm((half, dim), BF16), vm((CHIPS, tok, dim), BF16),
            vm((wide, (dim + ff) // 2), BF16), vm((wide, (dim + ff) // 2), BF16),
            vm((6, 16, dim), F32), vm((5, 16, dim), F32),
            DMA((3, 31)), DMA((3, 31)), DMA((31,)), DMA((31,)), DMA((4,)), DMA((4,)), DMA((2,)), DMA((2,)), DMA((2,)),
            DMA((2,)), DMA((4,)), DMA((4,)), DMA((2,)), DMA((2,)), DMA((5,)), DMA((5,)), DMA((2,)),
        ],
        compiler_params=pltpu.CompilerParams(collective_id=3, has_side_effects=True, vmem_limit_bytes=VMEM_BYTES),
    )(*attention, rows, heads, d_mid, sum_rows, grad_o2, grad_ff2)


def settle_kernel(
    repeat, out, d_tokens, g_qkv, g_out, g_ff1, g_ff2, g_rows,
    out_r, d_tokens_r, g_qkv_r, g_out_r, g_ff1_r, g_ff2_r, gains_r, shifts_r, biases_r, hidden_r,
):
    for source, target in (
        (out, out_r), (d_tokens, d_tokens_r), (g_qkv, g_qkv_r), (g_out, g_out_r), (g_ff1, g_ff1_r), (g_ff2, g_ff2_r)
    ):
        target[...] = source[...]
    width = g_rows.shape[1]
    per, hidden = gains_r.shape[1], hidden_r.shape[1]
    unit = div(lax.axis_index("blk") * 2 + lax.axis_index("head"), repeat)
    turned = pltpu.roll(g_rows[0:8, :], rem(width - unit * per, width), 1)
    gains_r[...] = turned[0:2, :per]
    shifts_r[...] = turned[2:4, :per]
    biases_r[...] = turned[4:8, :per]
    lines = g_rows[8:16, :]
    row = lax.broadcasted_iota(jnp.int32, lines.shape, 0)
    mine = jnp.sum(jnp.where(row == div(unit * hidden, width), lines, 0.0), axis=0, keepdims=True)
    turned = pltpu.roll(jnp.broadcast_to(mine, lines.shape), rem(width - rem(unit * hidden, width), width), 1)
    hidden_r[...] = turned[0:1, :hidden]


def settle(repeat, results):
    shape = jax.ShapeDtypeStruct
    per, hidden = results[2].shape[0], results[5].shape[0]
    small = [shape((count, per), F32) for count in (2, 2, 4)] + [shape((1, hidden), F32)]
    return pl.pallas_call(
        functools.partial(settle_kernel, repeat),
        out_shape=[shape(value.shape, value.dtype) for value in results[:6]] + small,
        in_specs=[VM] * 7,
        out_specs=[VM] * 10,
        compiler_params=pltpu.CompilerParams(vmem_limit_bytes=VMEM_BYTES),
    )(*results)


def gather_repeat(value, repeat, axis):
    if repeat == 1:
        return value
    count = repeat // 2
    sets = [list(range(at, at + count)) for at in range(0, lax.axis_size("blk"), count)]
    value = lax.all_gather(value, "head", axis=axis, tiled=True)
    if count == 1:
        return value
    return lax.all_gather(value, "blk", axis=axis, tiled=True, axis_index_groups=sets)


def own_share(value, repeat, axis):
    if repeat == 1:
        return value
    count = repeat // 2
    sets = [list(range(at, at + count)) for at in range(0, lax.axis_size("blk"), count)]
    value = lax.psum(value, "head")
    if count > 1:
        value = lax.psum(value, "blk", axis_index_groups=sets)
    size = value.shape[axis] // repeat
    at = jnp.mod(lax.axis_index("blk") * 2 + lax.axis_index("head"), repeat)
    return lax.dynamic_slice_in_dim(value, at * size, size, axis)


def body(tokens, w_qkv, w_out, w_ff1, w_ff2, norm_gains, norm_biases, proj_biases, ff_bias, doc_starts, d_out):
    blks = lax.axis_size("blk")
    repeat = blks * 2 // 32
    groups = blks // GROUP
    tok, dim = tokens.shape
    shard_qkv = gather_repeat(w_qkv, repeat, 0)
    shard2 = gather_repeat(jnp.concatenate([w_out, w_ff1], axis=1), repeat, 0)
    shard2 = jnp.pad(shard2, ((0, -shard2.shape[0] % 16), (0, 0)))
    shard_ff2 = gather_repeat(w_ff2, repeat, 0)
    small = pack_small(
        gather_repeat(norm_gains, repeat, 1), gather_repeat(norm_biases, repeat, 1),
        gather_repeat(proj_biases, repeat, 1), gather_repeat(ff_bias, repeat, 0),
    )
    all2, all_ff2, params, ffb, queries, window, rows, heads, context, sums, spans = enter(
        repeat, groups, doc_starts, shard_qkv, shard2, shard_ff2, small, tokens
    )
    out, d_mid, grads, grad_o2, grad_ff2, sum_rows = middle(
        repeat, groups, context, tokens, d_out, params, ffb, all2, all_ff2
    )
    d_tokens, g_qkv, g_out, g_ff1, g_ff2, g_rows = leave(
        repeat, groups, (queries, window, context, grads, sums, spans), rows, heads, d_mid, sum_rows, grad_o2, grad_ff2
    )
    results = settle(repeat, (out, d_tokens, g_qkv, g_out, g_ff1, g_ff2, g_rows))
    axes = (None, None, 0, 0, 0, 0, 1, 1, 1, 0)
    results = list(results[:9]) + [results[9].reshape(-1)]
    return tuple(
        value if axis is None else own_share(value, repeat, axis) for value, axis in zip(results, axes)
    )


def solution(mesh):
    rows, columns, flat = P(("blk", "head"), None), P(None, ("blk", "head")), P(("blk", "head"))
    return jax.shard_map(
        body,
        mesh=mesh,
        in_specs=(rows,) * 5 + (columns,) * 3 + (flat, P(), rows),
        out_specs=(rows,) * 6 + (columns,) * 3 + (flat,),
        check_vma=False,
    )
```

```python
import functools

import jax
import jax.numpy as jnp
from jax import lax
from jax.experimental import pallas as pl
from jax.experimental.pallas import tpu as pltpu
from jax.sharding import PartitionSpec as P

H = 12
HD = 64
DOC_MOST = 2048
EPSILON = 1e-06
NEGATIVE = -1e30
MESH = pl.DeviceIdType.MESH
F32 = jnp.float32
BF16 = jnp.bfloat16
VMEM_BYTES = 62 * 1024 * 1024
CHIPS = 4
GROUP = 4
QW = 256
KW = 384
HW = (H // CHIPS) * HD
PW = QW + KW


def div(a, b):
    return lax.div(a, jnp.int32(b))


def rem(a, b):
    return lax.rem(a, jnp.int32(b))


def nn(a, b):
    return lax.dot_general(a, b, (((1,), (0,)), ((), ())), preferred_element_type=F32)


def nt(a, b):
    return lax.dot_general(a, b, (((1,), (1,)), ((), ())), preferred_element_type=F32)


def tn(a, b):
    return lax.dot_general(a, b, (((0,), (0,)), ((), ())), preferred_element_type=F32)


def rows_at(start, count, unit=16):
    return pl.ds(pl.multiple_of(start, unit), count)


class Place:
    def __init__(self, repeat, groups):
        self.repeat = repeat
        blk, head = lax.axis_index("blk"), lax.axis_index("head")
        self.index = blk * 2 + head
        self.unit = div(self.index, repeat)
        self.core, self.x, self.y = rem(blk, 2), rem(div(blk, 2), 2), head
        self.group, self.groups = div(blk, GROUP), groups
        self.bits = [rem(div(self.unit, 1 << k), 2) for k in range(5)]
        others = [self.index + (1 - 2 * self.bits[k]) * (repeat << k) for k in range(5)]
        self.partners = [{"blk": div(other, 2), "head": rem(other, 2)} for other in others]

    def bit(self, k):
        return self.bits[k]

    def partner(self, k):
        return self.partners[k]

    def member(self, x, core, y):
        return {"blk": self.group * GROUP + 2 * x + core, "head": y}

    def beside(self, step):
        group = rem(self.group + self.groups + step, self.groups)
        return {"blk": group * GROUP + 2 * self.x + self.core, "head": self.y}

    def greet(self, cube=True, group=True, beside=True):
        barrier = pltpu.get_barrier_semaphore()
        partners = []
        if cube:
            partners += [self.partner(k) for k in range(5)]
        if group:
            partners += [
                self.member(
                    rem(self.x + dx, 2), rem(self.core + dc, 2), rem(self.y + dy, 2)
                )
                for dx in range(2)
                for dc in range(2)
                for dy in range(2)
                if dx + dc + dy
            ]
        if beside:
            partners += [self.beside(1), self.beside(-1)]
        for partner in partners:
            pl.semaphore_signal(barrier, inc=1, device_id=partner, device_id_type=MESH)
        pl.semaphore_wait(barrier, len(partners))


def remote(src, dst, send, recv, device):
    return pltpu.make_async_remote_copy(
        src_ref=src, dst_ref=dst, send_sem=send, recv_sem=recv, device_id=device, device_id_type=MESH
    )


class Pieces:
    def __init__(self, place, ref, rows, first, width, order, by_columns):
        self.place, self.ref, self.rows, self.first, self.width = place, ref, rows, first, width
        self.order, self.by_columns = order, by_columns
        if by_columns is not None:
            self.shape = (rows, width // 2) if by_columns else (rows // 2, width)
        self.deltas = [(1 - 2 * place.bit(k)) * (1 << k) for k in order]
        self.units = {0: place.unit}
        self.own = self.piece(0)

    def unit_of(self, mask):
        if mask not in self.units:
            at = mask.bit_length() - 1
            self.units[mask] = self.unit_of(mask - (1 << at)) + self.deltas[at]
        return self.units[mask]

    def region(self, unit):
        slab, half = div(unit, 2), rem(unit, 2)
        if self.by_columns:
            return (
                rows_at(slab * self.rows, self.rows),
                rows_at(self.first + half * self.shape[1], self.shape[1], 128),
            )
        return (rows_at(unit * self.shape[0], self.shape[0]), pl.ds(self.first, self.width))

    def piece(self, mask):
        return self.ref.at[self.region(self.unit_of(mask))]


class Gather(Pieces):
    def begin(self, send, recv, until=5):
        self.send, self.recv = send, recv
        self.feed(0, 0, until)

    def copy(self, phase, mask, ref):
        at = (1 << phase) - 1 + mask
        return remote(ref, ref, self.send.at[at], self.recv.at[at], self.place.partner(self.order[phase]))

    def feed(self, mask, phase, until=5):
        if phase < until:
            ref = self.piece(mask)
            for later in range(phase, until):
                self.copy(later, mask, ref).start()

    def release(self, phase):
        for mask in range(1 << phase):
            self.feed(mask, phase)

    def step(self, phase, until=5):
        for mask in range(1 << phase):
            self.copy(phase, mask, self.own).wait_recv()
            self.feed(mask + (1 << phase), phase + 1, until)

    def finish(self):
        for phase in range(5):
            for mask in range(1 << phase):
                self.copy(phase, mask, self.own).wait_send()


def soonest(count):
    return sorted(range(count), key=lambda j: (j & -j) if j else count)


class Scatter(Pieces):
    def begin(self, landing, send, recv, since=0):
        self.landing, self.send, self.recv, self.since = landing, send, recv, since
        for j in soonest(16 >> since):
            self.give(since, j)

    def slot(self, phase, j):
        return (32 >> self.since) - (1 << (5 - phase)) + j

    def copy(self, phase, j, ref):
        at = self.slot(phase, j)
        return remote(
            ref, self.landing.at[at], self.send.at[at], self.recv.at[at], self.place.partner(self.order[phase])
        )

    def give(self, phase, j):
        self.copy(phase, j, self.piece((2 * j + 1) * (1 << phase))).start()

    def absorb(self, phase, j):
        self.copy(phase, j, self.own).wait_recv()
        rows, columns = self.region(self.unit_of(j * (2 << phase)))
        if phase == 4:
            return self.ref[rows, columns].astype(F32) + self.landing[self.slot(phase, j)].astype(F32)
        self.ref[rows, columns] = self.ref[rows, columns] + self.landing[self.slot(phase, j)]

    def step(self, phase):
        half = 1 << (3 - phase)
        for jj in soonest(half):
            self.absorb(phase, 2 * jj + 1)
            self.give(phase + 1, jj)
        for jj in soonest(half):
            self.absorb(phase, 2 * jj)

    def stage(self, at):
        for j in soonest(1 << (4 - at)):
            if at < 4 and j % 2 == 0:
                continue
            for phase in range(1, at + 1):
                if phase < 4:
                    self.absorb(phase, j << (at - phase))
            if at < 4:
                self.give(at + 1, j >> 1)

    def last(self):
        return self.absorb(4, 0)

    def finish(self, until=5):
        for phase in range(self.since, until):
            for j in range(1 << (4 - phase)):
                self.copy(phase, j, self.own).wait_send()


class GatherBlocks(Gather):
    def __init__(self, place, ref, order):
        self.shape = ref.shape[1:]
        Pieces.__init__(self, place, ref, 0, 0, 0, order, None)

    def piece(self, mask):
        return self.ref.at[self.unit_of(mask)]


class ScatterBlocks(Scatter):
    def __init__(self, place, ref, order, until):
        Pieces.__init__(self, place, ref, 0, 0, 0, order, None)
        self.until = until

    def piece(self, mask):
        return self.ref.at[self.unit_of(mask)]

    def give(self, phase, j):
        if phase < self.until:
            Scatter.give(self, phase, j)

    def absorb(self, phase, j):
        self.copy(phase, j, self.own).wait_recv()
        unit = self.unit_of(j * (2 << phase))
        self.ref[unit] = self.ref[unit] + self.landing[self.slot(phase, j)]

    def finish(self):
        for phase in range(self.until):
            for j in range(1 << (4 - phase)):
                self.copy(phase, j, self.own).wait_send()


def to_heads(place, packed, landed, send, recv, part=None):
    tok = packed.shape[1] if part is None else part.shape[0]
    mine = rows_at(2 * tok * place.core + tok * place.y, tok)
    slot = 2 * place.core + place.y
    alone = place.core == place.x
    for dx, dy in ((0, 0), (1, 0), (0, 1), (1, 1)):
        if True:
            tx, ty = rem(place.x + dx, 2), rem(place.y + dy, 2)
            copy = remote(
                packed.at[2 * tx + ty] if part is None else part,
                landed.at[mine],
                send.at[2 * dx + dy],
                recv.at[slot],
                place.member(tx, place.x, ty),
            )
            if dx + dy:
                copy.start()
            else:
                pl.when(jnp.logical_not(alone))(copy.start)

                @pl.when(alone)
                def _(tx=tx, ty=ty):
                    landed[mine] = packed[2 * tx + ty] if part is None else part[...]


def to_heads_wait_one(place, landed, send, recv, cs, ys):
    tok = landed.shape[0] // 4
    part = landed.at[pl.ds(0, tok)]
    copy = remote(part, part, send.at[0], recv.at[2 * cs + ys], place.member(place.x, 1 - place.core, place.y))
    own = (place.core == place.x) & (place.core == cs) & (place.y == ys)
    pl.when(jnp.logical_not(own))(copy.wait_recv)


def to_heads_wait(place, landed, send, recv):
    for cs in range(2):
        for ys in range(2):
            to_heads_wait_one(place, landed, send, recv, cs, ys)


def to_heads_drain(place, landed, send, recv):
    part = landed.at[pl.ds(0, landed.shape[0] // 4)]
    for at in range(4):
        copy = remote(part, part, send.at[at], recv.at[0], place.member(place.x, 1 - place.core, place.y))
        if at:
            copy.wait_send()
        else:
            pl.when(place.core != place.x)(copy.wait_send)


def to_tokens(place, rows, landed, send, recv):
    tok = landed.shape[1]
    chip = 2 * place.x + place.y
    for cs in range(2):
        for ys in range(2):
            part = pl.ds(2 * tok * cs + tok * ys, tok)
            own = (place.core == place.x) & (place.core == cs) & (place.y == ys)
            copy = remote(
                rows.at[part], landed.at[chip], send.at[2 * cs + ys], recv.at[chip], place.member(place.core, cs, ys)
            )
            pl.when(jnp.logical_not(own))(copy.start)

            @pl.when(own)
            def _(part=part):
                landed[chip] = rows[part]


def to_tokens_wait(place, rows, landed, send, recv):
    for xs in range(2):
        for ys in range(2):
            at = 2 * xs + ys
            own = (place.core == place.x) & (place.x == xs) & (place.y == ys)
            copy = remote(
                landed.at[at], landed.at[at], send.at[at], recv.at[at], place.member(place.x, 1 - place.core, place.y)
            )
            pl.when(jnp.logical_not(own))(copy.wait_recv)


def to_tokens_drain(place, rows, landed, send, recv):
    for cs in range(2):
        for ys in range(2):
            own = (place.core == place.x) & (place.core == cs) & (place.y == ys)
            at = 2 * cs + ys
            copy = remote(
                landed.at[at], landed.at[at], send.at[at], recv.at[at], place.member(place.x, 1 - place.core, place.y)
            )
            pl.when(jnp.logical_not(own))(copy.wait_send)


def spread_rows(small, per, width, rows):
    lane = lax.broadcasted_iota(jnp.int32, (128, width), 1).astype(F32)
    spot = lane - per * jnp.floor((lane + 0.5) * (1.0 / per))
    pick = (spot == lax.broadcasted_iota(jnp.int32, (128, width), 0).astype(F32)).astype(BF16)
    wide = nn(small.astype(BF16), pick).reshape(32, rows, width)
    low = lax.broadcasted_iota(jnp.int32, wide.shape, 0) * per
    column = lax.broadcasted_iota(jnp.int32, wide.shape, 2)
    return jnp.sum(jnp.where((column >= low) & (column < low + per), wide, 0.0), axis=0)


AG_PLAN = dict(out=(4, 3, 0, 2, 1), ff1=(4, 3, 0, 2, 1), ff2=(4, 3, 2, 0, 1))
AG_HEADS = (2, 0, 4, 3, 1)
RS_PLAN = dict(out=(1, 2, 0, 3, 4), ff1=(1, 2, 0, 3, 4), ff2=(1, 0, 2, 3, 4))
RS_HEADS = (1, 3, 4, 2, 0)
REST = ("ff2", "ff1", "out")


def matrices(dim, ff):
    return (("out", 0, dim), ("ff1", dim, ff))


def plane(place, dx, dy):
    tx, ty = rem(place.x + dx, 2), rem(place.y + dy, 2)
    return 2 * tx + ty, place.member(tx, place.core, ty)


def enter_kernel(
    repeat, groups,
    starts, shard_qkv, shard2, shard_ff2, small, tokens,
    all2_out, ff2_out, params_out, ffb_out, q_out, kv_out, rows_out, heads_out, context, sums, spans,
    by_query, stats, weighted, stage, all2, all_ff2, q_rows, window, rows, pack_w, blocks, heads,
    y_sems, gather_send, gather_recv, block_send, block_recv, plane_send, plane_recv,
    row_send, row_recv, near_send, near_recv, side_send, side_recv, local,
):
    place = Place(repeat, groups)
    dim = all2.shape[0]
    ff = all_ff2.shape[0]
    tok = tokens.shape[0]
    unit_rows = dim // 32
    slab = 2 * unit_rows
    half = 4 * tok
    own_ff2 = pltpu.make_async_copy(
        shard_ff2, all_ff2.at[rows_at(place.unit * (ff // 32), ff // 32)], local.at[0]
    )
    own_ff2.start()
    wide = shard_qkv[...].astype(F32)
    for chip in range(CHIPS):
        cut = [wide[:, part * dim + HW * chip:part * dim + HW * (chip + 1)] for part in range(3)]
        block = jnp.concatenate([cut[0], jnp.zeros((unit_rows, QW - HW), F32), cut[1], cut[2]], axis=1)
        pack_w[chip] = jnp.concatenate([block, small[...].astype(F32)], axis=0).astype(BF16)
    role = 2 * place.x + place.y
    blocks[place.unit] = pack_w[role]
    place.greet()
    plane_copies = []
    if repeat == 1:
        for dx, dy in ((1, 1), (1, 0), (0, 1)):
            chip, device = plane(place, dx, dy)
            at = 2 * dx + dy
            copy = remote(pack_w.at[chip], blocks.at[place.unit], plane_send.at[at], plane_recv.at[at], device)
            copy.start()
            plane_copies.append(copy)
    to_heads(place, None, rows, row_send, row_recv, tokens)
    cuts = matrices(dim, ff)
    y_copies = []

    def half_columns(at, which):
        name, first, width = cuts[at]
        return (slice(None), rows_at(first + which * (width // 2), width // 2, 128))

    for at in range(2):
        mine, other = half_columns(at, place.bit(0)), half_columns(at, 1 - place.bit(0))
        out = remote(shard2.at[other], stage.at[other], y_sems.at[at], y_sems.at[2 + at], place.partner(0))
        back = remote(shard2.at[mine], stage.at[mine], y_sems.at[at], y_sems.at[2 + at], place.partner(0))
        out.start()
        y_copies.append((out, back))

    by_heads = GatherBlocks(place, blocks, AG_HEADS)
    gathers = {name: Gather(place, all2, slab, first, width, AG_PLAN[name], True) for name, first, width in cuts}
    gathers["ff2"] = Gather(place, all_ff2, ff // 16, 0, dim, AG_PLAN["ff2"], False)
    here = rows_at(div(place.unit, 2) * slab, slab)

    def merge(at):
        y_copies[at][1].wait_recv()
        name, first, width = cuts[at]
        low = place.bit(0) == 0
        for column in range(0, width // 2, 256):
            size = min(256, width // 2 - column)
            part = rows_at(first + place.bit(0) * (width // 2) + column, size, 128)
            mine, other = shard2[:unit_rows, part].astype(F32), stage[:unit_rows, part].astype(F32)
            whole = jnp.concatenate([jnp.where(low, mine, other), jnp.where(low, other, mine)], axis=0)
            all2[here, part] = whole.astype(BF16)
        gathers[name].begin(gather_send.at[at], gather_recv.at[at])

    by_heads.send, by_heads.recv = block_send, block_recv
    if repeat == 1:
        for copy in plane_copies:
            copy.wait_recv()
        by_heads.release(2)
    else:
        by_heads.feed(0, 0)
        by_heads.step(0)
        by_heads.step(1)
    own_ff2.wait()
    by_heads.step(2)
    gathers["ff2"].begin(gather_send.at[2], gather_recv.at[2])
    merge(1)
    merge(0)
    by_heads.step(3)
    for name in REST:
        gathers[name].step(0)
    by_heads.step(4)

    def compact(pair, carry):
        whole = jnp.concatenate(
            [blocks[2 * pair][:unit_rows].astype(F32), blocks[2 * pair + 1][:unit_rows].astype(F32)], axis=0
        )
        heads[rows_at(pair * slab, slab)] = whole.astype(BF16)
        return carry

    lax.fori_loop(0, 16, compact, 0)
    params_out[...] = spread_rows(blocks[:, unit_rows:, 0:128].astype(F32).reshape(-1, 128), unit_rows, dim, 8)
    bias = jnp.zeros((2, PW), F32)
    for chip in range(CHIPS):
        cut = params_out[4:6, HW * chip:HW * (chip + 1)]
        query = jnp.concatenate([cut[0:1], jnp.zeros((1, PW - HW), F32)], axis=1)
        value = jnp.concatenate([jnp.zeros((1, PW - HW), F32), cut[1:2]], axis=1)
        bias = jnp.where(role == chip, query + value, bias)
    sibling = place.member(place.x, 1 - place.core, place.y)

    def stretch(slot, core):
        return window.at[rows_at(half * (2 * slot + core), half)]

    def part_of(slot, at):
        return window.at[rows_at(half * (2 * slot + place.core) + tok * at, tok)]

    def side(to, at):
        return remote(
            part_of(1, at), part_of(2 * to, at), side_send.at[to, at], side_recv.at[to, at], place.beside(1 - 2 * to)
        )

    def near(at):
        ref = stretch(1, place.core) if at == 0 else stretch(2 - 2 * place.core, place.core)
        return remote(ref, ref, near_send.at[at], near_recv.at[at], sibling)

    for ys in (place.y, 1 - place.y):
        for cs in range(2):
            to_heads_wait_one(place, rows, row_send, row_recv, cs, ys)
            at = 2 * cs + ys
            part = rows_at(at * tok, tok)
            made = nn(rows[part, :], heads[...]) + bias[0:1]
            window[rows_at(half * (2 + place.core) + at * tok, tok)] = made[:, QW:].astype(BF16)
            side(0, at).start()
            side(1, at).start()
            q_rows[part, :] = made[:, :QW].astype(BF16)
    near(0).start()
    hidden = blocks[:, unit_rows:, 128:256].astype(F32).reshape(-1, 128)
    ffb_out[...] = spread_rows(hidden, ff // 32, ff, 8)
    first_copies = [
        pltpu.make_async_copy(q_rows, q_out, local.at[2]),
        pltpu.make_async_copy(rows, rows_out, local.at[3]),
        pltpu.make_async_copy(heads, heads_out, local.at[4]),
    ]
    for copy in first_copies:
        copy.start()

    def rest(slot):
        for phase, at in enumerate(ENTER_PLAN):
            if at == slot:
                for name in REST:
                    gathers[name].step(phase + 1)

    core = place.core
    doc_spans(starts, spans, 2 * half * groups)
    ahead = Forward(q_rows, window, spans, by_query, stats, weighted)
    rest(0)
    ahead.run(4, lambda n: (rem(n, 2), 4 + 2 * core + div(n, 2)))
    rest(1)
    near(0).wait_recv()
    ahead.run(4, lambda n: (rem(n, 2), 6 - 2 * core + div(n, 2)))
    rest(2)
    for at in range(4):
        side(0, at).wait_recv()
        side(1, at).wait_recv()
    near(1).start()
    rest(3)
    ahead.run(3, solo_tile(core))
    ahead.run(3, shared_tile(core))
    rest(4)
    near(1).wait_recv()
    ahead.run(4, lambda n: (rem(n, 2), 2 + 6 * core + div(n, 2)))
    ahead.finish(context, sums)
    rest(5)
    for gather in gathers.values():
        gather.finish()
    copies = [
        pltpu.make_async_copy(all2, all2_out, local.at[0]),
        pltpu.make_async_copy(all_ff2, ff2_out, local.at[1]),
    ]
    for copy in copies:
        copy.start()
    last = pltpu.make_async_copy(window, kv_out, local.at[5])
    last.start()
    for at in range(2):
        y_copies[at][0].wait_send()
        near(at).wait_send()
        for part in range(4):
            side(at, part).wait_send()
    for copy in plane_copies:
        copy.wait_send()
    for phase in range(2 if repeat == 1 else 0, 5):
        for mask in range(1 << phase):
            by_heads.copy(phase, mask, by_heads.own).wait_send()
    to_heads_drain(place, rows, row_send, row_recv)
    for copy in first_copies + copies + [last]:
        copy.wait()


VM = pl.BlockSpec(memory_space=pltpu.VMEM)
HBM = pl.BlockSpec(memory_space=pl.ANY)
SM = pl.BlockSpec(memory_space=pltpu.SMEM)
DMA = pltpu.SemaphoreType.DMA


ENTER_PLAN = (0, 2, 3, 4)


def enter(repeat, groups, starts, shard_qkv, shard2, shard_ff2, small, tokens):
    tok, dim = tokens.shape
    joined = shard2.shape[1]
    ff = shard_ff2.shape[0] * 32
    shape = jax.ShapeDtypeStruct
    vm = pltpu.VMEM
    return pl.pallas_call(
        functools.partial(enter_kernel, repeat, groups),
        out_shape=(
            shape((dim, joined), BF16), shape((ff, dim), BF16), shape((8, dim), F32), shape((8, ff), F32),
            shape((4 * tok, QW), BF16), shape((24 * tok, KW), BF16), shape((4 * tok, dim), BF16),
            shape((dim, PW), BF16), shape((4 * tok, QW), F32), shape((8, 4 * tok), F32), shape((8, 4 * tok), jnp.int32),
        ),
        in_specs=[SM] + [VM] * 5,
        out_specs=(HBM, HBM, VM, VM, HBM, HBM, HBM, HBM, VM, VM, VM),
        scratch_shapes=[
            vm((3, 4 * tok, 128), BF16), vm((4 * tok // QT, 8, QT), F32), vm((12 * tok // QT, 128, QT), F32),
            vm(shard2.shape, BF16), vm((dim, joined), BF16), vm((ff, dim), BF16),
            vm((4 * tok, QW), BF16), vm((24 * tok, KW), BF16), vm((4 * tok, dim), BF16),
            vm((CHIPS, shard2.shape[0], PW), BF16), vm((32, shard2.shape[0], PW), BF16), vm((dim, PW), BF16),
            DMA((4,)), DMA((3, 31)), DMA((3, 31)), DMA((31,)), DMA((31,)), DMA((4,)), DMA((4,)),
            DMA((4,)), DMA((4,)), DMA((2,)), DMA((2,)), DMA((2, 4)), DMA((2, 4)), DMA((6,)),
        ],
        compiler_params=pltpu.CompilerParams(
            collective_id=1, has_side_effects=True, vmem_limit_bytes=VMEM_BYTES
        ),
    )(starts, shard_qkv, shard2, shard_ff2, small, tokens)


def pack_small(norm_gains, norm_biases, proj_biases, ff_bias):
    rows = jnp.concatenate([norm_gains, norm_biases, proj_biases], axis=0)
    rows = jnp.pad(rows, ((0, 0), (0, 128 - rows.shape[1])))
    hidden = jnp.pad(ff_bias[None], ((0, 7), (0, PW - 128 - ff_bias.shape[0])))
    return jnp.concatenate([rows, hidden], axis=1)


QT = 512
KT = 512


def lane_mask(shape, low, high, axis):
    lane = lax.broadcasted_iota(jnp.int32, shape, axis)
    return (lane >= low) & (lane < high)


HEAD_QUERY = ((0, 0), (0, 64), (128, 0))
HEAD_VALUE = ((128, 64), (256, 0), (256, 64))
HEAD_CONTEXT = ((0, 64), (128, 0), (128, 64))


def head_rows(ref, rows, spot):
    tile, place = spot
    part = ref[rows, tile:tile + 128]
    return jnp.where(lane_mask(part.shape, place, place + HD, 1), part, jnp.zeros_like(part))


def doc_spans(starts, spans, total_rows):
    half = spans.shape[1]
    blk = lax.axis_index("blk")
    origin = (div(blk, GROUP) - 1) * 2 * half
    first = origin + (2 + rem(blk, 2)) * half
    far = jnp.int32(1 << 30)
    shape = (half // 128, 128)
    places = first + 128 * lax.broadcasted_iota(jnp.int32, shape, 0) + lax.broadcasted_iota(jnp.int32, shape, 1)

    def one(at, state):
        low, high, last = state
        start = starts[at]
        live = start < total_rows
        below = jnp.where(live, start, -far)
        above = jnp.where(live, start, far)
        low = jnp.where(below <= places, jnp.maximum(low, below), low)
        high = jnp.where(above > places, jnp.minimum(high, above), high)
        return low, high, jnp.maximum(last, below)

    low, high, last = lax.fori_loop(
        0, starts.shape[0], one, (jnp.full(shape, -far), jnp.full(shape, far), -far)
    )
    low = jnp.where(low == -far, last - total_rows, low) - origin
    high = jnp.where(high == far, starts[0] + total_rows, high) - origin
    spans[...] = jnp.zeros_like(spans)
    for at in range(shape[0]):
        spans[0:1, at * 128:(at + 1) * 128] = low[at:at + 1]
        spans[1:2, at * 128:(at + 1) * 128] = high[at:at + 1]


def meets(spans, columns, j):
    key = j * KT + lax.broadcasted_iota(jnp.int32, (KT, QT), 0)
    inside = (key >= spans[0:1, columns]) & (key < spans[1:2, columns])
    return jnp.where(inside, 0.0, NEGATIVE)


def solo_tile(core):
    def where(n):
        single = div(n, 2)
        return single * core + (1 - single) * n, single * (11 * core) + (1 - single) * (1 + 9 * core)

    return where


def shared_tile(core):
    def where(n):
        single = div(n, 2)
        return single * (1 - core) + (1 - single) * n, single * (9 - 7 * core) + (1 - single) * (8 - 5 * core)

    return where


class Forward:
    def __init__(self, queries, window, spans, by_query, stats, weighted):
        self.window, self.spans, self.by_query, self.stats, self.weighted = window, spans, by_query, stats, weighted
        scale = jnp.asarray(HD ** (-0.5), BF16)
        for head in range(3):
            by_query[head] = head_rows(queries, slice(None), HEAD_QUERY[head]) * scale
        stats[:, 0:3, :] = jnp.full(stats[:, 0:3, :].shape, NEGATIVE, F32)
        stats[:, 3:6, :] = jnp.zeros(stats[:, 3:6, :].shape, F32)
        weighted[...] = jnp.zeros_like(weighted)

    def visit(self, at, j):
        rows, columns, keys = rows_at(at * QT, QT), rows_at(at * QT, QT, 128), rows_at(j * KT, KT)
        bias = meets(self.spans, columns, j)
        heads = range(3)
        old = [self.stats[at, head:head + 1, :] for head in heads]
        scores = [
            nt(self.window[keys, tile:tile + 128], self.by_query[head, rows, :]) + bias
            for head, (tile, place) in enumerate(HEAD_QUERY)
        ]
        tops = [jnp.maximum(old[head], jnp.max(scores[head], axis=0, keepdims=True)) for head in heads]
        terms = [jnp.exp(scores[head] - tops[head]) for head in heads]
        for head in heads:
            tile = HEAD_VALUE[head][0]
            factor = jnp.exp(old[head] - tops[head])
            self.stats[at, head:head + 1, :] = tops[head]
            self.stats[at, 3 + head:4 + head, :] = (
                self.stats[at, 3 + head:4 + head, :] * factor + jnp.sum(terms[head], axis=0, keepdims=True)
            )
            self.weighted[3 * at + head] = self.weighted[3 * at + head] * factor + tn(
                self.window[keys, tile:tile + 128], terms[head].astype(BF16)
            )

    def run(self, count, where):
        def one(n, carry):
            self.visit(*where(n))
            return carry

        lax.fori_loop(0, count, one, 0)

    def finish(self, context, sums):
        sums[...] = jnp.zeros_like(sums)
        for at in range(context.shape[0] // QT):
            made = []
            rows = slice(at * QT, (at + 1) * QT)
            for head in range(3):
                total = self.stats[at, 3 + head:4 + head, :]
                whole = self.weighted[3 * at + head] / total
                place = HEAD_CONTEXT[head][1]
                made.append(jnp.where(lane_mask(whole.shape, place, place + HD, 0), whole, 0.0))
                sums[head:head + 1, rows] = self.stats[at, head:head + 1, :] + jnp.log(total)
            context[rows, 0:128] = made[0].T
            context[rows, 128:256] = (made[1] + made[2]).T


class Backward:
    def __init__(self, skip, queries, window, context, grads, sums, spans, by_query, by_grad, deltas, query_acc, acc):
        self.skip = skip
        self.window, self.sums, self.spans = window, sums, spans
        self.by_query, self.by_grad, self.deltas, self.query_acc, self.acc = by_query, by_grad, deltas, query_acc, acc
        scale = jnp.asarray(HD ** (-0.5), BF16)
        for head in range(3):
            every = slice(None)
            by_query[head] = head_rows(queries, every, HEAD_QUERY[head]) * scale
            mine = head_rows(grads, every, HEAD_CONTEXT[head])
            by_grad[head] = mine
            tile = HEAD_CONTEXT[head][0]
            product = mine.astype(F32) * context[:, tile:tile + 128]
            deltas[head:head + 1, :] = lax.dot_general(
                jnp.ones((8, 128), F32), product, (((1,), (1,)), ((), ())),
                precision=lax.Precision.HIGHEST, preferred_element_type=F32,
            )[0:1]
        acc[...] = jnp.zeros_like(acc)
        query_acc[...] = jnp.zeros_like(query_acc)

    def visit(self, at, j):
        rows, columns, keys = rows_at(at * QT, QT), rows_at(at * QT, QT, 128), rows_at(j * KT, KT)
        window, acc = self.window, self.acc.at[rows_at(j * KT - self.skip, KT)]
        bias = meets(self.spans, columns, j)
        key_grads, value_grads = [], []
        for head in range(3):
            key = window[keys, HEAD_QUERY[head][0]:HEAD_QUERY[head][0] + 128]
            value = window[keys, HEAD_VALUE[head][0]:HEAD_VALUE[head][0] + 128]
            query, grad = self.by_query[head, rows, :], self.by_grad[head, rows, :]
            probs = jnp.exp((nt(key, query) + bias) - self.sums[head:head + 1, columns])
            steps = (probs * (nt(value, grad) - self.deltas[head:head + 1, columns])).astype(BF16)
            value_grads.append(nn(probs.astype(BF16), grad))
            key_grads.append(nn(steps, query))
            self.query_acc[3 * at + head] += tn(key, steps)
        acc[:, 0:128] += key_grads[0] + key_grads[1]
        acc[:, 128:256] += key_grads[2] + value_grads[0]
        acc[:, 256:384] += value_grads[1] + value_grads[2]

    def run(self, count, where):
        def one(n, carry):
            self.visit(*where(n))
            return carry

        lax.fori_loop(0, count, one, 0)

    def query_rows(self, target):
        scale = HD ** (-0.5)
        for at in range(target.shape[0] // QT):
            made = []
            for head in range(3):
                place = HEAD_QUERY[head][1]
                mine = self.query_acc[3 * at + head]
                made.append(jnp.where(lane_mask(mine.shape, place, place + HD, 0), mine * scale, 0.0))
            rows = slice(at * QT, (at + 1) * QT)
            target[rows, 0:128] = (made[0] + made[1]).T.astype(BF16)
            target[rows, 128:256] = made[2].T.astype(BF16)


def norm_forward(values):
    center = values - jnp.mean(values, axis=-1, keepdims=True)
    scale = lax.rsqrt(jnp.mean(center * center, axis=-1, keepdims=True) + EPSILON)
    return center * scale, scale


def norm_backward(grad, unit_rows, scale, gain):
    inner = grad * gain
    gain_row = jnp.sum(grad * unit_rows, axis=0, keepdims=True)
    shift_row = jnp.sum(grad, axis=0, keepdims=True)
    back = scale * (
        inner
        - jnp.mean(inner, axis=-1, keepdims=True)
        - unit_rows * jnp.mean(inner * unit_rows, axis=-1, keepdims=True)
    )
    return back, gain_row, shift_row


def column_sum(values):
    return jnp.sum(values.astype(F32), axis=0, keepdims=True)


def middle_kernel(
    repeat, groups,
    context, tokens, d_out, params, ffb, all2, all_ff2,
    out, d_mid_out, grads_out, grad_o2, grad_ff2, sum_rows,
    w_out, w_ff1, w_ff2, ctx_rows, parts, pack, grad_rows, act, slope, d_pre,
    land_out, land_ff1, land_ff2,
    send, recv, back_send, back_recv, grad_send, grad_recv, local,
):
    place = Place(repeat, groups)
    tok, dim = tokens.shape
    ff = w_ff1.shape[1]
    scatters = {
        name: Scatter(place, grad_o2, dim // 16, first, width, RS_PLAN[name], True)
        for name, first, width in matrices(dim, ff)
    }
    scatters["ff2"] = Scatter(place, grad_ff2, ff // 16, 0, dim, RS_PLAN["ff2"], False)
    loads = [
        pltpu.make_async_copy(all2.at[:, pl.ds(0, dim)], w_out, local.at[0]),
        pltpu.make_async_copy(all2.at[:, pl.ds(dim, ff)], w_ff1, local.at[1]),
        pltpu.make_async_copy(all_ff2, w_ff2, local.at[2]),
    ]
    for load in loads:
        load.start()
    ctx_rows[...] = context[...].astype(BF16)
    place.greet(beside=False)
    to_tokens(place, ctx_rows, parts, send, recv)
    to_tokens_wait(place, ctx_rows, parts, send, recv)
    joined = jnp.concatenate([parts[chip][:, QW - HW:].astype(F32) for chip in range(CHIPS)], axis=1).astype(BF16)
    loads[0].wait()
    gains, shifts = [params[at:at + 1, :] for at in (0, 1)], [params[at:at + 1, :] for at in (2, 3)]
    mid = tokens[...].astype(F32) + (nn(joined, w_out[...]) + params[6:7, :])
    unit_first, scale_first = norm_forward(mid)
    hidden = unit_first * gains[0] + shifts[0]
    low = hidden.astype(BF16)
    loads[1].wait()
    loads[2].wait()
    ff_out = jnp.zeros((tok, dim), F32)
    for first in range(0, ff, dim):
        cut = slice(first, first + dim)
        pre = nn(low, w_ff1[:, cut]) + ffb[0:1, cut]
        bell = 0.5 * (1.0 + lax.erf(pre * 0.7071067811865476))
        made = (pre * bell).astype(BF16)
        act[:, cut] = made
        slope[:, cut] = bell + pre * jnp.exp(-0.5 * pre * pre) * 0.3989422804014327
        ff_out = ff_out + nn(made, w_ff2[cut, :])
    unit_second, scale_second = norm_forward(hidden + (ff_out + params[7:8, :]))
    out[...] = (unit_second * gains[1] + shifts[1]).astype(BF16)
    d_sum, gain_second, shift_second = norm_backward(d_out[...].astype(F32), unit_second, scale_second, gains[1])
    d_ff = d_sum.astype(BF16)
    for first in range(0, ff, dim):
        cut = slice(first, first + dim)
        grad_ff2[cut, :] = tn(act[:, cut], d_ff).astype(BF16)
    scatters["ff2"].begin(land_ff2, grad_send.at[2], grad_recv.at[2])
    d_hidden = d_sum
    for first in range(0, ff, dim):
        cut = slice(first, first + dim)
        made = (nt(d_ff, w_ff2[cut, :]) * slope[:, cut]).astype(BF16)
        d_pre[:, cut] = made
        d_hidden = d_hidden + nt(made, w_ff1[:, cut])
    d_mid, gain_first, shift_first = norm_backward(d_hidden, unit_first, scale_first, gains[0])
    d_mid_out[...] = d_mid
    d_attn = d_mid.astype(BF16)
    d_context = nt(d_attn, w_out[...])
    for chip in range(CHIPS):
        pack[chip] = jnp.concatenate(
            [jnp.zeros((tok, QW - HW), F32), d_context[:, HW * chip:HW * (chip + 1)]], axis=1
        ).astype(BF16)
    to_heads(place, pack, grad_rows, back_send, back_recv)
    for first in range(0, ff, dim):
        cut = slice(first, first + dim)
        grad_o2[:, dim + first:2 * dim + first] = tn(low, d_pre[:, cut]).astype(BF16)
        sum_rows[8 + first // dim:9 + first // dim, :] = column_sum(d_pre[:, cut])
    scatters["ff1"].begin(land_ff1, grad_send.at[1], grad_recv.at[1])
    grad_o2[:, 0:dim] = tn(joined, d_attn).astype(BF16)
    scatters["out"].begin(land_out, grad_send.at[0], grad_recv.at[0])
    for at, row in enumerate(
        (
            gain_first, gain_second, shift_first, shift_second,
            jnp.zeros((1, dim), F32), jnp.zeros((1, dim), F32), column_sum(d_attn), column_sum(d_ff),
        )
    ):
        sum_rows[at:at + 1, :] = row
    sum_rows[8 + ff // dim:, :] = jnp.zeros((8 - ff // dim, dim), F32)
    for name in REST:
        for j in range(16):
            scatters[name].absorb(0, j)
    to_heads_wait(place, grad_rows, back_send, back_recv)
    grads_out[...] = grad_rows[...]
    to_tokens_drain(place, ctx_rows, parts, send, recv)
    to_heads_drain(place, grad_rows, back_send, back_recv)
    for scatter in scatters.values():
        scatter.finish(1)


def middle(repeat, groups, context, tokens, d_out, params, ffb, all2, all_ff2):
    tok, dim = tokens.shape
    ff = all_ff2.shape[0]
    shape = jax.ShapeDtypeStruct
    vm = pltpu.VMEM
    return pl.pallas_call(
        functools.partial(middle_kernel, repeat, groups),
        out_shape=(
            shape((tok, dim), BF16), shape((tok, dim), F32), shape((4 * tok, QW), BF16),
            shape((dim, dim + ff), BF16), shape((ff, dim), BF16), shape((16, dim), F32),
        ),
        in_specs=[VM] * 5 + [HBM] * 2,
        out_specs=(VM,) * 6,
        scratch_shapes=[
            vm((dim, dim), BF16), vm((dim, ff), BF16), vm((ff, dim), BF16), vm((4 * tok, QW), BF16),
            vm((CHIPS, tok, QW), BF16), vm((CHIPS, tok, QW), BF16), vm((4 * tok, QW), BF16),
            vm((tok, ff), BF16), vm((tok, ff), F32), vm((tok, ff), BF16),
            vm((16, dim // 16, dim // 2), BF16), vm((16, dim // 16, ff // 2), BF16), vm((16, ff // 32, dim), BF16),
            DMA((4,)), DMA((4,)), DMA((4,)), DMA((4,)), DMA((3, 16)), DMA((3, 16)), DMA((4,)),
        ],
        compiler_params=pltpu.CompilerParams(collective_id=2, has_side_effects=True, vmem_limit_bytes=VMEM_BYTES),
    )(context, tokens, d_out, params, ffb, all2, all_ff2)


def leave_kernel(
    repeat, groups,
    queries, window, context, grads, sums, spans, rows, heads, d_mid, sum_rows, grad_o2, grad_ff2_in,
    d_tokens, g_qkv, g_out, g_ff1, g_ff2, g_rows,
    by_query, by_grad, deltas, query_acc, acc,
    grad2, grad_ff2, land_out, land_ff1, land_ff2, blocks, land_blocks, role_land,
    near_out, near_land, side_land, solo_out, joint, joined, partial, parts, swap_out, swap_in, rows_mine, rows_land,
    grad_send, grad_recv, block_send, block_recv, plane_send, plane_recv, near_send, near_recv, side_send, side_recv,
    part_send, part_recv, swap_send, swap_recv, rows_send, rows_recv, local,
):
    place = Place(repeat, groups)
    tok, dim = d_mid.shape
    ff = grad_ff2.shape[0]
    unit_rows = dim // 32
    half = 4 * tok
    role = 2 * place.x + place.y
    core = place.core
    loads = [
        pltpu.make_async_copy(grad_o2, grad2, local.at[0]),
        pltpu.make_async_copy(grad_ff2_in, grad_ff2, local.at[1]),
    ]
    for load in loads:
        load.start()
    place.greet()
    sibling = place.member(place.x, 1 - core, place.y)

    def near(at):
        return remote(near_out, near_land.at[at], near_send.at[at], near_recv.at[at], sibling)

    solo = remote(
        solo_out, side_land.at[core], side_send.at[core], side_recv.at[core], place.beside(2 * core - 1)
    )
    shared = remote(
        joint, side_land.at[1 - core], side_send.at[1 - core], side_recv.at[1 - core], place.beside(1 - 2 * core)
    )
    cuts = matrices(dim, ff)
    scatters = {
        name: Scatter(place, grad2, 2 * unit_rows, first, width, RS_PLAN[name], True) for name, first, width in cuts
    }
    scatters["ff2"] = Scatter(place, grad_ff2, ff // 16, 0, dim, RS_PLAN["ff2"], False)
    loads[0].wait()
    loads[1].wait()
    scatters["ff2"].begin(land_ff2, grad_send.at[2], grad_recv.at[2], 1)
    scatters["ff1"].begin(land_ff1, grad_send.at[1], grad_recv.at[1], 1)
    scatters["out"].begin(land_out, grad_send.at[0], grad_recv.at[0], 1)
    back = Backward(core * half, queries, window, context, grads, sums, spans, by_query, by_grad, deltas, query_acc, acc)

    def rest(slot):
        for stage, at in enumerate(LEAVE_PLAN):
            if at == slot:
                for name in REST:
                    scatters[name].stage(stage + 1)

    def made(slot, which):
        return acc[rows_at(2 * half * slot + half * which - half * core, half), :]


    back.run(3, solo_tile(core))
    solo_out[...] = made(2 * core, core).astype(BF16)
    solo.start()
    rest(0)
    back.run(4, lambda n: (rem(n, 2), 2 + 6 * core + div(n, 2)))
    near_out[...] = made(2 * core, 1 - core).astype(BF16)
    near(0).start()
    rest(1)
    back.run(3, shared_tile(core))
    near(0).wait_recv()
    joint[...] = (made(2 - 2 * core, core) + near_land[0].astype(F32)).astype(BF16)
    shared.start()
    rest(2)
    back.run(4, lambda n: (rem(n, 2), 6 - 2 * core + div(n, 2)))
    near(0).wait_send()
    near_out[...] = made(1, 1 - core).astype(BF16)
    near(1).start()
    rest(3)
    back.run(4, lambda n: (rem(n, 2), 4 + 2 * core + div(n, 2)))
    back.query_rows(joined)
    rest(4)
    near(1).wait_recv()
    own = made(1, core) + near_land[1].astype(F32)
    for at in range(2):
        remote(joint, side_land.at[at], side_send.at[at], side_recv.at[at], sibling).wait_recv()
    joined[:, QW:] = (own + side_land[0].astype(F32) + side_land[1].astype(F32)).astype(BF16)
    for at in range(4):
        part = slice(at * tok, (at + 1) * tok)
        partial[part, :] = nt(joined[part, :], heads[...]).astype(BF16)
    to_tokens(place, partial, parts, part_send, part_recv)
    whole = tn(rows[...], joined[...])
    for unit in range(32):
        block = whole[unit * unit_rows:(unit + 1) * unit_rows]
        pad = jnp.zeros((blocks.shape[1] - unit_rows, PW), F32)
        blocks[unit] = jnp.concatenate([block, pad], axis=0).astype(BF16)
    until = 3 if repeat == 1 else 5
    by_heads = ScatterBlocks(place, blocks, RS_HEADS, until)
    by_heads.begin(land_blocks, block_send, block_recv)
    rest(5)
    sums = column_sum(joined[...])
    rows_mine[0] = sum_rows[...]
    for row, first in ((4, 0), (5, PW - HW)):
        line = [jnp.where(role == chip, sums[:, first:first + HW], 0.0) for chip in range(CHIPS)]
        rows_mine[0, row:row + 1, :] = jnp.concatenate(line, axis=1)

    def rows_copy(phase):
        return remote(
            rows_mine.at[phase], rows_land.at[phase], rows_send.at[phase], rows_recv.at[phase],
            place.partner(RS_HEADS[phase]),
        )

    def rows_add(phase):
        rows_copy(phase).wait_recv()
        rows_mine[phase + 1] = rows_mine[phase] + rows_land[phase]
        if phase < 4:
            rows_copy(phase + 1).start()

    rows_copy(0).start()
    by_heads.step(0)
    rows_add(0)
    rest(6)
    by_heads.step(1)
    rows_add(1)
    rest(7)
    by_heads.step(2)
    rows_add(2)
    rest(8)

    def role_copy(dx, dy):
        chip, device = plane(place, dx, dy)
        at = 2 * dx + dy
        there = place.unit + dx * 4 * (1 - 2 * place.bit(2)) + dy * (1 - 2 * place.bit(0))
        return remote(blocks.at[there], role_land.at[role], plane_send.at[at], plane_recv.at[at], device)

    if repeat == 1:
        for dx, dy in ((1, 1), (1, 0), (0, 1)):
            role_copy(dx, dy).start()
    else:
        by_heads.step(3)
        by_heads.last()
        role_land[...] = jnp.zeros_like(role_land)
    role_land[role] = blocks[place.unit]
    rows_add(3)

    def swap(at):
        name, first, width = cuts[at]
        part = (slice(None), pl.ds(first // 2, width // 2))
        return remote(swap_out.at[part], swap_in.at[part], swap_send.at[at], swap_recv.at[at], place.partner(0))

    def finish_half(at):
        name, first, width = cuts[at]
        target = (g_out, g_ff1)[at]
        total = scatters[name].last()
        high = place.bit(0) == 1
        keep = jnp.where(high, total[unit_rows:], total[:unit_rows])
        give = jnp.where(high, total[:unit_rows], total[unit_rows:])
        pad = jnp.zeros((swap_out.shape[0] - unit_rows, give.shape[1]), F32)
        swap_out[:, first // 2:(first + width) // 2] = jnp.concatenate([give, pad], axis=0).astype(BF16)
        swap(at).start()
        target[:, rows_at(place.bit(0) * (width // 2), width // 2, 128)] = keep

    def finish_swap(at):
        name, first, width = cuts[at]
        target = (g_out, g_ff1)[at]
        swap(at).wait_recv()
        other = swap_in[:, first // 2:(first + width) // 2].astype(F32)[:unit_rows]
        target[:, rows_at((1 - place.bit(0)) * (width // 2), width // 2, 128)] = other

    for at in (1, 0):
        finish_half(at)
    g_ff2[...] = scatters["ff2"].last()
    rows_add(4)
    g_rows[...] = rows_mine[5]
    to_tokens_wait(place, partial, parts, part_send, part_recv)
    d_tokens[...] = (
        d_mid[...] + (parts[0].astype(F32) + parts[1].astype(F32)) + (parts[2].astype(F32) + parts[3].astype(F32))
    ).astype(BF16)
    for at in (1, 0):
        finish_swap(at)
    if repeat == 1:
        for dx, dy in ((1, 1), (1, 0), (0, 1)):
            role_copy(dx, dy).wait_recv()
    for part, first in ((0, 0), (1, QW), (2, QW + HW)):
        line = [role_land[chip][:unit_rows, first:first + HW].astype(F32) for chip in range(CHIPS)]
        g_qkv[:, part * dim:(part + 1) * dim] = jnp.concatenate(line, axis=1)
    for scatter in scatters.values():
        scatter.finish()
    by_heads.finish()
    if repeat == 1:
        for dx, dy in ((1, 1), (1, 0), (0, 1)):
            role_copy(dx, dy).wait_send()
    for at in range(2):
        swap(at).wait_send()
    near(1).wait_send()
    solo.wait_send()
    shared.wait_send()
    for phase in range(5):
        rows_copy(phase).wait_send()
    to_tokens_drain(place, partial, parts, part_send, part_recv)


LEAVE_PLAN = (3, 4, 6, 8)


def leave(repeat, groups, attention, rows, heads, d_mid, sum_rows, grad_o2, grad_ff2):
    tok, dim = d_mid.shape
    ff = grad_ff2.shape[0]
    unit = dim // 32
    slab = 2 * unit
    half = 4 * tok
    wide = -(-unit // 16) * 16
    shape = jax.ShapeDtypeStruct
    vm = pltpu.VMEM
    return pl.pallas_call(
        functools.partial(leave_kernel, repeat, groups),
        out_shape=(
            shape((tok, dim), BF16), shape((unit, 3 * dim), F32), shape((unit, dim), F32), shape((unit, ff), F32),
            shape((ff // 32, dim), F32), shape((16, dim), F32),
        ),
        in_specs=[VM] * 10 + [HBM] * 2,
        out_specs=(VM,) * 6,
        scratch_shapes=[
            vm((3, half, 128), BF16), vm((3, half, 128), BF16), vm((8, half), F32), vm((3 * half // QT, 128, QT), F32),
            vm((5 * half, KW), F32),
            vm((dim, dim + ff), BF16), vm((ff, dim), BF16),
            vm((15, slab, dim // 2), BF16), vm((15, slab, ff // 2), BF16), vm((15, ff // 32, dim), BF16),
            vm((32, wide, PW), BF16), vm((31, wide, PW), BF16), vm((CHIPS, wide, PW), BF16),
            vm((half, KW), BF16), vm((2, half, KW), BF16), vm((2, half, KW), BF16), vm((half, KW), BF16),
            vm((half, KW), BF16), vm((half, PW), BF16),
            vm((half, dim), BF16), vm((CHIPS, tok, dim), BF16),
            vm((wide, (dim + ff) // 2), BF16), vm((wide, (dim + ff) // 2), BF16),
            vm((6, 16, dim), F32), vm((5, 16, dim), F32),
            DMA((3, 31)), DMA((3, 31)), DMA((31,)), DMA((31,)), DMA((4,)), DMA((4,)), DMA((2,)), DMA((2,)), DMA((2,)),
            DMA((2,)), DMA((4,)), DMA((4,)), DMA((2,)), DMA((2,)), DMA((5,)), DMA((5,)), DMA((2,)),
        ],
        compiler_params=pltpu.CompilerParams(collective_id=3, has_side_effects=True, vmem_limit_bytes=VMEM_BYTES),
    )(*attention, rows, heads, d_mid, sum_rows, grad_o2, grad_ff2)


def settle_kernel(
    repeat, out, d_tokens, g_qkv, g_out, g_ff1, g_ff2, g_rows,
    out_r, d_tokens_r, g_qkv_r, g_out_r, g_ff1_r, g_ff2_r, gains_r, shifts_r, biases_r, hidden_r,
):
    for source, target in (
        (out, out_r), (d_tokens, d_tokens_r), (g_qkv, g_qkv_r), (g_out, g_out_r), (g_ff1, g_ff1_r), (g_ff2, g_ff2_r)
    ):
        target[...] = source[...]
    width = g_rows.shape[1]
    per, hidden = gains_r.shape[1], hidden_r.shape[1]
    unit = div(lax.axis_index("blk") * 2 + lax.axis_index("head"), repeat)
    turned = pltpu.roll(g_rows[0:8, :], rem(width - unit * per, width), 1)
    gains_r[...] = turned[0:2, :per]
    shifts_r[...] = turned[2:4, :per]
    biases_r[...] = turned[4:8, :per]
    lines = g_rows[8:16, :]
    row = lax.broadcasted_iota(jnp.int32, lines.shape, 0)
    mine = jnp.sum(jnp.where(row == div(unit * hidden, width), lines, 0.0), axis=0, keepdims=True)
    turned = pltpu.roll(jnp.broadcast_to(mine, lines.shape), rem(width - rem(unit * hidden, width), width), 1)
    hidden_r[...] = turned[0:1, :hidden]


def settle(repeat, results):
    shape = jax.ShapeDtypeStruct
    per, hidden = results[2].shape[0], results[5].shape[0]
    small = [shape((count, per), F32) for count in (2, 2, 4)] + [shape((1, hidden), F32)]
    return pl.pallas_call(
        functools.partial(settle_kernel, repeat),
        out_shape=[shape(value.shape, value.dtype) for value in results[:6]] + small,
        in_specs=[VM] * 7,
        out_specs=[VM] * 10,
        compiler_params=pltpu.CompilerParams(vmem_limit_bytes=VMEM_BYTES),
    )(*results)


def gather_repeat(value, repeat, axis):
    if repeat == 1:
        return value
    count = repeat // 2
    sets = [list(range(at, at + count)) for at in range(0, lax.axis_size("blk"), count)]
    value = lax.all_gather(value, "head", axis=axis, tiled=True)
    if count == 1:
        return value
    return lax.all_gather(value, "blk", axis=axis, tiled=True, axis_index_groups=sets)


def own_share(value, repeat, axis):
    if repeat == 1:
        return value
    count = repeat // 2
    sets = [list(range(at, at + count)) for at in range(0, lax.axis_size("blk"), count)]
    value = lax.psum(value, "head")
    if count > 1:
        value = lax.psum(value, "blk", axis_index_groups=sets)
    size = value.shape[axis] // repeat
    at = jnp.mod(lax.axis_index("blk") * 2 + lax.axis_index("head"), repeat)
    return lax.dynamic_slice_in_dim(value, at * size, size, axis)


def body(tokens, w_qkv, w_out, w_ff1, w_ff2, norm_gains, norm_biases, proj_biases, ff_bias, doc_starts, d_out):
    blks = lax.axis_size("blk")
    repeat = blks * 2 // 32
    groups = blks // GROUP
    tok, dim = tokens.shape
    shard_qkv = gather_repeat(w_qkv, repeat, 0)
    shard2 = gather_repeat(jnp.concatenate([w_out, w_ff1], axis=1), repeat, 0)
    shard2 = jnp.pad(shard2, ((0, -shard2.shape[0] % 16), (0, 0)))
    shard_ff2 = gather_repeat(w_ff2, repeat, 0)
    small = pack_small(
        gather_repeat(norm_gains, repeat, 1), gather_repeat(norm_biases, repeat, 1),
        gather_repeat(proj_biases, repeat, 1), gather_repeat(ff_bias, repeat, 0),
    )
    all2, all_ff2, params, ffb, queries, window, rows, heads, context, sums, spans = enter(
        repeat, groups, doc_starts, shard_qkv, shard2, shard_ff2, small, tokens
    )
    out, d_mid, grads, grad_o2, grad_ff2, sum_rows = middle(
        repeat, groups, context, tokens, d_out, params, ffb, all2, all_ff2
    )
    d_tokens, g_qkv, g_out, g_ff1, g_ff2, g_rows = leave(
        repeat, groups, (queries, window, context, grads, sums, spans), rows, heads, d_mid, sum_rows, grad_o2, grad_ff2
    )
    results = settle(repeat, (out, d_tokens, g_qkv, g_out, g_ff1, g_ff2, g_rows))
    axes = (None, None, 0, 0, 0, 0, 1, 1, 1, 0)
    results = list(results[:9]) + [results[9].reshape(-1)]
    return tuple(
        value if axis is None else own_share(value, repeat, axis) for value, axis in zip(results, axes)
    )


def solution(mesh):
    rows, columns, flat = P(("blk", "head"), None), P(None, ("blk", "head")), P(("blk", "head"))
    return jax.shard_map(
        body,
        mesh=mesh,
        in_specs=(rows,) * 5 + (columns,) * 3 + (flat, P(), rows),
        out_specs=(rows,) * 6 + (columns,) * 3 + (flat,),
        check_vma=False,
    )
```
